256 devices in a mesh: exp: 2 (over y_hi), gz: 64 (over x, y_lo, z), xy: 2 (over core).
Axes of the slice: x: 4, y: 4 (y_hi: 2, y_lo: 2; y = y_hi * 2 + y_lo), z: 8, core: 2. Of those that a mesh axis runs over, the one named last changes fastest.
Arguments:
- fluid_start: float32 [4, 2, 512, 64, 128], P('exp', None, 'gz', 'xy'), may hold values from 0 to 1
- pellet_start: float32 [4, 2, 4, 512, 64, 128], P('exp', None, None, 'gz', 'xy'), may hold values from 0 to 1
- porosity: float32 [512, 64, 128], P('gz', 'xy'), may hold values from 0.3 to 0.5
- feed_level: int32 [4], P('exp'), may hold values from 0 to 3, as said below
- sample_step: int32 [4], P('exp'), may hold values from 0 to 1, as said below
- observed_outlet: float32 [4, 2], P('exp'), may hold values from 0 to 1
- adjoint_fluid_end: float32 [4, 2, 512, 64, 128], P('exp', None, 'gz', 'xy'), may hold values from -6 to 6
- adjoint_pellet_end: float32 [4, 2, 4, 512, 64, 128], P('exp', None, None, 'gz', 'xy'), may hold values from -6 to 6
Outputs:
- breakthrough: float32 [4, 2], P('exp')
- adjoint_fluid: float32 [4, 2, 512, 64, 128], P('exp', None, 'gz', 'xy')
- adjoint_pellet: float32 [4, 2, 4, 512, 64, 128], P('exp', None, None, 'gz', 'xy')
- porosity_gradient: float32 [512, 64, 128], P('gz', 'xy')
The draws below stay inside these ranges and needn't reach their ends.
Inputs may be any that keep to these rules, and one draw needn't show every extreme that they name: `feed_level`: every level 0 to 3 is used by exactly one experiment. `sample_step`: each window step is sampled by the same number of experiments.
All inputs are finite; a program needn't handle non-finite values.
Results may differ from the reference program's by a relative error of at most 0.0003.
Values sent between devices are 32-bit elements; how exact they have to be, the bound alone decides.
No kernel may reach another device: no remote copies, remote signals or barrier semaphores. Data moves between devices by JAX's collectives and lax.ppermute only.
A program may use at most 64 MiB of HBM per device.

```python
import jax
import jax.numpy as jnp
from jax import lax

COMPS = 2
SHELLS = 4
STEPS = 2
EXP = 4
NZ = 512
NX = 64
NY = 128


def draw_feed_level(key, part):
    key = jax.random.fold_in(key, 11)
    return jax.random.permutation(key, EXP).astype(jnp.int32)


def draw_sample_step(key, part):
    key = jax.random.fold_in(key, 23)
    return (jax.random.permutation(key, EXP) % STEPS).astype(jnp.int32)


def steps_of(rng, extent, pieces, least, top_value):
    def one(axis_at, blocks):
        heights = jax.random.uniform(jax.random.fold_in(jax.random.fold_in(rng, 6), axis_at), (blocks,), jnp.float32, least / len(pieces), top_value / len(pieces))
        return jnp.repeat(jnp.exp(heights), extent[axis_at] // blocks).reshape((-1,) + (1,) * (len(extent) - axis_at - 1))

    level = one(*pieces[0])
    for cut in pieces[1:]:
        level = level * one(*cut)
    return level


def bell_draw(stream_key, extent, scale, limit, split=(), held_as=jnp.bfloat16):
    entries = jax.random.normal(stream_key, extent, jnp.float32) * scale
    if len(split) > 0:
        entries = steps_of(stream_key, extent, split, -0.22, 0.18) * entries
    return jnp.clip(entries, min=-limit, max=limit).astype(held_as)


def setup_inputs(seed: int = 0) -> dict:
    splits = jax.random.split(jax.random.key(seed), 9)
    return {
        "fluid_start": jnp.clip(1.0 * jax.random.uniform(splits[0], (EXP, COMPS, NZ, NX, NY), jnp.float32) ** steps_of(splits[0], (EXP, COMPS, NZ, NX, NY), ((0, 2), (2, 64), (3, 2)), -0.2, 0.2), 0.0, 1.0),
        "pellet_start": jnp.clip(1.0 * jax.random.uniform(splits[1], (EXP, COMPS, SHELLS, NZ, NX, NY), jnp.float32) ** steps_of(splits[1], (EXP, COMPS, SHELLS, NZ, NX, NY), ((0, 2), (3, 64), (4, 2)), -0.2, 0.2), 0.0, 1.0),
        "porosity": jnp.clip(0.3 + 0.19999999 * jax.random.uniform(splits[2], (NZ, NX, NY), jnp.float32) ** steps_of(splits[2], (NZ, NX, NY), ((0, 64), (1, 2)), -0.2, 0.2), 0.3, 0.5),
        "feed_level": draw_feed_level(jax.random.fold_in(splits[8], 71), 0),
        "sample_step": draw_sample_step(jax.random.fold_in(splits[8], 71), 0),
        "observed_outlet": jnp.clip(1.0 * jax.random.uniform(splits[5], (EXP, COMPS), jnp.float32) ** steps_of(splits[5], (EXP, COMPS), ((0, 2),), -0.2, 0.2), 0.0, 1.0),
        "adjoint_fluid_end": bell_draw(splits[6], (EXP, COMPS, NZ, NX, NY), 1.0, 6.0, ((0, 2), (2, 64), (3, 2)), jnp.float32),
        "adjoint_pellet_end": bell_draw(splits[7], (EXP, COMPS, SHELLS, NZ, NX, NY), 1.0, 6.0, ((0, 2), (3, 64), (4, 2)), jnp.float32),
    }


ADVECT = 0.12
AXIAL_MIX = 0.08
RADIAL_MIX = 0.05
FILM_RATE = 0.05
SHELL_MIX = 0.2
PELLET_SHARE = 0.6
AFFINITY = 0.5

def update(fluid, pellet, porosity, lower_cells, upper_cells, left_cells, right_cells):
    front_cells = jnp.concatenate([fluid[..., 0:1], fluid[..., :-1]], axis=-1)
    back_cells = jnp.concatenate([fluid[..., 1:], fluid[..., -1:]], axis=-1)
    advect_rate = ADVECT / porosity
    exchange_rate = FILM_RATE * (1.0 - porosity) / porosity
    core_shell = pellet[..., 0, :, :, :]
    second_shell = pellet[..., 1, :, :, :]
    third_shell = pellet[..., 2, :, :, :]
    outer_shell = pellet[..., 3, :, :, :]
    inhibit = 1.0 + AFFINITY * lax.optimization_barrier(jnp.sum(outer_shell, axis=-4, keepdims=True))
    film_flux = (fluid - outer_shell) / inhibit
    fluid_next = fluid + advect_rate * (lower_cells - fluid) + AXIAL_MIX * (lower_cells - 2.0 * fluid + upper_cells) + RADIAL_MIX * (left_cells + right_cells + front_cells + back_cells - 4.0 * fluid) - exchange_rate * film_flux
    pellet_next = jnp.stack([core_shell + SHELL_MIX * (second_shell - core_shell), second_shell + SHELL_MIX * (third_shell - 2.0 * second_shell + core_shell), third_shell + SHELL_MIX * (outer_shell - 2.0 * third_shell + second_shell), outer_shell + SHELL_MIX * (third_shell - outer_shell) + PELLET_SHARE * FILM_RATE * film_flux], axis=-4)
    return (fluid_next, pellet_next)

def advance_whole(fluid, pellet, porosity, inlet):
    inlet_plane = jnp.broadcast_to(inlet, fluid[..., :1, :, :].shape)
    lower_cells = jnp.concatenate([inlet_plane, fluid[..., :-1, :, :]], axis=-3)
    upper_cells = jnp.concatenate([fluid[..., 1:, :, :], fluid[..., -1:, :, :]], axis=-3)
    left_cells = jnp.concatenate([fluid[..., 0:1, :], fluid[..., :-1, :]], axis=-2)
    right_cells = jnp.concatenate([fluid[..., 1:, :], fluid[..., -1:, :]], axis=-2)
    return update(fluid, pellet, porosity, lower_cells, upper_cells, left_cells, right_cells)

def reference(fluid_start, pellet_start, porosity, feed_level, sample_step, observed_outlet, adjoint_fluid_end, adjoint_pellet_end):
    exp_count = fluid_start.shape[0]

    def one_experiment(items):
        fluid_zero, pellet_zero, level_int, sample, observed, seed_fluid, seed_pellet = items
        level = level_int.astype(jnp.float32)
        inlet = jnp.stack([(1.0 + level) / exp_count, (exp_count - level) / exp_count]).reshape(2, 1, 1, 1)
        chosen = (sample == jnp.arange(STEPS, dtype=jnp.int32)).astype(jnp.float32)

        def objective(fluid, pellet, field):
            means = []
            for step in range(STEPS):
                fluid, pellet = advance_whole(fluid, pellet, field, inlet)
                means.append(lax.optimization_barrier(jnp.sum(fluid[:, -1], axis=(-2, -1))) / (NX * NY))
            means = jnp.stack(means)
            picked = lax.optimization_barrier(jnp.sum(chosen[:, None] * means, axis=0))
            total = jnp.sum(seed_fluid * fluid) + jnp.sum(seed_pellet * pellet) + 0.5 * (NX * NY) * jnp.sum((picked - observed) ** 2)
            return (total, picked)
        grads, picked = jax.grad(objective, argnums=(0, 1, 2), has_aux=True)(fluid_zero, pellet_zero, porosity)
        return (picked, grads[0], grads[1], grads[2])
    picked, grad_fluid, grad_pellet, grad_field = lax.map(one_experiment, (fluid_start, pellet_start, feed_level, sample_step, observed_outlet, adjoint_fluid_end, adjoint_pellet_end))
    return (picked, grad_fluid, grad_pellet, lax.optimization_barrier(jnp.sum(grad_field, axis=0)))
```

```python
from functools import partial

import jax
import jax.numpy as jnp
from jax import lax
from jax.experimental import pallas as pl
from jax.experimental.pallas import tpu as pltpu
from jax.sharding import PartitionSpec as P

STEPS = 2

ADVECT = 0.12
AXIAL_MIX = 0.08
RADIAL_MIX = 0.05
FILM_RATE = 0.05
SHELL_MIX = 0.2
PELLET_GAIN = 0.03
AFFINITY = 0.5

KEEP_END = 1.0 - SHELL_MIX
KEEP_MID = 1.0 - 2.0 * SHELL_MIX


def row_index(cells):
    return lax.broadcasted_iota(jnp.int32, cells.shape, cells.ndim - 2)


def lane_index(cells):
    return lax.broadcasted_iota(jnp.int32, cells.shape, cells.ndim - 1)


def cross_mix(cells, rim, first_x):
    nx, ny = cells.shape[-2:]
    row, lane = row_index(cells), lane_index(cells)
    wall = jnp.where(first_x, 0, nx - 1)
    outside = jnp.where(row == wall, cells, jnp.broadcast_to(rim, cells.shape))
    left = jnp.where(row == 0, outside, pltpu.roll(cells, 1, cells.ndim - 2))
    right = jnp.where(row == nx - 1, outside, pltpu.roll(cells, nx - 1, cells.ndim - 2))
    front = jnp.where(lane == 0, cells, pltpu.roll(cells, 1, cells.ndim - 1))
    back = jnp.where(lane == ny - 1, cells, pltpu.roll(cells, ny - 1, cells.ndim - 1))
    return (left + right) + (front + back) - 4.0 * cells


def film(fluid, inner, outer):
    inverse = 1.0 / (1.0 + AFFINITY * (outer[0] + outer[1]))
    flux = (fluid - outer) * inverse
    outer_next = outer + SHELL_MIX * (inner - outer) + PELLET_GAIN * flux
    return flux, inverse, outer_next


def film_back(flux_cot, flux, inverse):
    direct = flux_cot * inverse
    shared = AFFINITY * (direct[0] * flux[0] + direct[1] * flux[1])
    return direct, -direct - shared


def pack_kernel(fluid, pellet, porosity, adjoint, up_out, down_out, row_out):
    experiments, comps, nz, nx, ny = fluid.shape
    first_x = lax.axis_index("xy") == 0
    for e in range(experiments):
        for k in range(comps):
            i = e * comps + k
            up_out[i] = fluid[e, k, nz - 1]
            up_out[4 + i] = adjoint[e, k, nz - 1]
            down_out[i] = fluid[e, k, 0]
            down_out[4 + i] = adjoint[e, k, 0]
            row_out[i] = jnp.where(first_x, fluid[e, k, :, nx - 1, :], fluid[e, k, :, 0, :])
            row_out[4 + i] = jnp.where(first_x, adjoint[e, k, :, nx - 1, :], adjoint[e, k, :, 0, :])
    down_out[8] = porosity[0]
    inverse_porosity = 1.0 / porosity[nz - 2 :]
    advect = ADVECT * inverse_porosity
    exchange = FILM_RATE * (inverse_porosity - 1.0)
    weight_below = advect[1] + AXIAL_MIX
    rim = jnp.zeros((comps, 1, ny), jnp.float32)
    for e in range(experiments):
        nexts, shells, inverses = [], [], []
        for j, z in enumerate((nz - 2, nz - 1)):
            here = fluid[e, :, z]
            below = fluid[e, :, z - 1]
            above = fluid[e, :, min(z + 1, nz - 1)]
            outer, inner = pellet[e, :, 3, z], pellet[e, :, 2, z]
            flux, _, outer_next = film(here, inner, outer)
            nexts.append(
                here
                + advect[j] * (below - here)
                + AXIAL_MIX * (below - 2.0 * here + above)
                + RADIAL_MIX * cross_mix(here, rim, first_x)
                - exchange[j] * flux
            )
            shells.append(outer_next)
        inverse = 1.0 / (1.0 + AFFINITY * (shells[1][0] + shells[1][1]))
        film_weight = exchange[1] * inverse
        weight_here = 1.0 - advect[1] - AXIAL_MIX - film_weight
        second = weight_here * nexts[1] + weight_below * nexts[0] + film_weight * shells[1]
        row_out[8, e : e + 1] = jnp.where(first_x, weight_here[nx - 1 : nx], weight_here[0:1])
        for k in range(comps):
            i = e * comps + k
            row_out[9, i : i + 1] = jnp.sum(nexts[1][k], axis=0, keepdims=True)
            row_out[9, 4 + i : 5 + i] = jnp.sum(second[k], axis=0, keepdims=True)
    row_out[8, 2:3] = jnp.where(first_x, weight_below[nx - 1 : nx], weight_below[0:1])
    row_out[8, 3:8] = jnp.zeros((5, ny), jnp.float32)


def outlet_kernel(cell_count, mine, theirs, sample, observed, picked_out, seed_out):
    first_x = lax.axis_index("xy") == 0
    last_z = lax.axis_index("gz") == lax.axis_size("gz") - 1
    nz = mine.shape[1]
    low = [jnp.where(first_x, mine[i], theirs[i]) for i in (0, 1, 2, 3, 8, 9)]
    high = [jnp.where(first_x, theirs[i], mine[i]) for i in (0, 1, 2, 3, 8, 9)]
    total = low[5] + high[5]
    scale = jnp.where(last_z, 1.0, 0.0)
    picked_out[...] = jnp.zeros_like(picked_out)
    for e in range(2):
        for k in range(2):
            i = e * 2 + k
            top = slice(nz - 1, nz)
            below = slice(nz - 2, nz - 1)
            first = low[i][top] + high[i][top]
            second = (low[4][e : e + 1] * high[i][top] + low[4][2:3] * high[i][below]) + (
                high[4][e : e + 1] * low[i][top] + high[4][2:3] * low[i][below]
            )
            chosen = jnp.where(sample[e] == 0, total[i : i + 1] + RADIAL_MIX * first, total[4 + i : 5 + i] + RADIAL_MIX * second)
            mean = jnp.sum(chosen, axis=1, keepdims=True) / cell_count
            mean = jnp.broadcast_to(mean, chosen.shape)
            picked_out[i : i + 1] = mean * scale
            seed = (mean - observed[e, k]) * scale
            seed_out[i : i + 1] = jnp.where(sample[e] == 0, seed, 0.0)
            seed_out[4 + i : 5 + i] = jnp.where(sample[e] == 1, seed, 0.0)


def main_kernel(
    fluid, pellet, porosity, adjoint, adjoint_pellet, up_in, down_in, row_in, seeds, level,
    pellet_out, late_out, direct_out, grad_out, up_out, down_out, row_out, share_out,
    fluid_pad, adjoint_pad, advect_pad, lower_next,
):
    experiments, comps, nz, nx, ny = fluid.shape
    first_x = lax.axis_index("xy") == 0
    first_z = lax.axis_index("gz") == 0
    last_z = lax.axis_index("gz") == lax.axis_size("gz") - 1
    fluid_pad[:, :, 1 : nz + 1] = fluid[...]
    adjoint_pad[:, :, 1 : nz + 1] = adjoint[...]
    advect_pad[0:nz] = ADVECT / porosity[...]
    advect_pad[nz] = jnp.where(last_z, 0.0, ADVECT / jnp.where(last_z, 1.0, down_in[8]))
    inlets = []
    for e in range(experiments):
        value = level[e].astype(jnp.float32)
        inlets.append([(1.0 + value) / 4.0, (4.0 - value) / 4.0])
        for k in range(comps):
            i = e * comps + k
            fluid_pad[e, k, 0] = jnp.where(first_z, inlets[e][k], up_in[i])
            fluid_pad[e, k, nz + 1] = jnp.where(last_z, fluid[e, k, nz - 1], down_in[i])
            adjoint_pad[e, k, 0] = up_in[4 + i]
            top = adjoint[e, k, nz - 1] + seeds[4 + i : 5 + i]
            adjoint_pad[e, k, nz] = top
            adjoint_pad[e, k, nz + 1] = jnp.where(last_z, top, down_in[4 + i])
            lower_next[e, k] = jnp.where(first_z, jnp.full((nx, ny), inlets[e][k]), 0.0)

    def plane(z, carry):
        inverse_porosity = 1.0 / porosity[z]
        advect = advect_pad[z]
        advect_above = advect_pad[z + 1] + AXIAL_MIX
        exchange = FILM_RATE * (inverse_porosity - 1.0)
        at_top = jnp.where(z == nz - 1, 1.0, 0.0)
        grad = jnp.zeros((nx, ny), jnp.float32)
        for e in range(experiments):
            here, below, above = fluid_pad[e, :, z + 1], fluid_pad[e, :, z], fluid_pad[e, :, z + 2]
            rows = jnp.stack([row_in[e * 2, pl.ds(z, 1)], row_in[e * 2 + 1, pl.ds(z, 1)]])
            flux, inverse, outer_next = film(here, pellet[e, :, 2, z], pellet[e, :, 3, z])
            nexts = (
                here
                + advect * (below - here)
                + AXIAL_MIX * (below - 2.0 * here + above)
                + RADIAL_MIX * cross_mix(here, rows, first_x)
                - exchange * flux
            )
            inverse_next = 1.0 / (1.0 + AFFINITY * (outer_next[0] + outer_next[1]))
            flux_next = (nexts - outer_next) * inverse_next
            cot = adjoint_pad[e, :, z + 1]
            core = adjoint_pellet[e, :, 0, z]
            second = adjoint_pellet[e, :, 1, z]
            third = adjoint_pellet[e, :, 2, z]
            outer = adjoint_pellet[e, :, 3, z]
            flux_cot = PELLET_GAIN * outer - exchange * cot
            direct, shell = film_back(flux_cot, flux_next, inverse_next)
            rows = jnp.stack([row_in[4 + e * 2, pl.ds(z, 1)], row_in[5 + e * 2, pl.ds(z, 1)]])
            rows = rows + at_top * jnp.stack([seeds[4 + e * 2 : 5 + e * 2], seeds[5 + e * 2 : 6 + e * 2]])
            late = (
                cot
                - (advect + 2.0 * AXIAL_MIX) * cot
                + AXIAL_MIX * adjoint_pad[e, :, z]
                + advect_above * adjoint_pad[e, :, z + 2]
                + RADIAL_MIX * cross_mix(cot, rows, first_x)
                + direct
            )
            late = late + at_top * jnp.stack([seeds[e * 2 : e * 2 + 1], seeds[e * 2 + 1 : e * 2 + 2]])
            outer_late = KEEP_END * outer + SHELL_MIX * third + shell
            third_late = KEEP_MID * third + SHELL_MIX * (second + outer)
            second_late = KEEP_MID * second + SHELL_MIX * (core + third)
            core_late = KEEP_END * core + SHELL_MIX * second
            flux_cot = PELLET_GAIN * outer_late - exchange * late
            direct, shell = film_back(flux_cot, flux, inverse)
            pellet_out[e, :, 3, z] = KEEP_END * outer_late + SHELL_MIX * third_late + shell
            pellet_out[e, :, 2, z] = KEEP_MID * third_late + SHELL_MIX * (second_late + outer_late)
            pellet_out[e, :, 1, z] = KEEP_MID * second_late + SHELL_MIX * (core_late + third_late)
            pellet_out[e, :, 0, z] = KEEP_END * core_late + SHELL_MIX * second_late
            late_out[e, :, z] = late
            direct_out[e, :, z] = direct
            term = cot * (FILM_RATE * flux_next + ADVECT * (nexts - lower_next[e])) + late * (
                FILM_RATE * flux + ADVECT * (here - below)
            )
            grad = grad + (term[0] + term[1])
            lower_next[e] = nexts
        grad_out[z] = grad * (inverse_porosity * inverse_porosity)
        return carry

    lax.fori_loop(0, nz, plane, 0)
    share = jnp.zeros((nx, ny), jnp.float32)
    for e in range(experiments):
        for k in range(comps):
            i = e * comps + k
            share = share + adjoint_pad[e, k, nz + 1] * lower_next[e, k]
            up_out[i] = late_out[e, k, nz - 1]
            down_out[i] = (advect_pad[0] + AXIAL_MIX) * late_out[e, k, 0]
            row_out[i] = jnp.where(first_x, late_out[e, k, :, nx - 1, :], late_out[e, k, :, 0, :])
    up_out[4] = share
    share_out[...] = share


def final_kernel(
    late, direct, porosity, grad, up_in, down_in, row_in, grad_in, share_in, fluid_out, grad_out
):
    experiments, comps, nz, nx, ny = late.shape
    first_x = lax.axis_index("xy") == 0
    last_z = lax.axis_index("gz") == lax.axis_size("gz") - 1
    grad_out[...] = grad[...] + grad_in[...]
    inverse_porosity = 1.0 / porosity[0]
    grad_out[0] = grad_out[0] - ADVECT * (inverse_porosity * inverse_porosity) * (up_in[4] + share_in[...])
    for z in range(nz):
        advect = ADVECT / porosity[z]
        if z < nz - 1:
            advect_above = ADVECT / porosity[z + 1] + AXIAL_MIX
        for e in range(experiments):
            here = late[e, :, z]
            lower = late[e, :, z - 1] if z > 0 else up_in[2 * e : 2 * e + 2]
            if z < nz - 1:
                upper = advect_above * late[e, :, z + 1]
            else:
                upper = jnp.where(last_z, AXIAL_MIX * here, down_in[2 * e : 2 * e + 2])
            rows = jnp.stack([row_in[e * 2, z : z + 1], row_in[e * 2 + 1, z : z + 1]])
            fluid_out[e, :, z] = (
                here
                - (advect + 2.0 * AXIAL_MIX) * here
                + AXIAL_MIX * lower
                + upper
                + RADIAL_MIX * cross_mix(here, rows, first_x)
                + direct[e, :, z]
            )


def shards(
    fluid_start,
    pellet_start,
    porosity,
    feed_level,
    sample_step,
    observed_outlet,
    adjoint_fluid_end,
    adjoint_pellet_end,
):
    f32 = jnp.float32
    experiments, comps, nz, nx, ny = fluid_start.shape
    planes = experiments * comps
    gz = lax.axis_size("gz")
    cell_count = nx * lax.axis_size("xy") * ny
    vmem = pl.BlockSpec(memory_space=pltpu.VMEM)
    smem = pl.BlockSpec(memory_space=pltpu.SMEM)
    params = pltpu.CompilerParams(vmem_limit_bytes=40 * 2**20)

    def shape(*dims):
        return jax.ShapeDtypeStruct(dims, f32)

    upward = [(i, i + 1) for i in range(gz - 1)]
    downward = [(i + 1, i) for i in range(gz - 1)]
    swap = [(0, 1), (1, 0)]

    up, down, rows = pl.pallas_call(
        pack_kernel,
        out_shape=(shape(2 * planes, nx, ny), shape(2 * planes + 1, nx, ny), shape(10, nz, ny)),
        in_specs=[vmem] * 4,
        out_specs=[vmem] * 3,
        compiler_params=params,
        name="pack",
    )(fluid_start, pellet_start, porosity, adjoint_fluid_end)
    rows_in = lax.ppermute(rows, "xy", swap)
    up_in = lax.ppermute(up, "gz", upward)
    down_in = lax.ppermute(down, "gz", downward)

    picked, seeds = pl.pallas_call(
        partial(outlet_kernel, cell_count),
        out_shape=(shape(8, ny), shape(8, ny)),
        in_specs=[vmem, vmem, smem, smem],
        out_specs=[vmem] * 2,
        name="outlet",
    )(rows, rows_in, sample_step, observed_outlet)

    stride = 4 ** ((gz - 1).bit_length() // 2 - 1) if gz > 1 else 0
    while stride:
        arrivals = []
        for k in (1, 2, 3):
            pairs = [(i, i - k * stride) for i in range(gz - 1, -1, -4 * stride) if i - k * stride >= 0]
            arrivals.append(lax.ppermute(picked, "gz", pairs))
        picked = picked + (arrivals[0] + arrivals[1] + arrivals[2])
        stride //= 4
    breakthrough = picked[:planes, 0].reshape(experiments, comps)

    adjoint_pellet, late, direct, grad, up, down, rows, share = pl.pallas_call(
        main_kernel,
        out_shape=(
            shape(*pellet_start.shape),
            shape(*fluid_start.shape),
            shape(*fluid_start.shape),
            shape(nz, nx, ny),
            shape(planes + 1, nx, ny),
            shape(planes, nx, ny),
            shape(planes, nz, ny),
            shape(nx, ny),
        ),
        in_specs=[vmem] * 9 + [smem],
        out_specs=[vmem] * 8,
        scratch_shapes=[
            pltpu.VMEM((experiments, comps, nz + 2, nx, ny), f32),
            pltpu.VMEM((experiments, comps, nz + 2, nx, ny), f32),
            pltpu.VMEM((nz + 1, nx, ny), f32),
            pltpu.VMEM((experiments, comps, nx, ny), f32),
        ],
        compiler_params=params,
        name="main",
    )(
        fluid_start, pellet_start, porosity, adjoint_fluid_end, adjoint_pellet_end,
        up_in, down_in, rows_in, seeds, feed_level,
    )
    grad_in = lax.ppermute(grad, "exp", swap)
    up_in = lax.ppermute(up, "gz", upward)
    down_in = lax.ppermute(down, "gz", downward)
    rows_in = lax.ppermute(rows, "xy", swap)
    share_in = lax.ppermute(
        share,
        ("exp", "gz"),
        [(e * gz + i, (1 - e) * gz + i + 1) for e in range(2) for i in range(gz - 1)],
    )
    adjoint_fluid, gradient = pl.pallas_call(
        final_kernel,
        out_shape=(shape(*fluid_start.shape), shape(nz, nx, ny)),
        in_specs=[vmem] * 9,
        out_specs=[vmem] * 2,
        compiler_params=params,
        name="final",
    )(late, direct, porosity, grad, up_in, down_in, rows_in, grad_in, share_in)
    return (breakthrough, adjoint_fluid, adjoint_pellet, gradient)


def solution(mesh):
    placed = (
        P("exp", None, "gz", "xy", None),
        P("exp", None, None, "gz", "xy", None),
        P("gz", "xy", None),
        P("exp"),
        P("exp"),
        P("exp", None),
        P("exp", None, "gz", "xy", None),
        P("exp", None, None, "gz", "xy", None),
    )
    return jax.shard_map(
        shards,
        mesh=mesh,
        in_specs=placed,
        out_specs=(
            P("exp", None),
            P("exp", None, "gz", "xy", None),
            P("exp", None, None, "gz", "xy", None),
            P("gz", "xy", None),
        ),
        check_vma=False,
    )
```

```python
from functools import partial

import jax
import jax.numpy as jnp
from jax import lax
from jax.experimental import pallas as pl
from jax.experimental.pallas import tpu as pltpu
from jax.sharding import PartitionSpec as P

STEPS = 2

ADVECT = 0.12
AXIAL_MIX = 0.08
RADIAL_MIX = 0.05
FILM_RATE = 0.05
SHELL_MIX = 0.2
PELLET_GAIN = 0.03
AFFINITY = 0.5

KEEP_END = 1.0 - SHELL_MIX
KEEP_MID = 1.0 - 2.0 * SHELL_MIX


def row_index(cells):
    return lax.broadcasted_iota(jnp.int32, cells.shape, cells.ndim - 2)


def lane_index(cells):
    return lax.broadcasted_iota(jnp.int32, cells.shape, cells.ndim - 1)


def cross_mix(cells, rim, first_x):
    nx, ny = cells.shape[-2:]
    row, lane = row_index(cells), lane_index(cells)
    wall = jnp.where(first_x, 0, nx - 1)
    outside = jnp.where(row == wall, cells, jnp.broadcast_to(rim, cells.shape))
    left = jnp.where(row == 0, outside, pltpu.roll(cells, 1, cells.ndim - 2))
    right = jnp.where(row == nx - 1, outside, pltpu.roll(cells, nx - 1, cells.ndim - 2))
    front = jnp.where(lane == 0, cells, pltpu.roll(cells, 1, cells.ndim - 1))
    back = jnp.where(lane == ny - 1, cells, pltpu.roll(cells, ny - 1, cells.ndim - 1))
    return (left + right) + (front + back) - 4.0 * cells


def film(fluid, inner, outer):
    inverse = 1.0 / (1.0 + AFFINITY * (outer[0] + outer[1]))
    flux = (fluid - outer) * inverse
    outer_next = outer + SHELL_MIX * (inner - outer) + PELLET_GAIN * flux
    return flux, inverse, outer_next


def film_back(flux_cot, flux, inverse):
    direct = flux_cot * inverse
    shared = AFFINITY * (direct[0] * flux[0] + direct[1] * flux[1])
    return direct, -direct - shared


def pack_kernel(
    fluid_hbm, pellet_hbm, porosity_hbm, adjoint_hbm, up_out, down_out, row_out,
    fluid, pellet, porosity, fluid_edge, adjoint_edge, sems,
):
    experiments, comps, nz, nx, ny = fluid_hbm.shape
    first_x = lax.axis_index("xy") == 0
    tile = pl.multiple_of(jnp.where(first_x, nx - 8, 0), 8)
    edge = pl.ds(tile, 8)
    moves = [
        (fluid_hbm.at[:, :, :, edge], fluid_edge),
        (adjoint_hbm.at[:, :, :, edge], adjoint_edge),
        (fluid_hbm.at[:, :, nz - 3 : nz], fluid),
        (pellet_hbm.at[:, :, 2:4, nz - 2 : nz], pellet),
        (porosity_hbm.at[nz - 2 : nz], porosity),
        (porosity_hbm.at[0], down_out.at[8]),
    ]
    for e in range(experiments):
        pair = slice(2 * e, 2 * e + 2)
        far = slice(4 + 2 * e, 6 + 2 * e)
        moves.append((fluid_hbm.at[e, :, nz - 1], up_out.at[pair]))
        moves.append((adjoint_hbm.at[e, :, nz - 1], up_out.at[far]))
        moves.append((fluid_hbm.at[e, :, 0], down_out.at[pair]))
        moves.append((adjoint_hbm.at[e, :, 0], down_out.at[far]))
    copies = [pltpu.make_async_copy(src, dst, sems.at[i]) for i, (src, dst) in enumerate(moves)]
    for copy in copies:
        copy.start()
    for copy in copies[:5]:
        copy.wait()
    for e in range(experiments):
        for k in range(comps):
            i = e * comps + k
            row_out[i] = jnp.where(first_x, fluid_edge[e, k, :, 7, :], fluid_edge[e, k, :, 0, :])
            row_out[4 + i] = jnp.where(first_x, adjoint_edge[e, k, :, 7, :], adjoint_edge[e, k, :, 0, :])
    inverse_porosity = 1.0 / porosity[...]
    advect = ADVECT * inverse_porosity
    exchange = FILM_RATE * (inverse_porosity - 1.0)
    weight_below = advect[1] + AXIAL_MIX
    rim = jnp.zeros((comps, 1, ny), jnp.float32)
    for e in range(experiments):
        nexts, shells = [], []
        for j in range(2):
            below, here, above = fluid[e, :, j], fluid[e, :, j + 1], fluid[e, :, min(j + 2, 2)]
            outer, inner = pellet[e, :, 1, j], pellet[e, :, 0, j]
            flux, _, outer_next = film(here, inner, outer)
            nexts.append(
                here
                + advect[j] * (below - here)
                + AXIAL_MIX * (below - 2.0 * here + above)
                + RADIAL_MIX * cross_mix(here, rim, first_x)
                - exchange[j] * flux
            )
            shells.append(outer_next)
        inverse = 1.0 / (1.0 + AFFINITY * (shells[1][0] + shells[1][1]))
        film_weight = exchange[1] * inverse
        weight_here = 1.0 - advect[1] - AXIAL_MIX - film_weight
        second = weight_here * nexts[1] + weight_below * nexts[0] + film_weight * shells[1]
        row_out[8, e : e + 1] = jnp.where(first_x, weight_here[nx - 1 : nx], weight_here[0:1])
        for k in range(comps):
            i = e * comps + k
            row_out[9, i : i + 1] = jnp.sum(nexts[1][k], axis=0, keepdims=True)
            row_out[9, 4 + i : 5 + i] = jnp.sum(second[k], axis=0, keepdims=True)
    row_out[8, 2:3] = jnp.where(first_x, weight_below[nx - 1 : nx], weight_below[0:1])
    row_out[8, 3:8] = jnp.zeros((5, ny), jnp.float32)
    for copy in copies[5:]:
        copy.wait()


def outlet_kernel(cell_count, mine, theirs, sample, observed, picked_out, seed_out):
    first_x = lax.axis_index("xy") == 0
    last_z = lax.axis_index("gz") == lax.axis_size("gz") - 1
    nz = mine.shape[1]
    low = [jnp.where(first_x, mine[i], theirs[i]) for i in (0, 1, 2, 3, 8, 9)]
    high = [jnp.where(first_x, theirs[i], mine[i]) for i in (0, 1, 2, 3, 8, 9)]
    total = low[5] + high[5]
    scale = jnp.where(last_z, 1.0, 0.0)
    picked_out[...] = jnp.zeros_like(picked_out)
    for e in range(2):
        for k in range(2):
            i = e * 2 + k
            top = slice(nz - 1, nz)
            below = slice(nz - 2, nz - 1)
            first = low[i][top] + high[i][top]
            second = (low[4][e : e + 1] * high[i][top] + low[4][2:3] * high[i][below]) + (
                high[4][e : e + 1] * low[i][top] + high[4][2:3] * low[i][below]
            )
            chosen = jnp.where(sample[e] == 0, total[i : i + 1] + RADIAL_MIX * first, total[4 + i : 5 + i] + RADIAL_MIX * second)
            mean = jnp.sum(chosen, axis=1, keepdims=True) / cell_count
            mean = jnp.broadcast_to(mean, chosen.shape)
            picked_out[i : i + 1] = mean * scale
            seed = (mean - observed[e, k]) * scale
            seed_out[i : i + 1] = jnp.where(sample[e] == 0, seed, 0.0)
            seed_out[4 + i : 5 + i] = jnp.where(sample[e] == 1, seed, 0.0)


def main_kernel(
    fluid, pellet, porosity, adjoint, adjoint_pellet, up_in, down_in, row_in, seeds, picked, spread_a, spread_b, spread_c, level,
    pellet_out, late_out, direct_out, grad_out, up_out, down_out, row_out, share_out, picked_out,
    fluid_pad, adjoint_pad, advect_pad, lower_next,
):
    experiments, comps, nz, nx, ny = fluid.shape
    first_x = lax.axis_index("xy") == 0
    first_z = lax.axis_index("gz") == 0
    last_z = lax.axis_index("gz") == lax.axis_size("gz") - 1
    fluid_pad[:, :, 1 : nz + 1] = fluid[...]
    adjoint_pad[:, :, 1 : nz + 1] = adjoint[...]
    advect_pad[0:nz] = ADVECT / porosity[...]
    advect_pad[nz] = jnp.where(last_z, 0.0, ADVECT / jnp.where(last_z, 1.0, down_in[8]))
    inlets = []
    for e in range(experiments):
        value = level[e].astype(jnp.float32)
        inlets.append([(1.0 + value) / 4.0, (4.0 - value) / 4.0])
        for k in range(comps):
            i = e * comps + k
            fluid_pad[e, k, 0] = jnp.where(first_z, inlets[e][k], up_in[i])
            fluid_pad[e, k, nz + 1] = jnp.where(last_z, fluid[e, k, nz - 1], down_in[i])
            adjoint_pad[e, k, 0] = up_in[4 + i]
            top = adjoint[e, k, nz - 1] + seeds[4 + i : 5 + i]
            adjoint_pad[e, k, nz] = top
            adjoint_pad[e, k, nz + 1] = jnp.where(last_z, top, down_in[4 + i])
            lower_next[e, k] = jnp.where(first_z, jnp.full((nx, ny), inlets[e][k]), 0.0)

    def plane(z, carry):
        inverse_porosity = 1.0 / porosity[z]
        advect = advect_pad[z]
        advect_above = advect_pad[z + 1] + AXIAL_MIX
        exchange = FILM_RATE * (inverse_porosity - 1.0)
        at_top = jnp.where(z == nz - 1, 1.0, 0.0)
        grad = jnp.zeros((nx, ny), jnp.float32)
        for e in range(experiments):
            here, below, above = fluid_pad[e, :, z + 1], fluid_pad[e, :, z], fluid_pad[e, :, z + 2]
            rows = jnp.stack([row_in[e * 2, pl.ds(z, 1)], row_in[e * 2 + 1, pl.ds(z, 1)]])
            flux, inverse, outer_next = film(here, pellet[e, :, 2, z], pellet[e, :, 3, z])
            nexts = (
                here
                + advect * (below - here)
                + AXIAL_MIX * (below - 2.0 * here + above)
                + RADIAL_MIX * cross_mix(here, rows, first_x)
                - exchange * flux
            )
            inverse_next = 1.0 / (1.0 + AFFINITY * (outer_next[0] + outer_next[1]))
            flux_next = (nexts - outer_next) * inverse_next
            cot = adjoint_pad[e, :, z + 1]
            core = adjoint_pellet[e, :, 0, z]
            second = adjoint_pellet[e, :, 1, z]
            third = adjoint_pellet[e, :, 2, z]
            outer = adjoint_pellet[e, :, 3, z]
            flux_cot = PELLET_GAIN * outer - exchange * cot
            direct, shell = film_back(flux_cot, flux_next, inverse_next)
            rows = jnp.stack([row_in[4 + e * 2, pl.ds(z, 1)], row_in[5 + e * 2, pl.ds(z, 1)]])
            rows = rows + at_top * jnp.stack([seeds[4 + e * 2 : 5 + e * 2], seeds[5 + e * 2 : 6 + e * 2]])
            late = (
                cot
                - (advect + 2.0 * AXIAL_MIX) * cot
                + AXIAL_MIX * adjoint_pad[e, :, z]
                + advect_above * adjoint_pad[e, :, z + 2]
                + RADIAL_MIX * cross_mix(cot, rows, first_x)
                + direct
            )
            late = late + at_top * jnp.stack([seeds[e * 2 : e * 2 + 1], seeds[e * 2 + 1 : e * 2 + 2]])
            outer_late = KEEP_END * outer + SHELL_MIX * third + shell
            third_late = KEEP_MID * third + SHELL_MIX * (second + outer)
            second_late = KEEP_MID * second + SHELL_MIX * (core + third)
            core_late = KEEP_END * core + SHELL_MIX * second
            flux_cot = PELLET_GAIN * outer_late - exchange * late
            direct, shell = film_back(flux_cot, flux, inverse)
            pellet_out[e, :, 3, z] = KEEP_END * outer_late + SHELL_MIX * third_late + shell
            pellet_out[e, :, 2, z] = KEEP_MID * third_late + SHELL_MIX * (second_late + outer_late)
            pellet_out[e, :, 1, z] = KEEP_MID * second_late + SHELL_MIX * (core_late + third_late)
            pellet_out[e, :, 0, z] = KEEP_END * core_late + SHELL_MIX * second_late
            late_out[e, :, z] = late
            direct_out[e, :, z] = direct
            term = cot * (FILM_RATE * flux_next + ADVECT * (nexts - lower_next[e])) + late * (
                FILM_RATE * flux + ADVECT * (here - below)
            )
            grad = grad + (term[0] + term[1])
            lower_next[e] = nexts
        grad_out[z] = grad * (inverse_porosity * inverse_porosity)
        return carry

    lax.fori_loop(0, nz, plane, 0)
    share = jnp.zeros((nx, ny), jnp.float32)
    for e in range(experiments):
        for k in range(comps):
            i = e * comps + k
            share = share + adjoint_pad[e, k, nz + 1] * lower_next[e, k]
            up_out[i] = late_out[e, k, nz - 1]
            down_out[i] = (advect_pad[0] + AXIAL_MIX) * late_out[e, k, 0]
            row_out[i] = jnp.where(first_x, late_out[e, k, :, nx - 1, :], late_out[e, k, :, 0, :])
    up_out[4] = share
    share_out[...] = share
    picked_out[...] = picked[...] + (spread_a[...] + spread_b[...] + spread_c[...])


def final_kernel(
    late, direct, porosity, grad, up_in, down_in, row_in, grad_in, share_in,
    picked, spread_a, spread_b, spread_c,
    fluid_out, grad_out, picked_out,
):
    experiments, comps, nz, nx, ny = late.shape
    first_x = lax.axis_index("xy") == 0
    last_z = lax.axis_index("gz") == lax.axis_size("gz") - 1
    picked_out[...] = picked[...] + (spread_a[...] + spread_b[...] + spread_c[...])
    grad_out[...] = grad[...] + grad_in[...]
    inverse_porosity = 1.0 / porosity[0]
    grad_out[0] = grad_out[0] - ADVECT * (inverse_porosity * inverse_porosity) * (up_in[4] + share_in[...])
    for z in range(nz):
        advect = ADVECT / porosity[z]
        if z < nz - 1:
            advect_above = ADVECT / porosity[z + 1] + AXIAL_MIX
        for e in range(experiments):
            here = late[e, :, z]
            lower = late[e, :, z - 1] if z > 0 else up_in[2 * e : 2 * e + 2]
            if z < nz - 1:
                upper = advect_above * late[e, :, z + 1]
            else:
                upper = jnp.where(last_z, AXIAL_MIX * here, down_in[2 * e : 2 * e + 2])
            rows = jnp.stack([row_in[e * 2, z : z + 1], row_in[e * 2 + 1, z : z + 1]])
            fluid_out[e, :, z] = (
                here
                - (advect + 2.0 * AXIAL_MIX) * here
                + AXIAL_MIX * lower
                + upper
                + RADIAL_MIX * cross_mix(here, rows, first_x)
                + direct[e, :, z]
            )


def shards(
    fluid_start,
    pellet_start,
    porosity,
    feed_level,
    sample_step,
    observed_outlet,
    adjoint_fluid_end,
    adjoint_pellet_end,
):
    f32 = jnp.float32
    experiments, comps, nz, nx, ny = fluid_start.shape
    planes = experiments * comps
    gz = lax.axis_size("gz")
    cell_count = nx * lax.axis_size("xy") * ny
    vmem = pl.BlockSpec(memory_space=pltpu.VMEM)
    smem = pl.BlockSpec(memory_space=pltpu.SMEM)
    hbm = pl.BlockSpec(memory_space=pltpu.HBM)
    params = pltpu.CompilerParams(vmem_limit_bytes=4 * 2**20)

    def shape(*dims):
        return jax.ShapeDtypeStruct(dims, f32)

    upward = [(i, i + 1) for i in range(gz - 1)]
    downward = [(i + 1, i) for i in range(gz - 1)]
    swap = [(0, 1), (1, 0)]

    up, down, rows = pl.pallas_call(
        pack_kernel,
        out_shape=(shape(2 * planes, nx, ny), shape(2 * planes + 1, nx, ny), shape(10, nz, ny)),
        in_specs=[hbm] * 4,
        out_specs=[vmem] * 3,
        scratch_shapes=[
            pltpu.VMEM((experiments, comps, 3, nx, ny), f32),
            pltpu.VMEM((experiments, comps, 2, 2, nx, ny), f32),
            pltpu.VMEM((2, nx, ny), f32),
            pltpu.VMEM((experiments, comps, nz, 8, ny), f32),
            pltpu.VMEM((experiments, comps, nz, 8, ny), f32),
            pltpu.SemaphoreType.DMA((14,)),
        ],
        compiler_params=params,
        name="pack",
    )(fluid_start, pellet_start, porosity, adjoint_fluid_end)
    rows_in = lax.ppermute(rows, "xy", swap)
    up_in = lax.ppermute(up, "gz", upward)
    down_in = lax.ppermute(down, "gz", downward)

    strides = [4**j for j in reversed(range((gz.bit_length() - 1) // 2))]

    def spread(picked, level):
        stride = strides[level] if level < len(strides) else 0
        if not stride:
            return [jnp.zeros_like(picked)] * 3
        return [
            lax.ppermute(picked, "gz", [(i, i - k * stride) for i in range(gz - 1, -1, -4 * stride)])
            for k in (1, 2, 3)
        ]

    picked, seeds = pl.pallas_call(
        partial(outlet_kernel, cell_count),
        out_shape=(shape(8, ny), shape(8, ny)),
        in_specs=[vmem, vmem, smem, smem],
        out_specs=[vmem] * 2,
        compiler_params=params,
        name="outlet",
    )(rows, rows_in, sample_step, observed_outlet)

    adjoint_pellet, late, direct, grad, up, down, rows, share, picked = pl.pallas_call(
        main_kernel,
        out_shape=(
            shape(*pellet_start.shape),
            shape(*fluid_start.shape),
            shape(*fluid_start.shape),
            shape(nz, nx, ny),
            shape(planes + 1, nx, ny),
            shape(planes, nx, ny),
            shape(planes, nz, ny),
            shape(nx, ny),
            shape(8, ny),
        ),
        in_specs=[vmem] * 13 + [smem],
        out_specs=[vmem] * 9,
        scratch_shapes=[
            pltpu.VMEM((experiments, comps, nz + 2, nx, ny), f32),
            pltpu.VMEM((experiments, comps, nz + 2, nx, ny), f32),
            pltpu.VMEM((nz + 1, nx, ny), f32),
            pltpu.VMEM((experiments, comps, nx, ny), f32),
        ],
        compiler_params=params,
        name="main",
    )(
        fluid_start, pellet_start, porosity, adjoint_fluid_end, adjoint_pellet_end,
        up_in, down_in, rows_in, seeds, picked, *spread(picked, 0), feed_level,
    )
    grad_in = lax.ppermute(grad, "exp", swap)
    up_in = lax.ppermute(up, "gz", upward)
    down_in = lax.ppermute(down, "gz", downward)
    rows_in = lax.ppermute(rows, "xy", swap)
    share_in = lax.ppermute(
        share,
        ("exp", "gz"),
        [(e * gz + i, (1 - e) * gz + i + 1) for e in range(2) for i in range(gz - 1)],
    )
    adjoint_fluid, gradient, picked = pl.pallas_call(
        final_kernel,
        out_shape=(shape(*fluid_start.shape), shape(nz, nx, ny), shape(8, ny)),
        in_specs=[vmem] * 13,
        out_specs=[vmem] * 3,
        compiler_params=params,
        name="final",
    )(late, direct, porosity, grad, up_in, down_in, rows_in, grad_in, share_in, picked, *spread(picked, 1))
    picked = picked + sum(spread(picked, 2))
    breakthrough = picked[:planes, 0].reshape(experiments, comps)
    return (breakthrough, adjoint_fluid, adjoint_pellet, gradient)


def solution(mesh):
    placed = (
        P("exp", None, "gz", "xy", None),
        P("exp", None, None, "gz", "xy", None),
        P("gz", "xy", None),
        P("exp"),
        P("exp"),
        P("exp", None),
        P("exp", None, "gz", "xy", None),
        P("exp", None, None, "gz", "xy", None),
    )
    return jax.shard_map(
        shards,
        mesh=mesh,
        in_specs=placed,
        out_specs=(
            P("exp", None),
            P("exp", None, "gz", "xy", None),
            P("exp", None, None, "gz", "xy", None),
            P("gz", "xy", None),
        ),
        check_vma=False,
    )
```

```python
from functools import partial

import jax
import jax.numpy as jnp
from jax import lax
from jax.experimental import pallas as pl
from jax.experimental.pallas import tpu as pltpu
from jax.sharding import PartitionSpec as P

STEPS = 2

ADVECT = 0.12
AXIAL_MIX = 0.08
RADIAL_MIX = 0.05
FILM_RATE = 0.05
SHELL_MIX = 0.2
PELLET_GAIN = 0.03
AFFINITY = 0.5

KEEP_END = 1.0 - SHELL_MIX
KEEP_MID = 1.0 - 2.0 * SHELL_MIX


def row_index(cells):
    return lax.broadcasted_iota(jnp.int32, cells.shape, cells.ndim - 2)


def lane_index(cells):
    return lax.broadcasted_iota(jnp.int32, cells.shape, cells.ndim - 1)


def cross_mix(cells, rim, first_x):
    nx, ny = cells.shape[-2:]
    row, lane = row_index(cells), lane_index(cells)
    wall = jnp.where(first_x, 0, nx - 1)
    outside = jnp.where(row == wall, cells, jnp.broadcast_to(rim, cells.shape))
    left = jnp.where(row == 0, outside, pltpu.roll(cells, 1, cells.ndim - 2))
    right = jnp.where(row == nx - 1, outside, pltpu.roll(cells, nx - 1, cells.ndim - 2))
    front = jnp.where(lane == 0, cells, pltpu.roll(cells, 1, cells.ndim - 1))
    back = jnp.where(lane == ny - 1, cells, pltpu.roll(cells, ny - 1, cells.ndim - 1))
    return (left + right) + (front + back) - 4.0 * cells


def film(fluid, inner, outer):
    inverse = 1.0 / (1.0 + AFFINITY * (outer[0] + outer[1]))
    flux = (fluid - outer) * inverse
    outer_next = outer + SHELL_MIX * (inner - outer) + PELLET_GAIN * flux
    return flux, inverse, outer_next


def film_back(flux_cot, flux, inverse):
    direct = flux_cot * inverse
    shared = AFFINITY * (direct[0] * flux[0] + direct[1] * flux[1])
    return direct, -direct - shared


def pack_kernel(
    fluid_hbm, pellet_hbm, porosity_hbm, adjoint_hbm, row_out,
    fluid, pellet, porosity, fluid_edge, adjoint_edge, sems,
):
    experiments, comps, nz, nx, ny = fluid_hbm.shape
    first_x = lax.axis_index("xy") == 0
    tile = pl.multiple_of(jnp.where(first_x, nx - 8, 0), 8)
    edge = pl.ds(tile, 8)
    moves = [
        (fluid_hbm.at[:, :, :, edge], fluid_edge),
        (adjoint_hbm.at[:, :, :, edge], adjoint_edge),
        (fluid_hbm.at[:, :, nz - 3 : nz], fluid),
        (pellet_hbm.at[:, :, 2:4, nz - 2 : nz], pellet),
        (porosity_hbm.at[nz - 2 : nz], porosity),
    ]
    copies = [pltpu.make_async_copy(src, dst, sems.at[i]) for i, (src, dst) in enumerate(moves)]
    for copy in copies:
        copy.start()
    for copy in copies:
        copy.wait()
    for e in range(experiments):
        for k in range(comps):
            i = e * comps + k
            row_out[i] = jnp.where(first_x, fluid_edge[e, k, :, 7, :], fluid_edge[e, k, :, 0, :])
            row_out[4 + i] = jnp.where(first_x, adjoint_edge[e, k, :, 7, :], adjoint_edge[e, k, :, 0, :])
    inverse_porosity = 1.0 / porosity[...]
    advect = ADVECT * inverse_porosity
    exchange = FILM_RATE * (inverse_porosity - 1.0)
    weight_below = advect[1] + AXIAL_MIX
    rim = jnp.zeros((comps, 1, ny), jnp.float32)
    for e in range(experiments):
        nexts, shells = [], []
        for j in range(2):
            below, here, above = fluid[e, :, j], fluid[e, :, j + 1], fluid[e, :, min(j + 2, 2)]
            outer, inner = pellet[e, :, 1, j], pellet[e, :, 0, j]
            flux, _, outer_next = film(here, inner, outer)
            nexts.append(
                here
                + advect[j] * (below - here)
                + AXIAL_MIX * (below - 2.0 * here + above)
                + RADIAL_MIX * cross_mix(here, rim, first_x)
                - exchange[j] * flux
            )
            shells.append(outer_next)
        inverse = 1.0 / (1.0 + AFFINITY * (shells[1][0] + shells[1][1]))
        film_weight = exchange[1] * inverse
        weight_here = 1.0 - advect[1] - AXIAL_MIX - film_weight
        second = weight_here * nexts[1] + weight_below * nexts[0] + film_weight * shells[1]
        row_out[8, e : e + 1] = jnp.where(first_x, weight_here[nx - 1 : nx], weight_here[0:1])
        for k in range(comps):
            i = e * comps + k
            row_out[9, i : i + 1] = jnp.sum(nexts[1][k], axis=0, keepdims=True)
            row_out[9, 4 + i : 5 + i] = jnp.sum(second[k], axis=0, keepdims=True)
    row_out[8, 2:3] = jnp.where(first_x, weight_below[nx - 1 : nx], weight_below[0:1])
    row_out[8, 3:8] = jnp.zeros((5, ny), jnp.float32)


def plane_update(
    here, below, above, rim, inner, outer, cot, cot_below, cot_above, cot_rim, shells, advect, exchange, first_x
):
    flux, inverse, outer_next = film(here, inner, outer)
    nexts = (
        here
        + advect * (below - here)
        + AXIAL_MIX * (below - 2.0 * here + above)
        + RADIAL_MIX * cross_mix(here, rim, first_x)
        - exchange * flux
    )
    inverse_next = 1.0 / (1.0 + AFFINITY * (outer_next[0] + outer_next[1]))
    direct = (PELLET_GAIN * shells[3] - exchange * cot) * inverse_next
    late = (
        cot
        - (advect + 2.0 * AXIAL_MIX) * cot
        + AXIAL_MIX * cot_below
        + cot_above
        + RADIAL_MIX * cross_mix(cot, cot_rim, first_x)
        + direct
    )
    return flux, inverse, nexts, (nexts - outer_next) * inverse_next, direct, late


def pellet_update(shells, direct, flux_next, late, flux, inverse, exchange):
    core, second, third, outer = shells
    shared = AFFINITY * (direct[0] * flux_next[0] + direct[1] * flux_next[1])
    outer_late = KEEP_END * outer + SHELL_MIX * third - direct - shared
    third_late = KEEP_MID * third + SHELL_MIX * (second + outer)
    second_late = KEEP_MID * second + SHELL_MIX * (core + third)
    core_late = KEEP_END * core + SHELL_MIX * second
    through = (PELLET_GAIN * outer_late - exchange * late) * inverse
    shared = AFFINITY * (through[0] * flux[0] + through[1] * flux[1])
    return through, (
        KEEP_END * core_late + SHELL_MIX * second_late,
        KEEP_MID * second_late + SHELL_MIX * (core_late + third_late),
        KEEP_MID * third_late + SHELL_MIX * (second_late + outer_late),
        KEEP_END * outer_late + SHELL_MIX * third_late - through - shared,
    )


def pair_of(ref, first, z):
    return jnp.stack([ref[first, pl.ds(z, 1)], ref[first + 1, pl.ds(z, 1)]])


def edge_kernel(
    cell_count,
    fluid_hbm, pellet_hbm, porosity_hbm, adjoint_hbm, adjoint_pellet_hbm, mine, theirs, sample, observed,
    up_out, down_out, seed_out, picked_out,
    fluid, pellet, porosity, adjoint, outer_cot, sems,
):
    experiments, comps, nz, nx, ny = fluid_hbm.shape
    first_x = lax.axis_index("xy") == 0
    last_z = lax.axis_index("gz") == lax.axis_size("gz") - 1
    ends = (slice(0, 2), slice(nz - 2, nz))
    moves = []
    for j, z in enumerate((0, nz - 1)):
        moves.append((fluid_hbm.at[:, :, ends[j]], fluid.at[j]))
        moves.append((adjoint_hbm.at[:, :, ends[j]], adjoint.at[j]))
        moves.append((porosity_hbm.at[ends[j]], porosity.at[j]))
        moves.append((pellet_hbm.at[:, :, 2:4, z], pellet.at[j]))
        moves.append((adjoint_pellet_hbm.at[:, :, 3, z], outer_cot.at[j]))
    copies = [pltpu.make_async_copy(src, dst, sems.at[i]) for i, (src, dst) in enumerate(moves)]
    for copy in copies:
        copy.start()

    low = [jnp.where(first_x, mine[i], theirs[i]) for i in (0, 1, 2, 3, 8, 9)]
    high = [jnp.where(first_x, theirs[i], mine[i]) for i in (0, 1, 2, 3, 8, 9)]
    total = low[5] + high[5]
    scale = jnp.where(last_z, 1.0, 0.0)
    picked_out[...] = jnp.zeros_like(picked_out)
    for e in range(2):
        for k in range(2):
            i = e * 2 + k
            top = slice(nz - 1, nz)
            below = slice(nz - 2, nz - 1)
            first = low[i][top] + high[i][top]
            second = (low[4][e : e + 1] * high[i][top] + low[4][2:3] * high[i][below]) + (
                high[4][e : e + 1] * low[i][top] + high[4][2:3] * low[i][below]
            )
            chosen = jnp.where(
                sample[e] == 0,
                total[i : i + 1] + RADIAL_MIX * first,
                total[4 + i : 5 + i] + RADIAL_MIX * second,
            )
            mean = jnp.sum(chosen, axis=1, keepdims=True) / cell_count
            mean = jnp.broadcast_to(mean, chosen.shape)
            picked_out[i : i + 1] = mean * scale
            seed = (mean - observed[e, k]) * scale
            seed_out[i : i + 1] = jnp.where(sample[e] == 0, seed, 0.0)
            seed_out[4 + i : 5 + i] = jnp.where(sample[e] == 1, seed, 0.0)

    for copy in copies:
        copy.wait()
    for j, z in enumerate((0, nz - 1)):
        inverse_porosity = 1.0 / porosity[j, j]
        advect = ADVECT * inverse_porosity
        exchange = FILM_RATE * (inverse_porosity - 1.0)
        if j == 0:
            advect_above = ADVECT / porosity[0, 1] + AXIAL_MIX
        for e in range(experiments):
            zero = jnp.zeros((comps, nx, ny), jnp.float32)
            here, cot = fluid[j, e, :, j], adjoint[j, e, :, j]
            shells = (None, None, None, outer_cot[j, e])
            _, _, nexts, _, _, late = plane_update(
                here,
                zero if j == 0 else fluid[1, e, :, 0],
                fluid[0, e, :, 1] if j == 0 else zero,
                pair_of(theirs, 2 * e, z),
                pellet[j, e, :, 0],
                pellet[j, e, :, 1],
                cot,
                zero if j == 0 else adjoint[1, e, :, 0],
                advect_above * adjoint[0, e, :, 1] if j == 0 else zero,
                pair_of(theirs, 4 + 2 * e, z),
                shells,
                advect,
                exchange,
                first_x,
            )
            pair = lambda n: slice(4 * n + 2 * e, 4 * n + 2 * e + 2)
            out = down_out if j == 0 else up_out
            out[pair(0)] = here
            out[pair(1)] = cot
            out[pair(2)] = late
            if j == 1:
                out[pair(3)] = nexts
    down_out[12] = porosity[0, 0]


def inner_kernel(
    fluid, pellet, porosity, adjoint, adjoint_pellet, row_in, seeds, picked, spread_a, spread_b, spread_c,
    pellet_out, late_out, direct_out, grad_out, next_out, picked_out,
    staged, lower_next, sems,
):
    experiments, comps, nz, nx, ny = fluid.shape
    first_x = lax.axis_index("xy") == 0
    picked_out[...] = picked[...] + (spread_a[...] + spread_b[...] + spread_c[...])
    lower_next[...] = jnp.zeros_like(lower_next)

    def send(z):
        return pltpu.make_async_copy(staged.at[z - 1], pellet_out.at[:, :, :, z], sems.at[z - 1])

    def plane(z, carry):
        inverse_porosity = 1.0 / porosity[z]
        advect = ADVECT * inverse_porosity
        advect_above = ADVECT / porosity[z + 1] + AXIAL_MIX
        exchange = FILM_RATE * (inverse_porosity - 1.0)
        under_top = jnp.where(z == nz - 2, 1.0, 0.0)
        grad = jnp.zeros((nx, ny), jnp.float32)
        for e in range(experiments):
            here, below, cot = fluid[e, :, z], fluid[e, :, z - 1], adjoint[e, :, z]
            shells = tuple(adjoint_pellet[e, :, shell, z] for shell in range(4))
            flux, inverse, nexts, flux_next, direct, late = plane_update(
                here,
                below,
                fluid[e, :, z + 1],
                pair_of(row_in, 2 * e, z),
                pellet[e, :, 2, z],
                pellet[e, :, 3, z],
                cot,
                adjoint[e, :, z - 1],
                advect_above * (adjoint[e, :, z + 1] + under_top * pair_of_rows(seeds, 4 + 2 * e)),
                pair_of(row_in, 4 + 2 * e, z),
                shells,
                advect,
                exchange,
                first_x,
            )
            through, shells = pellet_update(shells, direct, flux_next, late, flux, inverse, exchange)
            for shell in range(4):
                staged[z - 1, e, :, shell] = shells[shell]
            late_out[e, :, z] = late
            direct_out[e, :, z] = through
            term = cot * (FILM_RATE * flux_next + ADVECT * (nexts - lower_next[e])) + late * (
                FILM_RATE * flux + ADVECT * (here - below)
            )
            grad = grad + (term[0] + term[1])
            lower_next[e] = nexts
        send(z).start()
        grad_out[z] = grad * (inverse_porosity * inverse_porosity)
        return carry

    lax.fori_loop(1, nz - 1, plane, 0)
    next_out[...] = lower_next[...]
    for z in range(1, nz - 1):
        send(z).wait()


def pair_of_rows(ref, first):
    return jnp.stack([ref[first : first + 1], ref[first + 1 : first + 2]])


def outer_kernel(
    fluid, pellet, porosity, adjoint, adjoint_pellet, up_in, down_in, row_in, seeds, level,
    inner_late, inner_grad, inner_next, picked, spread_a, spread_b, spread_c, inner_pellet,
    pellet_out, late_out, direct_out, grad_out, halo_out, row_out, picked_out,
    staged, sems,
):
    experiments, comps, nz, nx, ny = fluid.shape
    first_x = lax.axis_index("xy") == 0
    first_z = lax.axis_index("gz") == 0
    last_z = lax.axis_index("gz") == lax.axis_size("gz") - 1
    picked_out[...] = picked[...] + (spread_a[...] + spread_b[...] + spread_c[...])
    grad_out[1 : nz - 1] = inner_grad[1 : nz - 1]
    sends = []
    for j, z in enumerate((0, nz - 1)):
        inverse_porosity = 1.0 / porosity[z]
        advect = ADVECT * inverse_porosity
        exchange = FILM_RATE * (inverse_porosity - 1.0)
        if j == 0:
            advect_above = ADVECT / porosity[1] + AXIAL_MIX
        else:
            advect_above = ADVECT / jnp.where(last_z, 1.0, down_in[12]) + AXIAL_MIX
        grad = jnp.zeros((nx, ny), jnp.float32)
        grad_next = jnp.zeros((nx, ny), jnp.float32)
        for e in range(experiments):
            pair = lambda n: slice(4 * n + 2 * e, 4 * n + 2 * e + 2)
            here, cot = fluid[e, :, z], adjoint[e, :, z]
            cot_rim = pair_of(row_in, 4 + 2 * e, z)
            if j == 0:
                inlets = []
                for k in range(comps):
                    value = level[e].astype(jnp.float32)
                    value = (1.0 + value) / 4.0 if k == 0 else (4.0 - value) / 4.0
                    inlets.append(jnp.full((nx, ny), value))
                inlet = jnp.stack(inlets)
                below = jnp.where(first_z, inlet, up_in[pair(0)])
                above = fluid[e, :, 1]
                cot_below = up_in[pair(1)]
                cot_above = advect_above * adjoint[e, :, 1]
                lower_next = jnp.where(first_z, inlet, up_in[pair(3)] + AXIAL_MIX * here)
                halo_out[pair(0)] = jnp.where(
                    first_z, 0.0, up_in[pair(2)] + (advect + AXIAL_MIX) * cot
                )
            else:
                seed = pair_of_rows(seeds, 4 + 2 * e)
                cot = cot + seed
                cot_rim = cot_rim + seed
                below = fluid[e, :, nz - 2]
                above = jnp.where(last_z, here, down_in[pair(0)])
                cot_below = adjoint[e, :, nz - 2]
                cot_above = jnp.where(last_z, AXIAL_MIX * cot, advect_above * down_in[pair(1)])
                lower_next = inner_next[e]
            shells = tuple(adjoint_pellet[e, :, shell, z] for shell in range(4))
            flux, inverse, nexts, flux_next, direct, late = plane_update(
                here, below, above, pair_of(row_in, 2 * e, z), pellet[e, :, 2, z], pellet[e, :, 3, z],
                cot, cot_below, cot_above, cot_rim, shells, advect, exchange, first_x,
            )
            if j == 1:
                late = late + pair_of_rows(seeds, 2 * e)
                halo_out[pair(1)] = jnp.where(
                    last_z, AXIAL_MIX * late, advect_above * (down_in[pair(2)] + AXIAL_MIX * cot)
                )
            through, shells = pellet_update(shells, direct, flux_next, late, flux, inverse, exchange)
            for shell in range(4):
                staged[j, e, :, shell] = shells[shell]
            late_out[j, e] = late
            direct_out[j, e] = through
            term = cot * (FILM_RATE * flux_next + ADVECT * (nexts - lower_next)) + late * (
                FILM_RATE * flux + ADVECT * (here - below)
            )
            grad = grad + (term[0] + term[1])
            if j == 0:
                follow = adjoint[e, :, 1] * nexts
                grad_next = grad_next + (follow[0] + follow[1])
            for k in range(comps):
                i = 2 * e + k
                if j == 0:
                    row_out[i, 1 : nz - 1] = jnp.where(
                        first_x, inner_late[e, k, 1 : nz - 1, nx - 1, :], inner_late[e, k, 1 : nz - 1, 0, :]
                    )
                row_out[i, z : z + 1] = jnp.where(first_x, late[k, nx - 1 : nx], late[k, 0:1])
        sends.append(pltpu.make_async_copy(staged.at[j], pellet_out.at[:, :, :, z], sems.at[j]))
        sends[j].start()
        grad_out[z] = grad * (inverse_porosity * inverse_porosity)
        if j == 0:
            inverse_porosity = 1.0 / porosity[1]
            grad_out[1] = grad_out[1] - ADVECT * (inverse_porosity * inverse_porosity) * grad_next
    for send in sends:
        send.wait()


def final_kernel(
    porosity, inner_late, inner_direct, edge_late, edge_direct, halo, row_in, fluid_out, done_out
):
    experiments, comps, nz, nx, ny = inner_late.shape
    first_x = lax.axis_index("xy") == 0
    done_out[...] = jnp.zeros_like(done_out)
    for z in range(nz):
        advect = ADVECT / porosity[z]
        if z < nz - 1:
            advect_above = ADVECT / porosity[z + 1] + AXIAL_MIX
        for e in range(experiments):
            def plane_at(w):
                if w in (0, nz - 1):
                    return edge_late[0 if w == 0 else 1, e]
                return inner_late[e, :, w]

            here = plane_at(z)
            lower = plane_at(z - 1) if z > 0 else halo[2 * e : 2 * e + 2]
            upper = advect_above * plane_at(z + 1) if z < nz - 1 else halo[4 + 2 * e : 6 + 2 * e]
            if z in (0, nz - 1):
                direct = edge_direct[0 if z == 0 else 1, e]
            else:
                direct = inner_direct[e, :, z]
            fluid_out[e, :, z] = (
                here
                - (advect + 2.0 * AXIAL_MIX) * here
                + AXIAL_MIX * lower
                + upper
                + RADIAL_MIX * cross_mix(here, pair_of(row_in, 2 * e, z), first_x)
                + direct
            )


def gather_kernel(grad, grad_in, picked, spread_a, spread_b, spread_c, done, grad_out, breakthrough_out):
    grad_out[...] = grad[...] + grad_in[...]
    total = (picked[0:4] + (spread_a[0:4] + spread_b[0:4] + spread_c[0:4]))[:, 0:2]
    shape = breakthrough_out.shape
    row, column = row_index(breakthrough_out), lane_index(breakthrough_out)
    value = jnp.zeros(shape, jnp.float32)
    for e in range(shape[0]):
        for k in range(shape[1]):
            i = e * shape[1] + k
            here = (row == e) & (column == k)
            value = jnp.where(here, jnp.broadcast_to(total[i : i + 1], shape), value)
    breakthrough_out[...] = value


def shards(
    fluid_start,
    pellet_start,
    porosity,
    feed_level,
    sample_step,
    observed_outlet,
    adjoint_fluid_end,
    adjoint_pellet_end,
):
    f32 = jnp.float32
    experiments, comps, nz, nx, ny = fluid_start.shape
    planes = experiments * comps
    gz = lax.axis_size("gz")
    cell_count = nx * lax.axis_size("xy") * ny
    vmem = pl.BlockSpec(memory_space=pltpu.VMEM)
    smem = pl.BlockSpec(memory_space=pltpu.SMEM)
    hbm = pl.BlockSpec(memory_space=pltpu.HBM)
    early = pltpu.CompilerParams(vmem_limit_bytes=56 * 2**20)
    params = pltpu.CompilerParams(vmem_limit_bytes=5 * 2**20)
    dma = pltpu.SemaphoreType.DMA

    def shape(*dims):
        return jax.ShapeDtypeStruct(dims, f32)

    upward = [(i, i + 1) for i in range(gz - 1)]
    downward = [(i + 1, i) for i in range(gz - 1)]
    swap = [(0, 1), (1, 0)]
    strides = [4**j for j in reversed(range((gz.bit_length() - 1) // 2))]

    def spread(picked, level):
        stride = strides[level] if level < len(strides) else 0
        if not stride:
            return [jnp.zeros_like(picked)] * 3
        return [
            lax.ppermute(picked, "gz", [(i, i - k * stride) for i in range(gz - 1, -1, -4 * stride)])
            for k in (1, 2, 3)
        ]

    rows = pl.pallas_call(
        pack_kernel,
        out_shape=shape(10, nz, ny),
        in_specs=[hbm] * 4,
        out_specs=vmem,
        scratch_shapes=[
            pltpu.VMEM((experiments, comps, 3, nx, ny), f32),
            pltpu.VMEM((experiments, comps, 2, 2, nx, ny), f32),
            pltpu.VMEM((2, nx, ny), f32),
            pltpu.VMEM((experiments, comps, nz, 8, ny), f32),
            pltpu.VMEM((experiments, comps, nz, 8, ny), f32),
            dma((5,)),
        ],
        compiler_params=early,
        name="pack",
    )(fluid_start, pellet_start, porosity, adjoint_fluid_end)
    rows_in = lax.ppermute(rows, "xy", swap)

    up, down, seeds, picked = pl.pallas_call(
        partial(edge_kernel, cell_count),
        out_shape=(shape(4 * planes, nx, ny), shape(3 * planes + 1, nx, ny), shape(8, ny), shape(8, ny)),
        in_specs=[hbm] * 5 + [vmem, vmem, smem, smem],
        out_specs=[vmem] * 4,
        scratch_shapes=[
            pltpu.VMEM((2, experiments, comps, 2, nx, ny), f32),
            pltpu.VMEM((2, experiments, comps, 2, nx, ny), f32),
            pltpu.VMEM((2, 2, nx, ny), f32),
            pltpu.VMEM((2, experiments, comps, 2, nx, ny), f32),
            pltpu.VMEM((2, experiments, comps, nx, ny), f32),
            dma((10,)),
        ],
        compiler_params=early,
        name="edge",
    )(
        fluid_start, pellet_start, porosity, adjoint_fluid_end, adjoint_pellet_end,
        rows, rows_in, sample_step, observed_outlet,
    )
    up_in = lax.ppermute(up, "gz", upward)
    down_in = lax.ppermute(down, "gz", downward)

    adjoint_pellet, late, direct, grad, next_fluid, picked = pl.pallas_call(
        inner_kernel,
        out_shape=(
            shape(*pellet_start.shape),
            shape(*fluid_start.shape),
            shape(*fluid_start.shape),
            shape(nz, nx, ny),
            shape(experiments, comps, nx, ny),
            shape(8, ny),
        ),
        in_specs=[vmem] * 11,
        out_specs=[hbm] + [vmem] * 5,
        scratch_shapes=[
            pltpu.VMEM((nz - 2, experiments, comps, 4, nx, ny), f32),
            pltpu.VMEM((experiments, comps, nx, ny), f32),
            dma((nz - 2,)),
        ],
        compiler_params=params,
        name="inner",
    )(
        fluid_start, pellet_start, porosity, adjoint_fluid_end, adjoint_pellet_end,
        rows_in, seeds, picked, *spread(picked, 0),
    )

    adjoint_pellet, edge_late, edge_direct, grad, halo, rows, picked = pl.pallas_call(
        outer_kernel,
        out_shape=(
            shape(*pellet_start.shape),
            shape(2, experiments, comps, nx, ny),
            shape(2, experiments, comps, nx, ny),
            shape(nz, nx, ny),
            shape(2 * planes, nx, ny),
            shape(planes, nz, ny),
            shape(8, ny),
        ),
        in_specs=[vmem] * 9 + [smem] + [vmem] * 7 + [hbm],
        out_specs=[hbm] + [vmem] * 6,
        scratch_shapes=[
            pltpu.VMEM((2, experiments, comps, 4, nx, ny), f32),
            dma((2,)),
        ],
        input_output_aliases={17: 0},
        compiler_params=params,
        name="outer",
    )(
        fluid_start, pellet_start, porosity, adjoint_fluid_end, adjoint_pellet_end,
        up_in, down_in, rows_in, seeds, feed_level,
        late, grad, next_fluid, picked, *spread(picked, 1), adjoint_pellet,
    )
    grad_in = lax.ppermute(grad, "exp", swap)
    rows_in = lax.ppermute(rows, "xy", swap)

    adjoint_fluid, done = pl.pallas_call(
        final_kernel,
        out_shape=(shape(*fluid_start.shape), shape(8, ny)),
        in_specs=[vmem] * 7,
        out_specs=[vmem] * 2,
        compiler_params=params,
        name="final",
    )(porosity, late, direct, edge_late, edge_direct, halo, rows_in)
    gradient, breakthrough = pl.pallas_call(
        gather_kernel,
        out_shape=(shape(nz, nx, ny), shape(experiments, comps)),
        in_specs=[vmem] * 7,
        out_specs=[vmem] * 2,
        compiler_params=params,
        name="gather",
    )(grad, grad_in, picked, *spread(picked, 2), done)
    return (breakthrough, adjoint_fluid, adjoint_pellet, gradient)


def solution(mesh):
    placed = (
        P("exp", None, "gz", "xy", None),
        P("exp", None, None, "gz", "xy", None),
        P("gz", "xy", None),
        P("exp"),
        P("exp"),
        P("exp", None),
        P("exp", None, "gz", "xy", None),
        P("exp", None, None, "gz", "xy", None),
    )
    return jax.shard_map(
        shards,
        mesh=mesh,
        in_specs=placed,
        out_specs=(
            P("exp", None),
            P("exp", None, "gz", "xy", None),
            P("exp", None, None, "gz", "xy", None),
            P("gz", "xy", None),
        ),
        check_vma=False,
    )
```

```python
from functools import partial

import jax
import jax.numpy as jnp
from jax import lax
from jax.experimental import pallas as pl
from jax.experimental.pallas import tpu as pltpu
from jax.sharding import PartitionSpec as P

STEPS = 2

ADVECT = 0.12
AXIAL_MIX = 0.08
RADIAL_MIX = 0.05
FILM_RATE = 0.05
SHELL_MIX = 0.2
PELLET_GAIN = 0.03
AFFINITY = 0.5

SPREAD = ((16, 32, 48), (4, 8, 12), (1, 2, 3))

KEEP_END = 1.0 - SHELL_MIX
KEEP_MID = 1.0 - 2.0 * SHELL_MIX


def row_index(cells):
    return lax.broadcasted_iota(jnp.int32, cells.shape, cells.ndim - 2)


def lane_index(cells):
    return lax.broadcasted_iota(jnp.int32, cells.shape, cells.ndim - 1)


def cross_mix(cells, rim, first_x):
    nx, ny = cells.shape[-2:]
    row, lane = row_index(cells), lane_index(cells)
    wall = jnp.where(first_x, 0, nx - 1)
    outside = jnp.where(row == wall, cells, jnp.broadcast_to(rim, cells.shape))
    left = jnp.where(row == 0, outside, pltpu.roll(cells, 1, cells.ndim - 2))
    right = jnp.where(row == nx - 1, outside, pltpu.roll(cells, nx - 1, cells.ndim - 2))
    front = jnp.where(lane == 0, cells, pltpu.roll(cells, 1, cells.ndim - 1))
    back = jnp.where(lane == ny - 1, cells, pltpu.roll(cells, ny - 1, cells.ndim - 1))
    return (left + right) + (front + back) - 4.0 * cells


def film(fluid, inner, outer):
    inverse = 1.0 / (1.0 + AFFINITY * (outer[0] + outer[1]))
    flux = (fluid - outer) * inverse
    outer_next = outer + SHELL_MIX * (inner - outer) + PELLET_GAIN * flux
    return flux, inverse, outer_next


def film_back(flux_cot, flux, inverse):
    direct = flux_cot * inverse
    shared = AFFINITY * (direct[0] * flux[0] + direct[1] * flux[1])
    return direct, -direct - shared


def pack_kernel(
    fluid_hbm, pellet_hbm, porosity_hbm, adjoint_hbm, row_out,
    fluid, pellet, porosity, fluid_edge, adjoint_edge, sems,
):
    experiments, comps, nz, nx, ny = fluid_hbm.shape
    first_x = lax.axis_index("xy") == 0
    tile = pl.multiple_of(jnp.where(first_x, nx - 8, 0), 8)
    edge = pl.ds(tile, 8)
    moves = [
        (fluid_hbm.at[:, :, :, edge], fluid_edge),
        (adjoint_hbm.at[:, :, :, edge], adjoint_edge),
        (fluid_hbm.at[:, :, nz - 3 : nz], fluid),
        (pellet_hbm.at[:, :, 2:4, nz - 2 : nz], pellet),
        (porosity_hbm.at[nz - 2 : nz], porosity),
    ]
    copies = [pltpu.make_async_copy(src, dst, sems.at[i]) for i, (src, dst) in enumerate(moves)]
    for copy in copies:
        copy.start()
    for copy in copies:
        copy.wait()
    for e in range(experiments):
        for k in range(comps):
            i = e * comps + k
            row_out[i] = jnp.where(first_x, fluid_edge[e, k, :, 7, :], fluid_edge[e, k, :, 0, :])
            row_out[4 + i] = jnp.where(first_x, adjoint_edge[e, k, :, 7, :], adjoint_edge[e, k, :, 0, :])
    inverse_porosity = 1.0 / porosity[...]
    advect = ADVECT * inverse_porosity
    exchange = FILM_RATE * (inverse_porosity - 1.0)
    weight_below = advect[1] + AXIAL_MIX
    rim = jnp.zeros((comps, 1, ny), jnp.float32)
    for e in range(experiments):
        nexts, shells = [], []
        for j in range(2):
            below, here, above = fluid[e, :, j], fluid[e, :, j + 1], fluid[e, :, min(j + 2, 2)]
            outer, inner = pellet[e, :, 1, j], pellet[e, :, 0, j]
            flux, _, outer_next = film(here, inner, outer)
            nexts.append(
                here
                + advect[j] * (below - here)
                + AXIAL_MIX * (below - 2.0 * here + above)
                + RADIAL_MIX * cross_mix(here, rim, first_x)
                - exchange[j] * flux
            )
            shells.append(outer_next)
        inverse = 1.0 / (1.0 + AFFINITY * (shells[1][0] + shells[1][1]))
        film_weight = exchange[1] * inverse
        weight_here = 1.0 - advect[1] - AXIAL_MIX - film_weight
        second = weight_here * nexts[1] + weight_below * nexts[0] + film_weight * shells[1]
        row_out[8, e : e + 1] = jnp.where(first_x, weight_here[nx - 1 : nx], weight_here[0:1])
        for k in range(comps):
            i = e * comps + k
            row_out[9, i : i + 1] = jnp.sum(nexts[1][k], axis=0, keepdims=True)
            row_out[9, 4 + i : 5 + i] = jnp.sum(second[k], axis=0, keepdims=True)
    row_out[8, 2:3] = jnp.where(first_x, weight_below[nx - 1 : nx], weight_below[0:1])
    row_out[8, 3:8] = jnp.zeros((5, ny), jnp.float32)


def plane_update(
    here, below, above, rim, inner, outer, cot, cot_below, cot_above, cot_rim, shells, advect, exchange, first_x
):
    flux, inverse, outer_next = film(here, inner, outer)
    nexts = (
        here
        + advect * (below - here)
        + AXIAL_MIX * (below - 2.0 * here + above)
        + RADIAL_MIX * cross_mix(here, rim, first_x)
        - exchange * flux
    )
    inverse_next = 1.0 / (1.0 + AFFINITY * (outer_next[0] + outer_next[1]))
    direct = (PELLET_GAIN * shells[3] - exchange * cot) * inverse_next
    late = (
        cot
        - (advect + 2.0 * AXIAL_MIX) * cot
        + AXIAL_MIX * cot_below
        + cot_above
        + RADIAL_MIX * cross_mix(cot, cot_rim, first_x)
        + direct
    )
    return flux, inverse, nexts, (nexts - outer_next) * inverse_next, direct, late


def pellet_update(shells, direct, flux_next, late, flux, inverse, exchange):
    core, second, third, outer = shells
    shared = AFFINITY * (direct[0] * flux_next[0] + direct[1] * flux_next[1])
    outer_late = KEEP_END * outer + SHELL_MIX * third - direct - shared
    third_late = KEEP_MID * third + SHELL_MIX * (second + outer)
    second_late = KEEP_MID * second + SHELL_MIX * (core + third)
    core_late = KEEP_END * core + SHELL_MIX * second
    through = (PELLET_GAIN * outer_late - exchange * late) * inverse
    shared = AFFINITY * (through[0] * flux[0] + through[1] * flux[1])
    return through, (
        KEEP_END * core_late + SHELL_MIX * second_late,
        KEEP_MID * second_late + SHELL_MIX * (core_late + third_late),
        KEEP_MID * third_late + SHELL_MIX * (second_late + outer_late),
        KEEP_END * outer_late + SHELL_MIX * third_late - through - shared,
    )


def pair_of(ref, first, z):
    return jnp.stack([ref[first, pl.ds(z, 1)], ref[first + 1, pl.ds(z, 1)]])


def outlet_kernel(cell_count, mine, theirs, sample, observed, seed_out, picked_out):
    nz = mine.shape[1]
    first_x = lax.axis_index("xy") == 0
    last_z = lax.axis_index("gz") == lax.axis_size("gz") - 1
    low = [jnp.where(first_x, mine[i], theirs[i]) for i in (0, 1, 2, 3, 8, 9)]
    high = [jnp.where(first_x, theirs[i], mine[i]) for i in (0, 1, 2, 3, 8, 9)]
    total = low[5] + high[5]
    scale = jnp.where(last_z, 1.0, 0.0)
    picked_out[...] = jnp.zeros_like(picked_out)
    for e in range(2):
        for k in range(2):
            i = e * 2 + k
            top = slice(nz - 1, nz)
            below = slice(nz - 2, nz - 1)
            first = low[i][top] + high[i][top]
            second = (low[4][e : e + 1] * high[i][top] + low[4][2:3] * high[i][below]) + (
                high[4][e : e + 1] * low[i][top] + high[4][2:3] * low[i][below]
            )
            chosen = jnp.where(
                sample[e] == 0,
                total[i : i + 1] + RADIAL_MIX * first,
                total[4 + i : 5 + i] + RADIAL_MIX * second,
            )
            mean = jnp.sum(chosen, axis=1, keepdims=True) / cell_count
            mean = jnp.broadcast_to(mean, chosen.shape)
            picked_out[i : i + 1] = mean * scale
            seed = (mean - observed[e, k]) * scale
            seed_out[i : i + 1] = jnp.where(sample[e] == 0, seed, 0.0)
            seed_out[4 + i : 5 + i] = jnp.where(sample[e] == 1, seed, 0.0)


def edge_kernel(
    fluid_hbm, pellet_hbm, porosity_hbm, adjoint_hbm, adjoint_pellet_hbm, theirs, seeds,
    first_out, second_out,
    fluid, pellet, porosity, adjoint, outer_cot, sems,
):
    experiments, comps, nz, nx, ny = fluid_hbm.shape
    first_x = lax.axis_index("xy") == 0
    even = lax.rem(lax.axis_index("gz"), 2) == 0

    def put(at_even, at_odd, where, value):
        @pl.when(even)
        def _():
            at_even[where] = value

        @pl.when(jnp.logical_not(even))
        def _():
            at_odd[where] = value

    ends = (slice(0, 2), slice(nz - 2, nz))
    moves = []
    for j, z in enumerate((0, nz - 1)):
        moves.append((fluid_hbm.at[:, :, ends[j]], fluid.at[j]))
        moves.append((adjoint_hbm.at[:, :, ends[j]], adjoint.at[j]))
        moves.append((porosity_hbm.at[ends[j]], porosity.at[j]))
        moves.append((pellet_hbm.at[:, :, 2:4, z], pellet.at[j]))
        moves.append((adjoint_pellet_hbm.at[:, :, 3, z], outer_cot.at[j]))
    copies = [pltpu.make_async_copy(src, dst, sems.at[i]) for i, (src, dst) in enumerate(moves)]
    for copy in copies:
        copy.start()

    for copy in copies:
        copy.wait()
    for j, z in enumerate((0, nz - 1)):
        inverse_porosity = 1.0 / porosity[j, j]
        advect = ADVECT * inverse_porosity
        exchange = FILM_RATE * (inverse_porosity - 1.0)
        if j == 0:
            advect_above = ADVECT / porosity[0, 1] + AXIAL_MIX
        for e in range(experiments):
            zero = jnp.zeros((comps, nx, ny), jnp.float32)
            here, cot = fluid[j, e, :, j], adjoint[j, e, :, j]
            shells = (None, None, None, outer_cot[j, e])
            _, _, nexts, _, _, late = plane_update(
                here,
                zero if j == 0 else fluid[1, e, :, 0],
                fluid[0, e, :, 1] if j == 0 else zero,
                pair_of(theirs, 2 * e, z),
                pellet[j, e, :, 0],
                pellet[j, e, :, 1],
                cot,
                zero if j == 0 else adjoint[1, e, :, 0],
                advect_above * adjoint[0, e, :, 1] if j == 0 else zero,
                pair_of(theirs, 4 + 2 * e, z),
                shells,
                advect,
                exchange,
                first_x,
            )
            pair = lambda n: slice(4 * n + 2 * e, 4 * n + 2 * e + 2)
            outs = (second_out, first_out) if j == 0 else (first_out, second_out)
            put(*outs, pair(0), here)
            put(*outs, pair(1), cot)
            put(*outs, pair(2), late)
            if j == 1:
                put(*outs, pair(3), nexts)
    for n in range(4 * experiments * comps - 4, 4 * experiments * comps):
        put(second_out, first_out, n, porosity[0, 0])


def inner_kernel(
    fluid, pellet, porosity, adjoint, adjoint_pellet, row_in, seeds,
    pellet_out, late_out, direct_out, grad_out, next_out,
    staged, lower_next, sems,
):
    experiments, comps, nz, nx, ny = fluid.shape
    first_x = lax.axis_index("xy") == 0
    lower_next[...] = jnp.zeros_like(lower_next)

    def send(z):
        return pltpu.make_async_copy(staged.at[z - 1], pellet_out.at[:, :, :, z], sems.at[z - 1])

    def plane(z, carry):
        inverse_porosity = 1.0 / porosity[z]
        advect = ADVECT * inverse_porosity
        advect_above = ADVECT / porosity[z + 1] + AXIAL_MIX
        exchange = FILM_RATE * (inverse_porosity - 1.0)
        under_top = jnp.where(z == nz - 2, 1.0, 0.0)
        grad = jnp.zeros((nx, ny), jnp.float32)
        for e in range(experiments):
            here, below, cot = fluid[e, :, z], fluid[e, :, z - 1], adjoint[e, :, z]
            shells = tuple(adjoint_pellet[e, :, shell, z] for shell in range(4))
            flux, inverse, nexts, flux_next, direct, late = plane_update(
                here,
                below,
                fluid[e, :, z + 1],
                pair_of(row_in, 2 * e, z),
                pellet[e, :, 2, z],
                pellet[e, :, 3, z],
                cot,
                adjoint[e, :, z - 1],
                advect_above * (adjoint[e, :, z + 1] + under_top * pair_of_rows(seeds, 4 + 2 * e)),
                pair_of(row_in, 4 + 2 * e, z),
                shells,
                advect,
                exchange,
                first_x,
            )
            through, shells = pellet_update(shells, direct, flux_next, late, flux, inverse, exchange)
            for shell in range(4):
                staged[z - 1, e, :, shell] = shells[shell]
            late_out[e, :, z] = late
            direct_out[e, :, z] = through
            term = cot * (FILM_RATE * flux_next + ADVECT * (nexts - lower_next[e])) + late * (
                FILM_RATE * flux + ADVECT * (here - below)
            )
            grad = grad + (term[0] + term[1])
            lower_next[e] = nexts
        send(z).start()
        grad_out[z] = grad * (inverse_porosity * inverse_porosity)
        return carry

    lax.fori_loop(1, nz - 1, plane, 0)
    next_out[...] = lower_next[...]
    for z in range(1, nz - 1):
        send(z).wait()


def pair_of_rows(ref, first):
    return jnp.stack([ref[first : first + 1], ref[first + 1 : first + 2]])


def outer_kernel(
    fluid, pellet, porosity, adjoint, adjoint_pellet, first_in, second_in, row_in, seeds, level,
    inner_late, inner_grad, inner_next, picked, spread_a, spread_b, spread_c, inner_pellet,
    pellet_out, late_out, direct_out, grad_out, halo_out, row_out, picked_out,
    staged, sems,
):
    experiments, comps, nz, nx, ny = fluid.shape
    first_x = lax.axis_index("xy") == 0
    first_z = lax.axis_index("gz") == 0
    last_z = lax.axis_index("gz") == lax.axis_size("gz") - 1
    even = lax.rem(lax.axis_index("gz"), 2) == 0

    def up_in(where):
        return jnp.where(even, second_in[where], first_in[where])

    def down_in(where):
        return jnp.where(even, first_in[where], second_in[where])

    picked_out[...] = picked[...] + (spread_a[...] + spread_b[...] + spread_c[...])
    grad_out[1 : nz - 1] = inner_grad[1 : nz - 1]
    sends = []
    for j, z in enumerate((0, nz - 1)):
        inverse_porosity = 1.0 / porosity[z]
        advect = ADVECT * inverse_porosity
        exchange = FILM_RATE * (inverse_porosity - 1.0)
        if j == 0:
            advect_above = ADVECT / porosity[1] + AXIAL_MIX
        else:
            advect_above = ADVECT / jnp.where(last_z, 1.0, down_in(12)) + AXIAL_MIX
        grad = jnp.zeros((nx, ny), jnp.float32)
        grad_next = jnp.zeros((nx, ny), jnp.float32)
        for e in range(experiments):
            pair = lambda n: slice(4 * n + 2 * e, 4 * n + 2 * e + 2)
            here, cot = fluid[e, :, z], adjoint[e, :, z]
            cot_rim = pair_of(row_in, 4 + 2 * e, z)
            if j == 0:
                inlets = []
                for k in range(comps):
                    value = level[e].astype(jnp.float32)
                    value = (1.0 + value) / 4.0 if k == 0 else (4.0 - value) / 4.0
                    inlets.append(jnp.full((nx, ny), value))
                inlet = jnp.stack(inlets)
                below = jnp.where(first_z, inlet, up_in(pair(0)))
                above = fluid[e, :, 1]
                cot_below = up_in(pair(1))
                cot_above = advect_above * adjoint[e, :, 1]
                lower_next = jnp.where(first_z, inlet, up_in(pair(3)) + AXIAL_MIX * here)
                halo_out[pair(0)] = jnp.where(
                    first_z, 0.0, up_in(pair(2)) + (advect + AXIAL_MIX) * cot
                )
            else:
                seed = pair_of_rows(seeds, 4 + 2 * e)
                cot = cot + seed
                cot_rim = cot_rim + seed
                below = fluid[e, :, nz - 2]
                above = jnp.where(last_z, here, down_in(pair(0)))
                cot_below = adjoint[e, :, nz - 2]
                cot_above = jnp.where(last_z, AXIAL_MIX * cot, advect_above * down_in(pair(1)))
                lower_next = inner_next[e]
            shells = tuple(adjoint_pellet[e, :, shell, z] for shell in range(4))
            flux, inverse, nexts, flux_next, direct, late = plane_update(
                here, below, above, pair_of(row_in, 2 * e, z), pellet[e, :, 2, z], pellet[e, :, 3, z],
                cot, cot_below, cot_above, cot_rim, shells, advect, exchange, first_x,
            )
            if j == 1:
                late = late + pair_of_rows(seeds, 2 * e)
                halo_out[pair(1)] = jnp.where(
                    last_z, AXIAL_MIX * late, advect_above * (down_in(pair(2)) + AXIAL_MIX * cot)
                )
            through, shells = pellet_update(shells, direct, flux_next, late, flux, inverse, exchange)
            for shell in range(4):
                staged[j, e, :, shell] = shells[shell]
            late_out[j, e] = late
            direct_out[j, e] = through
            term = cot * (FILM_RATE * flux_next + ADVECT * (nexts - lower_next)) + late * (
                FILM_RATE * flux + ADVECT * (here - below)
            )
            grad = grad + (term[0] + term[1])
            if j == 0:
                follow = adjoint[e, :, 1] * nexts
                grad_next = grad_next + (follow[0] + follow[1])
            for k in range(comps):
                i = 2 * e + k
                if j == 0:
                    row_out[i, 1 : nz - 1] = jnp.where(
                        first_x, inner_late[e, k, 1 : nz - 1, nx - 1, :], inner_late[e, k, 1 : nz - 1, 0, :]
                    )
                row_out[i, z : z + 1] = jnp.where(first_x, late[k, nx - 1 : nx], late[k, 0:1])
        sends.append(pltpu.make_async_copy(staged.at[j], pellet_out.at[:, :, :, z], sems.at[j]))
        sends[j].start()
        grad_out[z] = grad * (inverse_porosity * inverse_porosity)
        if j == 0:
            inverse_porosity = 1.0 / porosity[1]
            grad_out[1] = grad_out[1] - ADVECT * (inverse_porosity * inverse_porosity) * grad_next
    for send in sends:
        send.wait()


def final_kernel(
    porosity, inner_late, inner_direct, edge_late, edge_direct, halo, row_in, fluid_out, done_out
):
    experiments, comps, nz, nx, ny = inner_late.shape
    first_x = lax.axis_index("xy") == 0
    done_out[...] = jnp.zeros_like(done_out)
    for z in range(nz):
        advect = ADVECT / porosity[z]
        if z < nz - 1:
            advect_above = ADVECT / porosity[z + 1] + AXIAL_MIX
        for e in range(experiments):
            def plane_at(w):
                if w in (0, nz - 1):
                    return edge_late[0 if w == 0 else 1, e]
                return inner_late[e, :, w]

            here = plane_at(z)
            lower = plane_at(z - 1) if z > 0 else halo[2 * e : 2 * e + 2]
            upper = advect_above * plane_at(z + 1) if z < nz - 1 else halo[4 + 2 * e : 6 + 2 * e]
            if z in (0, nz - 1):
                direct = edge_direct[0 if z == 0 else 1, e]
            else:
                direct = inner_direct[e, :, z]
            fluid_out[e, :, z] = (
                here
                - (advect + 2.0 * AXIAL_MIX) * here
                + AXIAL_MIX * lower
                + upper
                + RADIAL_MIX * cross_mix(here, pair_of(row_in, 2 * e, z), first_x)
                + direct
            )


def gather_kernel(grad, grad_in, picked, spread_a, spread_b, spread_c, done, grad_out, breakthrough_out):
    grad_out[...] = grad[...] + grad_in[...]
    total = (picked[0:4] + (spread_a[0:4] + spread_b[0:4] + spread_c[0:4]))[:, 0:2]
    shape = breakthrough_out.shape
    row, column = row_index(breakthrough_out), lane_index(breakthrough_out)
    value = jnp.zeros(shape, jnp.float32)
    for e in range(shape[0]):
        for k in range(shape[1]):
            i = e * shape[1] + k
            here = (row == e) & (column == k)
            value = jnp.where(here, jnp.broadcast_to(total[i : i + 1], shape), value)
    breakthrough_out[...] = value


def shards(
    fluid_start,
    pellet_start,
    porosity,
    feed_level,
    sample_step,
    observed_outlet,
    adjoint_fluid_end,
    adjoint_pellet_end,
):
    f32 = jnp.float32
    experiments, comps, nz, nx, ny = fluid_start.shape
    planes = experiments * comps
    gz = lax.axis_size("gz")
    cell_count = nx * lax.axis_size("xy") * ny
    vmem = pl.BlockSpec(memory_space=pltpu.VMEM)
    smem = pl.BlockSpec(memory_space=pltpu.SMEM)
    hbm = pl.BlockSpec(memory_space=pltpu.HBM)
    params = pltpu.CompilerParams(vmem_limit_bytes=5 * 2**20)
    dma = pltpu.SemaphoreType.DMA

    def shape(*dims):
        return jax.ShapeDtypeStruct(dims, f32)

    low_pairs = [pair for i in range(0, gz - 1, 2) for pair in ((i, i + 1), (i + 1, i))]
    high_pairs = [pair for i in range(1, gz - 1, 2) for pair in ((i, i + 1), (i + 1, i))]
    swap = [(0, 1), (1, 0)]
    holders, levels = [gz - 1], []
    for offsets in SPREAD:
        level = [[(i, i - step) for i in holders] for step in offsets if step < gz]
        holders = holders + [target for pairs in level for _, target in pairs]
        levels.append(level)
    assert sorted(holders) == list(range(gz))

    def spread(picked, level):
        arrivals = [lax.ppermute(picked, "gz", pairs) for pairs in levels[level]]
        return arrivals + [jnp.zeros_like(picked)] * (3 - len(arrivals))

    in_hbm = [
        pltpu.with_memory_space_constraint(x, pltpu.HBM)
        for x in (fluid_start, pellet_start, porosity, adjoint_fluid_end, adjoint_pellet_end)
    ]
    rows = pl.pallas_call(
        pack_kernel,
        out_shape=shape(10, nz, ny),
        in_specs=[hbm] * 4,
        out_specs=vmem,
        scratch_shapes=[
            pltpu.VMEM((experiments, comps, 3, nx, ny), f32),
            pltpu.VMEM((experiments, comps, 2, 2, nx, ny), f32),
            pltpu.VMEM((2, nx, ny), f32),
            pltpu.VMEM((experiments, comps, nz, 8, ny), f32),
            pltpu.VMEM((experiments, comps, nz, 8, ny), f32),
            dma((5,)),
        ],
        compiler_params=params,
        name="pack",
    )(*in_hbm[:4])
    rows_in = lax.ppermute(rows, "xy", swap)

    seeds, picked = pl.pallas_call(
        partial(outlet_kernel, cell_count),
        out_shape=(shape(8, ny), shape(8, ny)),
        in_specs=[vmem, vmem, smem, smem],
        out_specs=[vmem] * 2,
        compiler_params=params,
        name="outlet",
    )(rows, rows_in, sample_step, observed_outlet)
    picked = picked + sum(spread(picked, 0))

    first, second = pl.pallas_call(
        edge_kernel,
        out_shape=(shape(4 * planes, nx, ny), shape(4 * planes, nx, ny)),
        in_specs=[hbm] * 5 + [vmem] * 2,
        out_specs=[vmem] * 2,
        scratch_shapes=[
            pltpu.VMEM((2, experiments, comps, 2, nx, ny), f32),
            pltpu.VMEM((2, experiments, comps, 2, nx, ny), f32),
            pltpu.VMEM((2, 2, nx, ny), f32),
            pltpu.VMEM((2, experiments, comps, 2, nx, ny), f32),
            pltpu.VMEM((2, experiments, comps, nx, ny), f32),
            dma((10,)),
        ],
        compiler_params=params,
        name="edge",
    )(*in_hbm, rows_in, seeds)
    first_in = lax.ppermute(first, "gz", low_pairs)
    second_in = lax.ppermute(second, "gz", high_pairs)

    adjoint_pellet, late, direct, grad, next_fluid = pl.pallas_call(
        inner_kernel,
        out_shape=(
            shape(*pellet_start.shape),
            shape(*fluid_start.shape),
            shape(*fluid_start.shape),
            shape(nz, nx, ny),
            shape(experiments, comps, nx, ny),
        ),
        in_specs=[vmem] * 7,
        out_specs=[hbm] + [vmem] * 4,
        scratch_shapes=[
            pltpu.VMEM((nz - 2, experiments, comps, 4, nx, ny), f32),
            pltpu.VMEM((experiments, comps, nx, ny), f32),
            dma((nz - 2,)),
        ],
        compiler_params=params,
        name="inner",
    )(
        fluid_start, pellet_start, porosity, adjoint_fluid_end, adjoint_pellet_end,
        rows_in, seeds,
    )

    adjoint_pellet, edge_late, edge_direct, grad, halo, rows, picked = pl.pallas_call(
        outer_kernel,
        out_shape=(
            shape(*pellet_start.shape),
            shape(2, experiments, comps, nx, ny),
            shape(2, experiments, comps, nx, ny),
            shape(nz, nx, ny),
            shape(2 * planes, nx, ny),
            shape(planes, nz, ny),
            shape(8, ny),
        ),
        in_specs=[vmem] * 9 + [smem] + [vmem] * 7 + [hbm],
        out_specs=[hbm] + [vmem] * 6,
        scratch_shapes=[
            pltpu.VMEM((2, experiments, comps, 4, nx, ny), f32),
            dma((2,)),
        ],
        input_output_aliases={17: 0},
        compiler_params=params,
        name="outer",
    )(
        fluid_start, pellet_start, porosity, adjoint_fluid_end, adjoint_pellet_end,
        first_in, second_in, rows_in, seeds, feed_level,
        late, grad, next_fluid, picked, *spread(picked, 1), adjoint_pellet,
    )
    grad_in = lax.ppermute(grad, "exp", swap)
    rows_in = lax.ppermute(rows, "xy", swap)

    adjoint_fluid, done = pl.pallas_call(
        final_kernel,
        out_shape=(shape(*fluid_start.shape), shape(8, ny)),
        in_specs=[vmem] * 7,
        out_specs=[vmem] * 2,
        compiler_params=params,
        name="final",
    )(porosity, late, direct, edge_late, edge_direct, halo, rows_in)
    gradient, breakthrough = pl.pallas_call(
        gather_kernel,
        out_shape=(shape(nz, nx, ny), shape(experiments, comps)),
        in_specs=[vmem] * 7,
        out_specs=[vmem] * 2,
        compiler_params=params,
        name="gather",
    )(grad, grad_in, picked, *spread(picked, 2), done)
    return (breakthrough, adjoint_fluid, adjoint_pellet, gradient)


def solution(mesh):
    placed = (
        P("exp", None, "gz", "xy", None),
        P("exp", None, None, "gz", "xy", None),
        P("gz", "xy", None),
        P("exp"),
        P("exp"),
        P("exp", None),
        P("exp", None, "gz", "xy", None),
        P("exp", None, None, "gz", "xy", None),
    )
    return jax.shard_map(
        shards,
        mesh=mesh,
        in_specs=placed,
        out_specs=(
            P("exp", None),
            P("exp", None, "gz", "xy", None),
            P("exp", None, None, "gz", "xy", None),
            P("gz", "xy", None),
        ),
        check_vma=False,
    )
```

```python
from functools import partial

import jax
import jax.numpy as jnp
from jax import lax
from jax.experimental import pallas as pl
from jax.experimental.pallas import tpu as pltpu
from jax.sharding import PartitionSpec as P

STEPS = 2

ADVECT = 0.12
AXIAL_MIX = 0.08
RADIAL_MIX = 0.05
FILM_RATE = 0.05
SHELL_MIX = 0.2
PELLET_GAIN = 0.03
AFFINITY = 0.5

SPREAD = (((0, 0, 0, 0, 0, 0, 0, 23), (0, 0, 0, 0, 0, 0, 0, 39), (0, 0, 0, 0, 0, 0, 0, 55)), ((-6, 0, 0, 0, 0, 0, 0, 2), (-4, 0, 0, 0, 0, 0, 0, 4), (-2, 0, 0, 0, 0, 0, 0, 6)), ((7, 9, 7, 9, 7, 9, 7, 9), (-1, 1, -1, 1, -1, 1, -1, 1), (8, 8, 8, 8, 8, 8, 8, 8)))

KEEP_END = 1.0 - SHELL_MIX
KEEP_MID = 1.0 - 2.0 * SHELL_MIX


def row_index(cells):
    return lax.broadcasted_iota(jnp.int32, cells.shape, cells.ndim - 2)


def lane_index(cells):
    return lax.broadcasted_iota(jnp.int32, cells.shape, cells.ndim - 1)


def cross_mix(cells, rim, first_x):
    nx, ny = cells.shape[-2:]
    row, lane = row_index(cells), lane_index(cells)
    wall = jnp.where(first_x, 0, nx - 1)
    outside = jnp.where(row == wall, cells, jnp.broadcast_to(rim, cells.shape))
    left = jnp.where(row == 0, outside, pltpu.roll(cells, 1, cells.ndim - 2))
    right = jnp.where(row == nx - 1, outside, pltpu.roll(cells, nx - 1, cells.ndim - 2))
    front = jnp.where(lane == 0, cells, pltpu.roll(cells, 1, cells.ndim - 1))
    back = jnp.where(lane == ny - 1, cells, pltpu.roll(cells, ny - 1, cells.ndim - 1))
    return (left + right) + (front + back) - 4.0 * cells


def film(fluid, inner, outer):
    inverse = 1.0 / (1.0 + AFFINITY * (outer[0] + outer[1]))
    flux = (fluid - outer) * inverse
    outer_next = outer + SHELL_MIX * (inner - outer) + PELLET_GAIN * flux
    return flux, inverse, outer_next


def film_back(flux_cot, flux, inverse):
    direct = flux_cot * inverse
    shared = AFFINITY * (direct[0] * flux[0] + direct[1] * flux[1])
    return direct, -direct - shared


def pack_kernel(
    fluid_hbm, pellet_hbm, porosity_hbm, adjoint_hbm, row_out,
    fluid, pellet, porosity, fluid_edge, adjoint_edge, sems,
):
    experiments, comps, nz, nx, ny = fluid_hbm.shape
    first_x = lax.axis_index("xy") == 0
    tile = pl.multiple_of(jnp.where(first_x, nx - 8, 0), 8)
    edge = pl.ds(tile, 8)
    moves = [
        (fluid_hbm.at[:, :, :, edge], fluid_edge),
        (adjoint_hbm.at[:, :, :, edge], adjoint_edge),
        (fluid_hbm.at[:, :, nz - 3 : nz], fluid),
        (pellet_hbm.at[:, :, 2:4, nz - 2 : nz], pellet),
        (porosity_hbm.at[nz - 2 : nz], porosity),
    ]
    copies = [pltpu.make_async_copy(src, dst, sems.at[i]) for i, (src, dst) in enumerate(moves)]
    for copy in copies:
        copy.start()
    for copy in copies:
        copy.wait()
    for e in range(experiments):
        for k in range(comps):
            i = e * comps + k
            row_out[i] = jnp.where(first_x, fluid_edge[e, k, :, 7, :], fluid_edge[e, k, :, 0, :])
            row_out[4 + i] = jnp.where(first_x, adjoint_edge[e, k, :, 7, :], adjoint_edge[e, k, :, 0, :])
    inverse_porosity = 1.0 / porosity[...]
    advect = ADVECT * inverse_porosity
    exchange = FILM_RATE * (inverse_porosity - 1.0)
    weight_below = advect[1] + AXIAL_MIX
    rim = jnp.zeros((comps, 1, ny), jnp.float32)
    for e in range(experiments):
        nexts, shells = [], []
        for j in range(2):
            below, here, above = fluid[e, :, j], fluid[e, :, j + 1], fluid[e, :, min(j + 2, 2)]
            outer, inner = pellet[e, :, 1, j], pellet[e, :, 0, j]
            flux, _, outer_next = film(here, inner, outer)
            nexts.append(
                here
                + advect[j] * (below - here)
                + AXIAL_MIX * (below - 2.0 * here + above)
                + RADIAL_MIX * cross_mix(here, rim, first_x)
                - exchange[j] * flux
            )
            shells.append(outer_next)
        inverse = 1.0 / (1.0 + AFFINITY * (shells[1][0] + shells[1][1]))
        film_weight = exchange[1] * inverse
        weight_here = 1.0 - advect[1] - AXIAL_MIX - film_weight
        second = weight_here * nexts[1] + weight_below * nexts[0] + film_weight * shells[1]
        row_out[8, e : e + 1] = jnp.where(first_x, weight_here[nx - 1 : nx], weight_here[0:1])
        for k in range(comps):
            i = e * comps + k
            row_out[9, i : i + 1] = jnp.sum(nexts[1][k], axis=0, keepdims=True)
            row_out[9, 4 + i : 5 + i] = jnp.sum(second[k], axis=0, keepdims=True)
    row_out[8, 2:3] = jnp.where(first_x, weight_below[nx - 1 : nx], weight_below[0:1])
    row_out[8, 3:8] = jnp.zeros((5, ny), jnp.float32)


def plane_update(
    here, below, above, rim, inner, outer, cot, cot_below, cot_above, cot_rim, shells, advect, exchange, first_x
):
    flux, inverse, outer_next = film(here, inner, outer)
    nexts = (
        here
        + advect * (below - here)
        + AXIAL_MIX * (below - 2.0 * here + above)
        + RADIAL_MIX * cross_mix(here, rim, first_x)
        - exchange * flux
    )
    inverse_next = 1.0 / (1.0 + AFFINITY * (outer_next[0] + outer_next[1]))
    direct = (PELLET_GAIN * shells[3] - exchange * cot) * inverse_next
    late = (
        cot
        - (advect + 2.0 * AXIAL_MIX) * cot
        + AXIAL_MIX * cot_below
        + cot_above
        + RADIAL_MIX * cross_mix(cot, cot_rim, first_x)
        + direct
    )
    return flux, inverse, nexts, (nexts - outer_next) * inverse_next, direct, late


def pellet_update(shells, direct, flux_next, late, flux, inverse, exchange):
    core, second, third, outer = shells
    shared = AFFINITY * (direct[0] * flux_next[0] + direct[1] * flux_next[1])
    outer_late = KEEP_END * outer + SHELL_MIX * third - direct - shared
    third_late = KEEP_MID * third + SHELL_MIX * (second + outer)
    second_late = KEEP_MID * second + SHELL_MIX * (core + third)
    core_late = KEEP_END * core + SHELL_MIX * second
    through = (PELLET_GAIN * outer_late - exchange * late) * inverse
    shared = AFFINITY * (through[0] * flux[0] + through[1] * flux[1])
    return through, (
        KEEP_END * core_late + SHELL_MIX * second_late,
        KEEP_MID * second_late + SHELL_MIX * (core_late + third_late),
        KEEP_MID * third_late + SHELL_MIX * (second_late + outer_late),
        KEEP_END * outer_late + SHELL_MIX * third_late - through - shared,
    )


def pair_of(ref, first, z):
    return jnp.stack([ref[first, pl.ds(z, 1)], ref[first + 1, pl.ds(z, 1)]])


def outlet_kernel(cell_count, mine, theirs, sample, observed, seed_out, picked_out):
    nz = mine.shape[1]
    first_x = lax.axis_index("xy") == 0
    last_z = lax.axis_index("gz") == lax.axis_size("gz") - 1
    low = [jnp.where(first_x, mine[i], theirs[i]) for i in (0, 1, 2, 3, 8, 9)]
    high = [jnp.where(first_x, theirs[i], mine[i]) for i in (0, 1, 2, 3, 8, 9)]
    total = low[5] + high[5]
    scale = jnp.where(last_z, 1.0, 0.0)
    picked_out[...] = jnp.zeros_like(picked_out)
    for e in range(2):
        for k in range(2):
            i = e * 2 + k
            top = slice(nz - 1, nz)
            below = slice(nz - 2, nz - 1)
            first = low[i][top] + high[i][top]
            second = (low[4][e : e + 1] * high[i][top] + low[4][2:3] * high[i][below]) + (
                high[4][e : e + 1] * low[i][top] + high[4][2:3] * low[i][below]
            )
            chosen = jnp.where(
                sample[e] == 0,
                total[i : i + 1] + RADIAL_MIX * first,
                total[4 + i : 5 + i] + RADIAL_MIX * second,
            )
            mean = jnp.sum(chosen, axis=1, keepdims=True) / cell_count
            mean = jnp.broadcast_to(mean, chosen.shape)
            picked_out[i : i + 1] = mean * scale
            seed = (mean - observed[e, k]) * scale
            seed_out[i : i + 1] = jnp.where(sample[e] == 0, seed, 0.0)
            seed_out[4 + i : 5 + i] = jnp.where(sample[e] == 1, seed, 0.0)


def edge_kernel(
    fluid_hbm, pellet_hbm, porosity_hbm, adjoint_hbm, adjoint_pellet_hbm, theirs, seeds,
    first_out, second_out,
    fluid, pellet, porosity, adjoint, outer_cot, sems,
):
    experiments, comps, nz, nx, ny = fluid_hbm.shape
    first_x = lax.axis_index("xy") == 0
    even = lax.rem(lax.axis_index("gz"), 2) == 0

    def put(at_even, at_odd, where, value):
        @pl.when(even)
        def _():
            at_even[where] = value

        @pl.when(jnp.logical_not(even))
        def _():
            at_odd[where] = value

    ends = (slice(0, 2), slice(nz - 2, nz))
    moves = []
    for j, z in enumerate((0, nz - 1)):
        moves.append((fluid_hbm.at[:, :, ends[j]], fluid.at[j]))
        moves.append((adjoint_hbm.at[:, :, ends[j]], adjoint.at[j]))
        moves.append((porosity_hbm.at[ends[j]], porosity.at[j]))
        moves.append((pellet_hbm.at[:, :, 2:4, z], pellet.at[j]))
        moves.append((adjoint_pellet_hbm.at[:, :, 3, z], outer_cot.at[j]))
    copies = [pltpu.make_async_copy(src, dst, sems.at[i]) for i, (src, dst) in enumerate(moves)]
    for copy in copies:
        copy.start()

    for copy in copies:
        copy.wait()
    for j, z in enumerate((0, nz - 1)):
        inverse_porosity = 1.0 / porosity[j, j]
        advect = ADVECT * inverse_porosity
        exchange = FILM_RATE * (inverse_porosity - 1.0)
        if j == 0:
            advect_above = ADVECT / porosity[0, 1] + AXIAL_MIX
        for e in range(experiments):
            zero = jnp.zeros((comps, nx, ny), jnp.float32)
            here, cot = fluid[j, e, :, j], adjoint[j, e, :, j]
            shells = (None, None, None, outer_cot[j, e])
            _, _, nexts, _, _, late = plane_update(
                here,
                zero if j == 0 else fluid[1, e, :, 0],
                fluid[0, e, :, 1] if j == 0 else zero,
                pair_of(theirs, 2 * e, z),
                pellet[j, e, :, 0],
                pellet[j, e, :, 1],
                cot,
                zero if j == 0 else adjoint[1, e, :, 0],
                advect_above * adjoint[0, e, :, 1] if j == 0 else zero,
                pair_of(theirs, 4 + 2 * e, z),
                shells,
                advect,
                exchange,
                first_x,
            )
            pair = lambda n: slice(4 * n + 2 * e, 4 * n + 2 * e + 2)
            outs = (second_out, first_out) if j == 0 else (first_out, second_out)
            put(*outs, pair(0), here)
            put(*outs, pair(1), cot)
            put(*outs, pair(2), late)
            if j == 1:
                put(*outs, pair(3), nexts)
    for n in range(4 * experiments * comps - 4, 4 * experiments * comps):
        put(second_out, first_out, n, porosity[0, 0])


def inner_kernel(
    fluid, pellet, porosity, adjoint, adjoint_pellet, row_in, seeds,
    pellet_out, late_out, direct_out, grad_out, next_out,
    staged, lower_next, sems,
):
    experiments, comps, nz, nx, ny = fluid.shape
    first_x = lax.axis_index("xy") == 0
    lower_next[...] = jnp.zeros_like(lower_next)

    def send(z):
        return pltpu.make_async_copy(staged.at[z - 1], pellet_out.at[:, :, :, z], sems.at[z - 1])

    def plane(z, carry):
        inverse_porosity = 1.0 / porosity[z]
        advect = ADVECT * inverse_porosity
        advect_above = ADVECT / porosity[z + 1] + AXIAL_MIX
        exchange = FILM_RATE * (inverse_porosity - 1.0)
        under_top = jnp.where(z == nz - 2, 1.0, 0.0)
        grad = jnp.zeros((nx, ny), jnp.float32)
        for e in range(experiments):
            here, below, cot = fluid[e, :, z], fluid[e, :, z - 1], adjoint[e, :, z]
            shells = tuple(adjoint_pellet[e, :, shell, z] for shell in range(4))
            flux, inverse, nexts, flux_next, direct, late = plane_update(
                here,
                below,
                fluid[e, :, z + 1],
                pair_of(row_in, 2 * e, z),
                pellet[e, :, 2, z],
                pellet[e, :, 3, z],
                cot,
                adjoint[e, :, z - 1],
                advect_above * (adjoint[e, :, z + 1] + under_top * pair_of_rows(seeds, 4 + 2 * e)),
                pair_of(row_in, 4 + 2 * e, z),
                shells,
                advect,
                exchange,
                first_x,
            )
            through, shells = pellet_update(shells, direct, flux_next, late, flux, inverse, exchange)
            for shell in range(4):
                staged[z - 1, e, :, shell] = shells[shell]
            late_out[e, :, z] = late
            direct_out[e, :, z] = through
            term = cot * (FILM_RATE * flux_next + ADVECT * (nexts - lower_next[e])) + late * (
                FILM_RATE * flux + ADVECT * (here - below)
            )
            grad = grad + (term[0] + term[1])
            lower_next[e] = nexts
        send(z).start()
        grad_out[z] = grad * (inverse_porosity * inverse_porosity)
        return carry

    lax.fori_loop(1, nz - 1, plane, 0)
    next_out[...] = lower_next[...]
    for z in range(1, nz - 1):
        send(z).wait()


def pair_of_rows(ref, first):
    return jnp.stack([ref[first : first + 1], ref[first + 1 : first + 2]])


def outer_kernel(
    fluid, pellet, porosity, adjoint, adjoint_pellet, first_in, second_in, row_in, seeds, level,
    inner_late, inner_grad, inner_next, picked, spread_a, spread_b, spread_c, inner_pellet,
    pellet_out, late_out, direct_out, grad_out, halo_out, row_out, picked_out,
    staged, sems,
):
    experiments, comps, nz, nx, ny = fluid.shape
    first_x = lax.axis_index("xy") == 0
    first_z = lax.axis_index("gz") == 0
    last_z = lax.axis_index("gz") == lax.axis_size("gz") - 1
    even = lax.rem(lax.axis_index("gz"), 2) == 0

    def up_in(where):
        return jnp.where(even, second_in[where], first_in[where])

    def down_in(where):
        return jnp.where(even, first_in[where], second_in[where])

    picked_out[...] = picked[...] + (spread_a[...] + spread_b[...] + spread_c[...])
    grad_out[1 : nz - 1] = inner_grad[1 : nz - 1]
    sends = []
    for j, z in enumerate((0, nz - 1)):
        inverse_porosity = 1.0 / porosity[z]
        advect = ADVECT * inverse_porosity
        exchange = FILM_RATE * (inverse_porosity - 1.0)
        if j == 0:
            advect_above = ADVECT / porosity[1] + AXIAL_MIX
        else:
            advect_above = ADVECT / jnp.where(last_z, 1.0, down_in(12)) + AXIAL_MIX
        grad = jnp.zeros((nx, ny), jnp.float32)
        grad_next = jnp.zeros((nx, ny), jnp.float32)
        for e in range(experiments):
            pair = lambda n: slice(4 * n + 2 * e, 4 * n + 2 * e + 2)
            here, cot = fluid[e, :, z], adjoint[e, :, z]
            cot_rim = pair_of(row_in, 4 + 2 * e, z)
            if j == 0:
                inlets = []
                for k in range(comps):
                    value = level[e].astype(jnp.float32)
                    value = (1.0 + value) / 4.0 if k == 0 else (4.0 - value) / 4.0
                    inlets.append(jnp.full((nx, ny), value))
                inlet = jnp.stack(inlets)
                below = jnp.where(first_z, inlet, up_in(pair(0)))
                above = fluid[e, :, 1]
                cot_below = up_in(pair(1))
                cot_above = advect_above * adjoint[e, :, 1]
                lower_next = jnp.where(first_z, inlet, up_in(pair(3)) + AXIAL_MIX * here)
                halo_out[pair(0)] = jnp.where(
                    first_z, 0.0, up_in(pair(2)) + (advect + AXIAL_MIX) * cot
                )
            else:
                seed = pair_of_rows(seeds, 4 + 2 * e)
                cot = cot + seed
                cot_rim = cot_rim + seed
                below = fluid[e, :, nz - 2]
                above = jnp.where(last_z, here, down_in(pair(0)))
                cot_below = adjoint[e, :, nz - 2]
                cot_above = jnp.where(last_z, AXIAL_MIX * cot, advect_above * down_in(pair(1)))
                lower_next = inner_next[e]
            shells = tuple(adjoint_pellet[e, :, shell, z] for shell in range(4))
            flux, inverse, nexts, flux_next, direct, late = plane_update(
                here, below, above, pair_of(row_in, 2 * e, z), pellet[e, :, 2, z], pellet[e, :, 3, z],
                cot, cot_below, cot_above, cot_rim, shells, advect, exchange, first_x,
            )
            if j == 1:
                late = late + pair_of_rows(seeds, 2 * e)
                halo_out[pair(1)] = jnp.where(
                    last_z, AXIAL_MIX * late, advect_above * (down_in(pair(2)) + AXIAL_MIX * cot)
                )
            through, shells = pellet_update(shells, direct, flux_next, late, flux, inverse, exchange)
            for shell in range(4):
                staged[j, e, :, shell] = shells[shell]
            late_out[j, e] = late
            direct_out[j, e] = through
            term = cot * (FILM_RATE * flux_next + ADVECT * (nexts - lower_next)) + late * (
                FILM_RATE * flux + ADVECT * (here - below)
            )
            grad = grad + (term[0] + term[1])
            if j == 0:
                follow = adjoint[e, :, 1] * nexts
                grad_next = grad_next + (follow[0] + follow[1])
            for k in range(comps):
                i = 2 * e + k
                if j == 0:
                    row_out[i, 1 : nz - 1] = jnp.where(
                        first_x, inner_late[e, k, 1 : nz - 1, nx - 1, :], inner_late[e, k, 1 : nz - 1, 0, :]
                    )
                row_out[i, z : z + 1] = jnp.where(first_x, late[k, nx - 1 : nx], late[k, 0:1])
        sends.append(pltpu.make_async_copy(staged.at[j], pellet_out.at[:, :, :, z], sems.at[j]))
        sends[j].start()
        grad_out[z] = grad * (inverse_porosity * inverse_porosity)
        if j == 0:
            inverse_porosity = 1.0 / porosity[1]
            grad_out[1] = grad_out[1] - ADVECT * (inverse_porosity * inverse_porosity) * grad_next
    for send in sends:
        send.wait()


def final_kernel(
    porosity, inner_late, inner_direct, edge_late, edge_direct, halo, row_in, fluid_out, done_out
):
    experiments, comps, nz, nx, ny = inner_late.shape
    first_x = lax.axis_index("xy") == 0
    done_out[...] = jnp.zeros_like(done_out)
    for z in range(nz):
        advect = ADVECT / porosity[z]
        if z < nz - 1:
            advect_above = ADVECT / porosity[z + 1] + AXIAL_MIX
        for e in range(experiments):
            def plane_at(w):
                if w in (0, nz - 1):
                    return edge_late[0 if w == 0 else 1, e]
                return inner_late[e, :, w]

            here = plane_at(z)
            lower = plane_at(z - 1) if z > 0 else halo[2 * e : 2 * e + 2]
            upper = advect_above * plane_at(z + 1) if z < nz - 1 else halo[4 + 2 * e : 6 + 2 * e]
            if z in (0, nz - 1):
                direct = edge_direct[0 if z == 0 else 1, e]
            else:
                direct = inner_direct[e, :, z]
            fluid_out[e, :, z] = (
                here
                - (advect + 2.0 * AXIAL_MIX) * here
                + AXIAL_MIX * lower
                + upper
                + RADIAL_MIX * cross_mix(here, pair_of(row_in, 2 * e, z), first_x)
                + direct
            )


def gather_kernel(grad, grad_in, picked, spread_a, spread_b, spread_c, done, grad_out, breakthrough_out):
    grad_out[...] = grad[...] + grad_in[...]
    total = (picked[0:4] + (spread_a[0:4] + spread_b[0:4] + spread_c[0:4]))[:, 0:2]
    shape = breakthrough_out.shape
    row, column = row_index(breakthrough_out), lane_index(breakthrough_out)
    value = jnp.zeros(shape, jnp.float32)
    for e in range(shape[0]):
        for k in range(shape[1]):
            i = e * shape[1] + k
            here = (row == e) & (column == k)
            value = jnp.where(here, jnp.broadcast_to(total[i : i + 1], shape), value)
    breakthrough_out[...] = value


def spread_levels(gz):
    holders, levels = [gz - 1], []
    for steps in SPREAD:
        level = [[(i, i - step[i % 8]) for i in holders if step[i % 8]] for step in steps]
        holders = holders + [target for pairs in level for _, target in pairs]
        levels.append(level)
    assert sorted(holders) == list(range(gz))
    return levels


def shards(
    fluid_start,
    pellet_start,
    porosity,
    feed_level,
    sample_step,
    observed_outlet,
    adjoint_fluid_end,
    adjoint_pellet_end,
):
    f32 = jnp.float32
    experiments, comps, nz, nx, ny = fluid_start.shape
    planes = experiments * comps
    gz = lax.axis_size("gz")
    cell_count = nx * lax.axis_size("xy") * ny
    vmem = pl.BlockSpec(memory_space=pltpu.VMEM)
    smem = pl.BlockSpec(memory_space=pltpu.SMEM)
    hbm = pl.BlockSpec(memory_space=pltpu.HBM)
    params = pltpu.CompilerParams(vmem_limit_bytes=5 * 2**20)
    dma = pltpu.SemaphoreType.DMA

    def shape(*dims):
        return jax.ShapeDtypeStruct(dims, f32)

    trades = ([], [])
    for i in range(gz - 1):
        for x in range(2):
            low, high = 2 * i + x, 2 * i + 2 + x
            trades[i % 2].extend([(low, high), (high, low)])
    swap = [(0, 1), (1, 0)]
    levels = spread_levels(gz)

    def spread(picked, level):
        arrivals = [lax.ppermute(picked, "gz", pairs) for pairs in levels[level]]
        return arrivals + [jnp.zeros_like(picked)] * (3 - len(arrivals))

    in_hbm = [
        pltpu.with_memory_space_constraint(x, pltpu.HBM)
        for x in (fluid_start, pellet_start, porosity, adjoint_fluid_end, adjoint_pellet_end)
    ]
    rows = pl.pallas_call(
        pack_kernel,
        out_shape=shape(10, nz, ny),
        in_specs=[hbm] * 4,
        out_specs=vmem,
        scratch_shapes=[
            pltpu.VMEM((experiments, comps, 3, nx, ny), f32),
            pltpu.VMEM((experiments, comps, 2, 2, nx, ny), f32),
            pltpu.VMEM((2, nx, ny), f32),
            pltpu.VMEM((experiments, comps, nz, 8, ny), f32),
            pltpu.VMEM((experiments, comps, nz, 8, ny), f32),
            dma((5,)),
        ],
        compiler_params=params,
        name="pack",
    )(*in_hbm[:4])
    rows_in = lax.ppermute(rows, "xy", swap)

    seeds, picked = pl.pallas_call(
        partial(outlet_kernel, cell_count),
        out_shape=(shape(8, ny), shape(8, ny)),
        in_specs=[vmem, vmem, smem, smem],
        out_specs=[vmem] * 2,
        compiler_params=params,
        name="outlet",
    )(rows, rows_in, sample_step, observed_outlet)
    picked = picked + sum(spread(picked, 0))

    first, second = pl.pallas_call(
        edge_kernel,
        out_shape=(shape(4 * planes, nx, ny), shape(4 * planes, nx, ny)),
        in_specs=[hbm] * 5 + [vmem] * 2,
        out_specs=[vmem] * 2,
        scratch_shapes=[
            pltpu.VMEM((2, experiments, comps, 2, nx, ny), f32),
            pltpu.VMEM((2, experiments, comps, 2, nx, ny), f32),
            pltpu.VMEM((2, 2, nx, ny), f32),
            pltpu.VMEM((2, experiments, comps, 2, nx, ny), f32),
            pltpu.VMEM((2, experiments, comps, nx, ny), f32),
            dma((10,)),
        ],
        compiler_params=params,
        name="edge",
    )(*in_hbm, rows_in, seeds)
    first_in = lax.ppermute(first, ("gz", "xy"), trades[0])
    second_in = lax.ppermute(second, ("gz", "xy"), trades[1])

    adjoint_pellet, late, direct, grad, next_fluid = pl.pallas_call(
        inner_kernel,
        out_shape=(
            shape(*pellet_start.shape),
            shape(*fluid_start.shape),
            shape(*fluid_start.shape),
            shape(nz, nx, ny),
            shape(experiments, comps, nx, ny),
        ),
        in_specs=[vmem] * 7,
        out_specs=[hbm] + [vmem] * 4,
        scratch_shapes=[
            pltpu.VMEM((nz - 2, experiments, comps, 4, nx, ny), f32),
            pltpu.VMEM((experiments, comps, nx, ny), f32),
            dma((nz - 2,)),
        ],
        compiler_params=params,
        cost_estimate=pl.CostEstimate(flops=10**10, bytes_accessed=10**9, transcendentals=0),
        name="inner",
    )(
        fluid_start, pellet_start, porosity, adjoint_fluid_end, adjoint_pellet_end,
        rows_in, seeds,
    )

    adjoint_pellet, edge_late, edge_direct, grad, halo, rows, picked = pl.pallas_call(
        outer_kernel,
        out_shape=(
            shape(*pellet_start.shape),
            shape(2, experiments, comps, nx, ny),
            shape(2, experiments, comps, nx, ny),
            shape(nz, nx, ny),
            shape(2 * planes, nx, ny),
            shape(planes, nz, ny),
            shape(8, ny),
        ),
        in_specs=[vmem] * 9 + [smem] + [vmem] * 7 + [hbm],
        out_specs=[hbm] + [vmem] * 6,
        scratch_shapes=[
            pltpu.VMEM((2, experiments, comps, 4, nx, ny), f32),
            dma((2,)),
        ],
        input_output_aliases={17: 0},
        compiler_params=params,
        name="outer",
    )(
        fluid_start, pellet_start, porosity, adjoint_fluid_end, adjoint_pellet_end,
        first_in, second_in, rows_in, seeds, feed_level,
        late, grad, next_fluid, picked, *spread(picked, 1), adjoint_pellet,
    )
    grad_in = lax.ppermute(grad, "exp", swap)
    rows_in = lax.ppermute(rows, "xy", swap)

    adjoint_fluid, done = pl.pallas_call(
        final_kernel,
        out_shape=(shape(*fluid_start.shape), shape(8, ny)),
        in_specs=[vmem] * 7,
        out_specs=[vmem] * 2,
        compiler_params=params,
        name="final",
    )(porosity, late, direct, edge_late, edge_direct, halo, rows_in)
    gradient, breakthrough = pl.pallas_call(
        gather_kernel,
        out_shape=(shape(nz, nx, ny), shape(experiments, comps)),
        in_specs=[vmem] * 7,
        out_specs=[vmem] * 2,
        compiler_params=params,
        name="gather",
    )(grad, grad_in, picked, *spread(picked, 2), done)
    return (breakthrough, adjoint_fluid, adjoint_pellet, gradient)


def solution(mesh):
    placed = (
        P("exp", None, "gz", "xy", None),
        P("exp", None, None, "gz", "xy", None),
        P("gz", "xy", None),
        P("exp"),
        P("exp"),
        P("exp", None),
        P("exp", None, "gz", "xy", None),
        P("exp", None, None, "gz", "xy", None),
    )
    return jax.shard_map(
        shards,
        mesh=mesh,
        in_specs=placed,
        out_specs=(
            P("exp", None),
            P("exp", None, "gz", "xy", None),
            P("exp", None, None, "gz", "xy", None),
            P("gz", "xy", None),
        ),
        check_vma=False,
    )
```

```python
from functools import partial

import jax
import jax.numpy as jnp
from jax import lax
from jax.experimental import pallas as pl
from jax.experimental.pallas import tpu as pltpu
from jax.sharding import PartitionSpec as P

STEPS = 2

ADVECT = 0.12
AXIAL_MIX = 0.08
RADIAL_MIX = 0.05
FILM_RATE = 0.05
SHELL_MIX = 0.2
PELLET_GAIN = 0.03
AFFINITY = 0.5

SPREAD = ((((126, 16), (127, 49)), ((126, 80), (127, 113))), (((16, 22), (49, 55), (80, 86), (113, 117), (126, 122), (127, 121)), ((16, 2), (49, 35), (80, 66), (113, 99), (126, 108), (127, 41)), ((16, 28), (49, 61), (80, 92), (113, 103), (126, 72), (127, 9))), (((2, 0), (3, 1), (8, 6), (9, 7), (16, 18), (17, 19), (22, 20), (23, 21), (34, 32), (35, 33), (40, 38), (41, 39), (48, 50), (49, 51), (54, 52), (55, 53), (66, 64), (67, 65), (72, 70), (73, 71), (80, 82), (81, 83), (86, 84), (87, 85), (98, 96), (99, 97), (102, 100), (103, 101), (112, 114), (113, 115), (116, 118), (117, 119), (120, 4), (121, 5), (60, 36), (61, 37), (92, 68), (93, 69), (28, 12), (29, 13), (108, 76), (109, 77), (122, 26), (123, 27), (126, 30), (127, 31)), ((8, 10), (9, 11), (22, 24), (23, 25), (28, 124), (29, 125), (40, 42), (41, 43), (48, 62), (49, 63), (54, 56), (55, 57), (60, 44), (61, 45), (72, 74), (73, 75), (80, 94), (81, 95), (86, 88), (87, 89), (92, 90), (93, 91), (102, 104), (103, 105), (108, 106), (109, 107), (126, 110), (127, 111), (2, 14), (3, 15), (34, 46), (35, 47), (66, 78), (67, 79), (122, 58), (123, 59))))

KEEP_END = 1.0 - SHELL_MIX
KEEP_MID = 1.0 - 2.0 * SHELL_MIX


def row_index(cells):
    return lax.broadcasted_iota(jnp.int32, cells.shape, cells.ndim - 2)


def lane_index(cells):
    return lax.broadcasted_iota(jnp.int32, cells.shape, cells.ndim - 1)


def cross_mix(cells, rim, first_x):
    nx, ny = cells.shape[-2:]
    row, lane = row_index(cells), lane_index(cells)
    wall = jnp.where(first_x, 0, nx - 1)
    outside = jnp.where(row == wall, cells, jnp.broadcast_to(rim, cells.shape))
    left = jnp.where(row == 0, outside, pltpu.roll(cells, 1, cells.ndim - 2))
    right = jnp.where(row == nx - 1, outside, pltpu.roll(cells, nx - 1, cells.ndim - 2))
    front = jnp.where(lane == 0, cells, pltpu.roll(cells, 1, cells.ndim - 1))
    back = jnp.where(lane == ny - 1, cells, pltpu.roll(cells, ny - 1, cells.ndim - 1))
    return (left + right) + (front + back) - 4.0 * cells


def film(fluid, inner, outer):
    inverse = 1.0 / (1.0 + AFFINITY * (outer[0] + outer[1]))
    flux = (fluid - outer) * inverse
    outer_next = outer + SHELL_MIX * (inner - outer) + PELLET_GAIN * flux
    return flux, inverse, outer_next


def film_back(flux_cot, flux, inverse):
    direct = flux_cot * inverse
    shared = AFFINITY * (direct[0] * flux[0] + direct[1] * flux[1])
    return direct, -direct - shared


def pack_kernel(
    fluid_hbm, pellet_hbm, porosity_hbm, adjoint_hbm, row_out,
    fluid, pellet, porosity, fluid_edge, adjoint_edge, sems,
):
    experiments, comps, nz, nx, ny = fluid_hbm.shape
    first_x = lax.axis_index("xy") == 0
    tile = pl.multiple_of(jnp.where(first_x, nx - 8, 0), 8)
    edge = pl.ds(tile, 8)
    moves = [
        (fluid_hbm.at[:, :, :, edge], fluid_edge),
        (adjoint_hbm.at[:, :, :, edge], adjoint_edge),
        (fluid_hbm.at[:, :, nz - 3 : nz], fluid),
        (pellet_hbm.at[:, :, 2:4, nz - 2 : nz], pellet),
        (porosity_hbm.at[nz - 2 : nz], porosity),
    ]
    copies = [pltpu.make_async_copy(src, dst, sems.at[i]) for i, (src, dst) in enumerate(moves)]
    for copy in copies:
        copy.start()
    for copy in copies:
        copy.wait()
    for e in range(experiments):
        for k in range(comps):
            i = e * comps + k
            row_out[i] = jnp.where(first_x, fluid_edge[e, k, :, 7, :], fluid_edge[e, k, :, 0, :])
            row_out[4 + i] = jnp.where(first_x, adjoint_edge[e, k, :, 7, :], adjoint_edge[e, k, :, 0, :])
    inverse_porosity = 1.0 / porosity[...]
    advect = ADVECT * inverse_porosity
    exchange = FILM_RATE * (inverse_porosity - 1.0)
    weight_below = advect[1] + AXIAL_MIX
    rim = jnp.zeros((comps, 1, ny), jnp.float32)
    for e in range(experiments):
        nexts, shells = [], []
        for j in range(2):
            below, here, above = fluid[e, :, j], fluid[e, :, j + 1], fluid[e, :, min(j + 2, 2)]
            outer, inner = pellet[e, :, 1, j], pellet[e, :, 0, j]
            flux, _, outer_next = film(here, inner, outer)
            nexts.append(
                here
                + advect[j] * (below - here)
                + AXIAL_MIX * (below - 2.0 * here + above)
                + RADIAL_MIX * cross_mix(here, rim, first_x)
                - exchange[j] * flux
            )
            shells.append(outer_next)
        inverse = 1.0 / (1.0 + AFFINITY * (shells[1][0] + shells[1][1]))
        film_weight = exchange[1] * inverse
        weight_here = 1.0 - advect[1] - AXIAL_MIX - film_weight
        second = weight_here * nexts[1] + weight_below * nexts[0] + film_weight * shells[1]
        row_out[8, e : e + 1] = jnp.where(first_x, weight_here[nx - 1 : nx], weight_here[0:1])
        for k in range(comps):
            i = e * comps + k
            row_out[9, i : i + 1] = jnp.sum(nexts[1][k], axis=0, keepdims=True)
            row_out[9, 4 + i : 5 + i] = jnp.sum(second[k], axis=0, keepdims=True)
    row_out[8, 2:3] = jnp.where(first_x, weight_below[nx - 1 : nx], weight_below[0:1])
    row_out[8, 3:8] = jnp.zeros((5, ny), jnp.float32)


def plane_update(
    here, below, above, rim, inner, outer, cot, cot_below, cot_above, cot_rim, shells, advect, exchange, first_x
):
    flux, inverse, outer_next = film(here, inner, outer)
    nexts = (
        here
        + advect * (below - here)
        + AXIAL_MIX * (below - 2.0 * here + above)
        + RADIAL_MIX * cross_mix(here, rim, first_x)
        - exchange * flux
    )
    inverse_next = 1.0 / (1.0 + AFFINITY * (outer_next[0] + outer_next[1]))
    direct = (PELLET_GAIN * shells[3] - exchange * cot) * inverse_next
    late = (
        cot
        - (advect + 2.0 * AXIAL_MIX) * cot
        + AXIAL_MIX * cot_below
        + cot_above
        + RADIAL_MIX * cross_mix(cot, cot_rim, first_x)
        + direct
    )
    return flux, inverse, nexts, (nexts - outer_next) * inverse_next, direct, late


def pellet_update(shells, direct, flux_next, late, flux, inverse, exchange):
    core, second, third, outer = shells
    shared = AFFINITY * (direct[0] * flux_next[0] + direct[1] * flux_next[1])
    outer_late = KEEP_END * outer + SHELL_MIX * third - direct - shared
    third_late = KEEP_MID * third + SHELL_MIX * (second + outer)
    second_late = KEEP_MID * second + SHELL_MIX * (core + third)
    core_late = KEEP_END * core + SHELL_MIX * second
    through = (PELLET_GAIN * outer_late - exchange * late) * inverse
    shared = AFFINITY * (through[0] * flux[0] + through[1] * flux[1])
    return through, (
        KEEP_END * core_late + SHELL_MIX * second_late,
        KEEP_MID * second_late + SHELL_MIX * (core_late + third_late),
        KEEP_MID * third_late + SHELL_MIX * (second_late + outer_late),
        KEEP_END * outer_late + SHELL_MIX * third_late - through - shared,
    )


def pair_of(ref, first, z):
    return jnp.stack([ref[first, pl.ds(z, 1)], ref[first + 1, pl.ds(z, 1)]])


def outlet_kernel(cell_count, mine, theirs, sample, observed, seed_out, picked_out):
    nz = mine.shape[1]
    first_x = lax.axis_index("xy") == 0
    last_z = lax.axis_index("gz") == lax.axis_size("gz") - 1
    low = [jnp.where(first_x, mine[i], theirs[i]) for i in (0, 1, 2, 3, 8, 9)]
    high = [jnp.where(first_x, theirs[i], mine[i]) for i in (0, 1, 2, 3, 8, 9)]
    total = low[5] + high[5]
    scale = jnp.where(last_z, 1.0, 0.0)
    picked_out[...] = jnp.zeros_like(picked_out)
    for e in range(2):
        for k in range(2):
            i = e * 2 + k
            top = slice(nz - 1, nz)
            below = slice(nz - 2, nz - 1)
            first = low[i][top] + high[i][top]
            second = (low[4][e : e + 1] * high[i][top] + low[4][2:3] * high[i][below]) + (
                high[4][e : e + 1] * low[i][top] + high[4][2:3] * low[i][below]
            )
            chosen = jnp.where(
                sample[e] == 0,
                total[i : i + 1] + RADIAL_MIX * first,
                total[4 + i : 5 + i] + RADIAL_MIX * second,
            )
            mean = jnp.sum(chosen, axis=1, keepdims=True) / cell_count
            mean = jnp.broadcast_to(mean, chosen.shape)
            picked_out[i : i + 1] = mean * scale
            seed = (mean - observed[e, k]) * scale
            seed_out[i : i + 1] = jnp.where(sample[e] == 0, seed, 0.0)
            seed_out[4 + i : 5 + i] = jnp.where(sample[e] == 1, seed, 0.0)


def edge_kernel(
    fluid_hbm, pellet_hbm, porosity_hbm, adjoint_hbm, adjoint_pellet_hbm, theirs, seeds,
    first_out, second_out,
    fluid, pellet, porosity, adjoint, outer_cot, sems,
):
    experiments, comps, nz, nx, ny = fluid_hbm.shape
    first_x = lax.axis_index("xy") == 0
    even = lax.rem(lax.axis_index("gz"), 2) == 0

    def put(at_even, at_odd, where, value):
        @pl.when(even)
        def _():
            at_even[where] = value

        @pl.when(jnp.logical_not(even))
        def _():
            at_odd[where] = value

    ends = (slice(0, 2), slice(nz - 2, nz))
    moves = []
    for j, z in enumerate((0, nz - 1)):
        moves.append((fluid_hbm.at[:, :, ends[j]], fluid.at[j]))
        moves.append((adjoint_hbm.at[:, :, ends[j]], adjoint.at[j]))
        moves.append((porosity_hbm.at[ends[j]], porosity.at[j]))
        moves.append((pellet_hbm.at[:, :, 2:4, z], pellet.at[j]))
        moves.append((adjoint_pellet_hbm.at[:, :, 3, z], outer_cot.at[j]))
    copies = [pltpu.make_async_copy(src, dst, sems.at[i]) for i, (src, dst) in enumerate(moves)]
    for copy in copies:
        copy.start()

    for copy in copies:
        copy.wait()
    for j, z in enumerate((0, nz - 1)):
        inverse_porosity = 1.0 / porosity[j, j]
        advect = ADVECT * inverse_porosity
        exchange = FILM_RATE * (inverse_porosity - 1.0)
        if j == 0:
            advect_above = ADVECT / porosity[0, 1] + AXIAL_MIX
        for e in range(experiments):
            zero = jnp.zeros((comps, nx, ny), jnp.float32)
            here, cot = fluid[j, e, :, j], adjoint[j, e, :, j]
            shells = (None, None, None, outer_cot[j, e])
            _, _, nexts, _, _, late = plane_update(
                here,
                zero if j == 0 else fluid[1, e, :, 0],
                fluid[0, e, :, 1] if j == 0 else zero,
                pair_of(theirs, 2 * e, z),
                pellet[j, e, :, 0],
                pellet[j, e, :, 1],
                cot,
                zero if j == 0 else adjoint[1, e, :, 0],
                advect_above * adjoint[0, e, :, 1] if j == 0 else zero,
                pair_of(theirs, 4 + 2 * e, z),
                shells,
                advect,
                exchange,
                first_x,
            )
            pair = lambda n: slice(4 * n + 2 * e, 4 * n + 2 * e + 2)
            outs = (second_out, first_out) if j == 0 else (first_out, second_out)
            put(*outs, pair(0), here)
            put(*outs, pair(1), cot)
            put(*outs, pair(2), late)
            if j == 1:
                put(*outs, pair(3), nexts)
    for n in range(4 * experiments * comps - 4, 4 * experiments * comps):
        put(second_out, first_out, n, porosity[0, 0])


def inner_kernel(
    fluid, pellet, porosity, adjoint, adjoint_pellet, row_in, seeds,
    pellet_out, late_out, direct_out, grad_out, next_out,
    staged, lower_next, sems,
):
    experiments, comps, nz, nx, ny = fluid.shape
    first_x = lax.axis_index("xy") == 0
    lower_next[...] = jnp.zeros_like(lower_next)

    def send(z):
        return pltpu.make_async_copy(staged.at[z - 1], pellet_out.at[:, :, :, z], sems.at[z - 1])

    def plane(z, carry):
        inverse_porosity = 1.0 / porosity[z]
        advect = ADVECT * inverse_porosity
        advect_above = ADVECT / porosity[z + 1] + AXIAL_MIX
        exchange = FILM_RATE * (inverse_porosity - 1.0)
        under_top = jnp.where(z == nz - 2, 1.0, 0.0)
        grad = jnp.zeros((nx, ny), jnp.float32)
        for e in range(experiments):
            here, below, cot = fluid[e, :, z], fluid[e, :, z - 1], adjoint[e, :, z]
            shells = tuple(adjoint_pellet[e, :, shell, z] for shell in range(4))
            flux, inverse, nexts, flux_next, direct, late = plane_update(
                here,
                below,
                fluid[e, :, z + 1],
                pair_of(row_in, 2 * e, z),
                pellet[e, :, 2, z],
                pellet[e, :, 3, z],
                cot,
                adjoint[e, :, z - 1],
                advect_above * (adjoint[e, :, z + 1] + under_top * pair_of_rows(seeds, 4 + 2 * e)),
                pair_of(row_in, 4 + 2 * e, z),
                shells,
                advect,
                exchange,
                first_x,
            )
            through, shells = pellet_update(shells, direct, flux_next, late, flux, inverse, exchange)
            for shell in range(4):
                staged[z - 1, e, :, shell] = shells[shell]
            late_out[e, :, z] = late
            direct_out[e, :, z] = through
            term = cot * (FILM_RATE * flux_next + ADVECT * (nexts - lower_next[e])) + late * (
                FILM_RATE * flux + ADVECT * (here - below)
            )
            grad = grad + (term[0] + term[1])
            lower_next[e] = nexts
        send(z).start()
        grad_out[z] = grad * (inverse_porosity * inverse_porosity)
        return carry

    lax.fori_loop(1, nz - 1, plane, 0)
    next_out[...] = lower_next[...]
    for z in range(1, nz - 1):
        send(z).wait()


def pair_of_rows(ref, first):
    return jnp.stack([ref[first : first + 1], ref[first + 1 : first + 2]])


def outer_kernel(
    fluid, pellet, porosity, adjoint, adjoint_pellet, first_in, second_in, row_in, seeds, level,
    inner_late, inner_grad, inner_next, picked, spread_a, spread_b, spread_c, inner_pellet,
    pellet_out, late_out, direct_out, grad_out, halo_out, row_out, picked_out,
    staged, sems,
):
    experiments, comps, nz, nx, ny = fluid.shape
    first_x = lax.axis_index("xy") == 0
    first_z = lax.axis_index("gz") == 0
    last_z = lax.axis_index("gz") == lax.axis_size("gz") - 1
    even = lax.rem(lax.axis_index("gz"), 2) == 0

    def up_in(where):
        return jnp.where(even, second_in[where], first_in[where])

    def down_in(where):
        return jnp.where(even, first_in[where], second_in[where])

    picked_out[...] = picked[...] + (spread_a[...] + spread_b[...] + spread_c[...])
    row_out[experiments * comps] = picked_out[...]
    grad_out[1 : nz - 1] = inner_grad[1 : nz - 1]
    sends = []
    for j, z in enumerate((0, nz - 1)):
        inverse_porosity = 1.0 / porosity[z]
        advect = ADVECT * inverse_porosity
        exchange = FILM_RATE * (inverse_porosity - 1.0)
        if j == 0:
            advect_above = ADVECT / porosity[1] + AXIAL_MIX
        else:
            advect_above = ADVECT / jnp.where(last_z, 1.0, down_in(12)) + AXIAL_MIX
        grad = jnp.zeros((nx, ny), jnp.float32)
        grad_next = jnp.zeros((nx, ny), jnp.float32)
        for e in range(experiments):
            pair = lambda n: slice(4 * n + 2 * e, 4 * n + 2 * e + 2)
            here, cot = fluid[e, :, z], adjoint[e, :, z]
            cot_rim = pair_of(row_in, 4 + 2 * e, z)
            if j == 0:
                inlets = []
                for k in range(comps):
                    value = level[e].astype(jnp.float32)
                    value = (1.0 + value) / 4.0 if k == 0 else (4.0 - value) / 4.0
                    inlets.append(jnp.full((nx, ny), value))
                inlet = jnp.stack(inlets)
                below = jnp.where(first_z, inlet, up_in(pair(0)))
                above = fluid[e, :, 1]
                cot_below = up_in(pair(1))
                cot_above = advect_above * adjoint[e, :, 1]
                lower_next = jnp.where(first_z, inlet, up_in(pair(3)) + AXIAL_MIX * here)
                halo_out[pair(0)] = jnp.where(
                    first_z, 0.0, up_in(pair(2)) + (advect + AXIAL_MIX) * cot
                )
            else:
                seed = pair_of_rows(seeds, 4 + 2 * e)
                cot = cot + seed
                cot_rim = cot_rim + seed
                below = fluid[e, :, nz - 2]
                above = jnp.where(last_z, here, down_in(pair(0)))
                cot_below = adjoint[e, :, nz - 2]
                cot_above = jnp.where(last_z, AXIAL_MIX * cot, advect_above * down_in(pair(1)))
                lower_next = inner_next[e]
            shells = tuple(adjoint_pellet[e, :, shell, z] for shell in range(4))
            flux, inverse, nexts, flux_next, direct, late = plane_update(
                here, below, above, pair_of(row_in, 2 * e, z), pellet[e, :, 2, z], pellet[e, :, 3, z],
                cot, cot_below, cot_above, cot_rim, shells, advect, exchange, first_x,
            )
            if j == 1:
                late = late + pair_of_rows(seeds, 2 * e)
                halo_out[pair(1)] = jnp.where(
                    last_z, AXIAL_MIX * late, advect_above * (down_in(pair(2)) + AXIAL_MIX * cot)
                )
            through, shells = pellet_update(shells, direct, flux_next, late, flux, inverse, exchange)
            for shell in range(4):
                staged[j, e, :, shell] = shells[shell]
            late_out[j, e] = late
            direct_out[j, e] = through
            term = cot * (FILM_RATE * flux_next + ADVECT * (nexts - lower_next)) + late * (
                FILM_RATE * flux + ADVECT * (here - below)
            )
            grad = grad + (term[0] + term[1])
            if j == 0:
                follow = adjoint[e, :, 1] * nexts
                grad_next = grad_next + (follow[0] + follow[1])
            for k in range(comps):
                i = 2 * e + k
                if j == 0:
                    row_out[i, 1 : nz - 1] = jnp.where(
                        first_x, inner_late[e, k, 1 : nz - 1, nx - 1, :], inner_late[e, k, 1 : nz - 1, 0, :]
                    )
                row_out[i, z : z + 1] = jnp.where(first_x, late[k, nx - 1 : nx], late[k, 0:1])
        sends.append(pltpu.make_async_copy(staged.at[j], pellet_out.at[:, :, :, z], sems.at[j]))
        sends[j].start()
        grad_out[z] = grad * (inverse_porosity * inverse_porosity)
        if j == 0:
            inverse_porosity = 1.0 / porosity[1]
            grad_out[1] = grad_out[1] - ADVECT * (inverse_porosity * inverse_porosity) * grad_next
    for send in sends:
        send.wait()


def final_kernel(
    porosity, inner_late, inner_direct, edge_late, edge_direct, halo, row_in, fluid_out, done_out
):
    experiments, comps, nz, nx, ny = inner_late.shape
    first_x = lax.axis_index("xy") == 0
    done_out[...] = jnp.zeros_like(done_out)
    for z in range(nz):
        advect = ADVECT / porosity[z]
        if z < nz - 1:
            advect_above = ADVECT / porosity[z + 1] + AXIAL_MIX
        for e in range(experiments):
            def plane_at(w):
                if w in (0, nz - 1):
                    return edge_late[0 if w == 0 else 1, e]
                return inner_late[e, :, w]

            here = plane_at(z)
            lower = plane_at(z - 1) if z > 0 else halo[2 * e : 2 * e + 2]
            upper = advect_above * plane_at(z + 1) if z < nz - 1 else halo[4 + 2 * e : 6 + 2 * e]
            if z in (0, nz - 1):
                direct = edge_direct[0 if z == 0 else 1, e]
            else:
                direct = inner_direct[e, :, z]
            fluid_out[e, :, z] = (
                here
                - (advect + 2.0 * AXIAL_MIX) * here
                + AXIAL_MIX * lower
                + upper
                + RADIAL_MIX * cross_mix(here, pair_of(row_in, 2 * e, z), first_x)
                + direct
            )


def gather_kernel(grad, grad_in, picked, spread_a, spread_b, spread_c, done, grad_out, breakthrough_out):
    grad_out[...] = grad[...] + grad_in[...]
    total = (picked[0:4] + (spread_a[0:4] + spread_b[0:4] + spread_c[0:4]))[:, 0:2]
    shape = breakthrough_out.shape
    row, column = row_index(breakthrough_out), lane_index(breakthrough_out)
    value = jnp.zeros(shape, jnp.float32)
    for e in range(shape[0]):
        for k in range(shape[1]):
            i = e * shape[1] + k
            here = (row == e) & (column == k)
            value = jnp.where(here, jnp.broadcast_to(total[i : i + 1], shape), value)
    breakthrough_out[...] = value


def spread_levels(gz):
    reached = {2 * gz - 2, 2 * gz - 1}
    for n, level in enumerate(SPREAD):
        if n == 2:
            reached |= {i ^ 1 for i in reached}
        senders = set(reached)
        for pairs in level:
            targets = {i for _, i in pairs}
            assert {i for i, _ in pairs} <= senders and not targets & reached
            reached |= targets
    assert reached == set(range(2 * gz))
    return SPREAD


def shards(
    fluid_start,
    pellet_start,
    porosity,
    feed_level,
    sample_step,
    observed_outlet,
    adjoint_fluid_end,
    adjoint_pellet_end,
):
    f32 = jnp.float32
    experiments, comps, nz, nx, ny = fluid_start.shape
    planes = experiments * comps
    gz = lax.axis_size("gz")
    cell_count = nx * lax.axis_size("xy") * ny
    vmem = pl.BlockSpec(memory_space=pltpu.VMEM)
    smem = pl.BlockSpec(memory_space=pltpu.SMEM)
    hbm = pl.BlockSpec(memory_space=pltpu.HBM)
    params = pltpu.CompilerParams(vmem_limit_bytes=5 * 2**20)
    dma = pltpu.SemaphoreType.DMA

    def shape(*dims):
        return jax.ShapeDtypeStruct(dims, f32)

    trades = ([], [])
    for i in range(gz - 1):
        for x in range(2):
            low, high = 2 * i + x, 2 * i + 2 + x
            trades[i % 2].extend([(low, high), (high, low)])
    swap = [(0, 1), (1, 0)]
    levels = spread_levels(gz)

    def spread(picked, level):
        arrivals = [lax.ppermute(picked, ("gz", "xy"), pairs) for pairs in levels[level]]
        return arrivals + [jnp.zeros_like(picked)] * (3 - len(arrivals))

    in_hbm = [
        pltpu.with_memory_space_constraint(x, pltpu.HBM)
        for x in (fluid_start, pellet_start, porosity, adjoint_fluid_end, adjoint_pellet_end)
    ]
    rows = pl.pallas_call(
        pack_kernel,
        out_shape=shape(10, nz, ny),
        in_specs=[hbm] * 4,
        out_specs=vmem,
        scratch_shapes=[
            pltpu.VMEM((experiments, comps, 3, nx, ny), f32),
            pltpu.VMEM((experiments, comps, 2, 2, nx, ny), f32),
            pltpu.VMEM((2, nx, ny), f32),
            pltpu.VMEM((experiments, comps, nz, 8, ny), f32),
            pltpu.VMEM((experiments, comps, nz, 8, ny), f32),
            dma((5,)),
        ],
        compiler_params=params,
        name="pack",
    )(*in_hbm[:4])
    rows_in = lax.ppermute(rows, "xy", swap)

    seeds, picked = pl.pallas_call(
        partial(outlet_kernel, cell_count),
        out_shape=(shape(8, ny), shape(8, ny)),
        in_specs=[vmem, vmem, smem, smem],
        out_specs=[vmem] * 2,
        compiler_params=params,
        name="outlet",
    )(rows, rows_in, sample_step, observed_outlet)
    picked = picked + sum(spread(picked, 0))

    first, second = pl.pallas_call(
        edge_kernel,
        out_shape=(shape(4 * planes, nx, ny), shape(4 * planes, nx, ny)),
        in_specs=[hbm] * 5 + [vmem] * 2,
        out_specs=[vmem] * 2,
        scratch_shapes=[
            pltpu.VMEM((2, experiments, comps, 2, nx, ny), f32),
            pltpu.VMEM((2, experiments, comps, 2, nx, ny), f32),
            pltpu.VMEM((2, 2, nx, ny), f32),
            pltpu.VMEM((2, experiments, comps, 2, nx, ny), f32),
            pltpu.VMEM((2, experiments, comps, nx, ny), f32),
            dma((10,)),
        ],
        compiler_params=params,
        name="edge",
    )(*in_hbm, rows_in, seeds)
    first_in = lax.ppermute(first, ("gz", "xy"), trades[0])
    second_in = lax.ppermute(second, ("gz", "xy"), trades[1])

    adjoint_pellet, late, direct, grad, next_fluid = pl.pallas_call(
        inner_kernel,
        out_shape=(
            shape(*pellet_start.shape),
            shape(*fluid_start.shape),
            shape(*fluid_start.shape),
            shape(nz, nx, ny),
            shape(experiments, comps, nx, ny),
        ),
        in_specs=[vmem] * 7,
        out_specs=[hbm] + [vmem] * 4,
        scratch_shapes=[
            pltpu.VMEM((nz - 2, experiments, comps, 4, nx, ny), f32),
            pltpu.VMEM((experiments, comps, nx, ny), f32),
            dma((nz - 2,)),
        ],
        compiler_params=params,
        cost_estimate=pl.CostEstimate(flops=10**10, bytes_accessed=10**9, transcendentals=0),
        name="inner",
    )(
        fluid_start, pellet_start, porosity, adjoint_fluid_end, adjoint_pellet_end,
        rows_in, seeds,
    )

    adjoint_pellet, edge_late, edge_direct, grad, halo, rows, picked = pl.pallas_call(
        outer_kernel,
        out_shape=(
            shape(*pellet_start.shape),
            shape(2, experiments, comps, nx, ny),
            shape(2, experiments, comps, nx, ny),
            shape(nz, nx, ny),
            shape(2 * planes, nx, ny),
            shape(planes + 1, nz, ny),
            shape(8, ny),
        ),
        in_specs=[vmem] * 9 + [smem] + [vmem] * 7 + [hbm],
        out_specs=[hbm] + [vmem] * 6,
        scratch_shapes=[
            pltpu.VMEM((2, experiments, comps, 4, nx, ny), f32),
            dma((2,)),
        ],
        input_output_aliases={17: 0},
        compiler_params=params,
        name="outer",
    )(
        fluid_start, pellet_start, porosity, adjoint_fluid_end, adjoint_pellet_end,
        first_in, second_in, rows_in, seeds, feed_level,
        late, grad, next_fluid, picked, *spread(picked, 1), adjoint_pellet,
    )
    grad_in = lax.ppermute(grad, "exp", swap)
    rows_in = lax.ppermute(rows, "xy", swap)
    last_z = lax.axis_index("gz") == gz - 1
    picked = picked + jnp.where(last_z, 0.0, rows_in[planes])

    adjoint_fluid, done = pl.pallas_call(
        final_kernel,
        out_shape=(shape(*fluid_start.shape), shape(8, ny)),
        in_specs=[vmem] * 7,
        out_specs=[vmem] * 2,
        compiler_params=params,
        name="final",
    )(porosity, late, direct, edge_late, edge_direct, halo, rows_in)
    gradient, breakthrough = pl.pallas_call(
        gather_kernel,
        out_shape=(shape(nz, nx, ny), shape(experiments, comps)),
        in_specs=[vmem] * 7,
        out_specs=[vmem] * 2,
        compiler_params=params,
        name="gather",
    )(grad, grad_in, picked, *spread(picked, 2), done)
    return (breakthrough, adjoint_fluid, adjoint_pellet, gradient)


def solution(mesh):
    placed = (
        P("exp", None, "gz", "xy", None),
        P("exp", None, None, "gz", "xy", None),
        P("gz", "xy", None),
        P("exp"),
        P("exp"),
        P("exp", None),
        P("exp", None, "gz", "xy", None),
        P("exp", None, None, "gz", "xy", None),
    )
    return jax.shard_map(
        shards,
        mesh=mesh,
        in_specs=placed,
        out_specs=(
            P("exp", None),
            P("exp", None, "gz", "xy", None),
            P("exp", None, None, "gz", "xy", None),
            P("gz", "xy", None),
        ),
        check_vma=False,
    )
```

```python
from functools import partial

import jax
import jax.numpy as jnp
from jax import lax
from jax.experimental import pallas as pl
from jax.experimental.pallas import tpu as pltpu
from jax.sharding import PartitionSpec as P

STEPS = 2

ADVECT = 0.12
AXIAL_MIX = 0.08
RADIAL_MIX = 0.05
FILM_RATE = 0.05
SHELL_MIX = 0.2
PELLET_GAIN = 0.03
AFFINITY = 0.5

SPREAD = ((((126, 20), (127, 53)), ((126, 84), (127, 117))), (((20, 18), (53, 51), (84, 82), (117, 101), (126, 68), (127, 5)), ((20, 24), (53, 57), (84, 88), (117, 115), (126, 106), (127, 37)), ((20, 10), (53, 43), (84, 74), (117, 121), (126, 108), (127, 125))), (((18, 0), (19, 1), (20, 16), (21, 17), (4, 2), (5, 3), (24, 22), (25, 23), (10, 6), (11, 7), (50, 32), (51, 33), (52, 48), (53, 49), (36, 34), (37, 35), (56, 54), (57, 55), (42, 38), (43, 39), (82, 64), (83, 65), (84, 80), (85, 81), (68, 66), (69, 67), (88, 86), (89, 87), (74, 70), (75, 71), (114, 96), (115, 97), (116, 112), (117, 113), (100, 98), (101, 99), (120, 118), (121, 119), (106, 102), (107, 103), (108, 110), (109, 111), (124, 122), (125, 123), (126, 104), (127, 105)), ((20, 28), (21, 29), (24, 30), (25, 31), (10, 12), (11, 13), (4, 8), (5, 9), (52, 60), (53, 61), (56, 62), (57, 63), (42, 44), (43, 45), (36, 40), (37, 41), (84, 92), (85, 93), (88, 94), (89, 95), (74, 76), (75, 77), (68, 72), (69, 73), (18, 14), (19, 15), (126, 78), (127, 79), (50, 46), (51, 47), (120, 58), (121, 59), (124, 90), (125, 91), (106, 26), (107, 27))))

KEEP_END = 1.0 - SHELL_MIX
KEEP_MID = 1.0 - 2.0 * SHELL_MIX


def row_index(cells):
    return lax.broadcasted_iota(jnp.int32, cells.shape, cells.ndim - 2)


def lane_index(cells):
    return lax.broadcasted_iota(jnp.int32, cells.shape, cells.ndim - 1)


def cross_mix(cells, rim, first_x):
    nx, ny = cells.shape[-2:]
    row, lane = row_index(cells), lane_index(cells)
    wall = jnp.where(first_x, 0, nx - 1)
    outside = jnp.where(row == wall, cells, jnp.broadcast_to(rim, cells.shape))
    left = jnp.where(row == 0, outside, pltpu.roll(cells, 1, cells.ndim - 2))
    right = jnp.where(row == nx - 1, outside, pltpu.roll(cells, nx - 1, cells.ndim - 2))
    front = jnp.where(lane == 0, cells, pltpu.roll(cells, 1, cells.ndim - 1))
    back = jnp.where(lane == ny - 1, cells, pltpu.roll(cells, ny - 1, cells.ndim - 1))
    return (left + right) + (front + back) - 4.0 * cells


def film(fluid, inner, outer):
    inverse = 1.0 / (1.0 + AFFINITY * (outer[0] + outer[1]))
    flux = (fluid - outer) * inverse
    outer_next = outer + SHELL_MIX * (inner - outer) + PELLET_GAIN * flux
    return flux, inverse, outer_next


def film_back(flux_cot, flux, inverse):
    direct = flux_cot * inverse
    shared = AFFINITY * (direct[0] * flux[0] + direct[1] * flux[1])
    return direct, -direct - shared


def pack_kernel(
    fluid_hbm, pellet_hbm, porosity_hbm, adjoint_hbm, row_out,
    fluid, pellet, porosity, fluid_edge, adjoint_edge, sems,
):
    experiments, comps, nz, nx, ny = fluid_hbm.shape
    first_x = lax.axis_index("xy") == 0
    tile = pl.multiple_of(jnp.where(first_x, nx - 8, 0), 8)
    edge = pl.ds(tile, 8)
    moves = [
        (fluid_hbm.at[:, :, :, edge], fluid_edge),
        (adjoint_hbm.at[:, :, :, edge], adjoint_edge),
        (fluid_hbm.at[:, :, nz - 3 : nz], fluid),
        (pellet_hbm.at[:, :, 2:4, nz - 2 : nz], pellet),
        (porosity_hbm.at[nz - 2 : nz], porosity),
    ]
    copies = [pltpu.make_async_copy(src, dst, sems.at[i]) for i, (src, dst) in enumerate(moves)]
    for copy in copies:
        copy.start()
    for copy in copies:
        copy.wait()
    for e in range(experiments):
        for k in range(comps):
            i = e * comps + k
            row_out[i] = jnp.where(first_x, fluid_edge[e, k, :, 7, :], fluid_edge[e, k, :, 0, :])
            row_out[4 + i] = jnp.where(first_x, adjoint_edge[e, k, :, 7, :], adjoint_edge[e, k, :, 0, :])
    inverse_porosity = 1.0 / porosity[...]
    advect = ADVECT * inverse_porosity
    exchange = FILM_RATE * (inverse_porosity - 1.0)
    weight_below = advect[1] + AXIAL_MIX
    rim = jnp.zeros((comps, 1, ny), jnp.float32)
    for e in range(experiments):
        nexts, shells = [], []
        for j in range(2):
            below, here, above = fluid[e, :, j], fluid[e, :, j + 1], fluid[e, :, min(j + 2, 2)]
            outer, inner = pellet[e, :, 1, j], pellet[e, :, 0, j]
            flux, _, outer_next = film(here, inner, outer)
            nexts.append(
                here
                + advect[j] * (below - here)
                + AXIAL_MIX * (below - 2.0 * here + above)
                + RADIAL_MIX * cross_mix(here, rim, first_x)
                - exchange[j] * flux
            )
            shells.append(outer_next)
        inverse = 1.0 / (1.0 + AFFINITY * (shells[1][0] + shells[1][1]))
        film_weight = exchange[1] * inverse
        weight_here = 1.0 - advect[1] - AXIAL_MIX - film_weight
        second = weight_here * nexts[1] + weight_below * nexts[0] + film_weight * shells[1]
        row_out[8, e : e + 1] = jnp.where(first_x, weight_here[nx - 1 : nx], weight_here[0:1])
        for k in range(comps):
            i = e * comps + k
            row_out[9, i : i + 1] = jnp.sum(nexts[1][k], axis=0, keepdims=True)
            row_out[9, 4 + i : 5 + i] = jnp.sum(second[k], axis=0, keepdims=True)
    row_out[8, 2:3] = jnp.where(first_x, weight_below[nx - 1 : nx], weight_below[0:1])
    row_out[8, 3:8] = jnp.zeros((5, ny), jnp.float32)


def plane_update(
    here, below, above, rim, inner, outer, cot, cot_below, cot_above, cot_rim, shells, advect, exchange, first_x
):
    flux, inverse, outer_next = film(here, inner, outer)
    nexts = (
        here
        + advect * (below - here)
        + AXIAL_MIX * (below - 2.0 * here + above)
        + RADIAL_MIX * cross_mix(here, rim, first_x)
        - exchange * flux
    )
    inverse_next = 1.0 / (1.0 + AFFINITY * (outer_next[0] + outer_next[1]))
    direct = (PELLET_GAIN * shells[3] - exchange * cot) * inverse_next
    late = (
        cot
        - (advect + 2.0 * AXIAL_MIX) * cot
        + AXIAL_MIX * cot_below
        + cot_above
        + RADIAL_MIX * cross_mix(cot, cot_rim, first_x)
        + direct
    )
    return flux, inverse, nexts, (nexts - outer_next) * inverse_next, direct, late


def pellet_update(shells, direct, flux_next, late, flux, inverse, exchange):
    core, second, third, outer = shells
    shared = AFFINITY * (direct[0] * flux_next[0] + direct[1] * flux_next[1])
    outer_late = KEEP_END * outer + SHELL_MIX * third - direct - shared
    third_late = KEEP_MID * third + SHELL_MIX * (second + outer)
    second_late = KEEP_MID * second + SHELL_MIX * (core + third)
    core_late = KEEP_END * core + SHELL_MIX * second
    through = (PELLET_GAIN * outer_late - exchange * late) * inverse
    shared = AFFINITY * (through[0] * flux[0] + through[1] * flux[1])
    return through, (
        KEEP_END * core_late + SHELL_MIX * second_late,
        KEEP_MID * second_late + SHELL_MIX * (core_late + third_late),
        KEEP_MID * third_late + SHELL_MIX * (second_late + outer_late),
        KEEP_END * outer_late + SHELL_MIX * third_late - through - shared,
    )


def pair_of(ref, first, z):
    return jnp.stack([ref[first, pl.ds(z, 1)], ref[first + 1, pl.ds(z, 1)]])


def outlet_kernel(cell_count, mine, theirs, sample, observed, seed_out, picked_out):
    nz = mine.shape[1]
    first_x = lax.axis_index("xy") == 0
    last_z = lax.axis_index("gz") == lax.axis_size("gz") - 1
    low = [jnp.where(first_x, mine[i], theirs[i]) for i in (0, 1, 2, 3, 8, 9)]
    high = [jnp.where(first_x, theirs[i], mine[i]) for i in (0, 1, 2, 3, 8, 9)]
    total = low[5] + high[5]
    scale = jnp.where(last_z, 1.0, 0.0)
    picked_out[...] = jnp.zeros_like(picked_out)
    for e in range(2):
        for k in range(2):
            i = e * 2 + k
            top = slice(nz - 1, nz)
            below = slice(nz - 2, nz - 1)
            first = low[i][top] + high[i][top]
            second = (low[4][e : e + 1] * high[i][top] + low[4][2:3] * high[i][below]) + (
                high[4][e : e + 1] * low[i][top] + high[4][2:3] * low[i][below]
            )
            chosen = jnp.where(
                sample[e] == 0,
                total[i : i + 1] + RADIAL_MIX * first,
                total[4 + i : 5 + i] + RADIAL_MIX * second,
            )
            mean = jnp.sum(chosen, axis=1, keepdims=True) / cell_count
            mean = jnp.broadcast_to(mean, chosen.shape)
            picked_out[i : i + 1] = mean * scale
            seed = (mean - observed[e, k]) * scale
            seed_out[i : i + 1] = jnp.where(sample[e] == 0, seed, 0.0)
            seed_out[4 + i : 5 + i] = jnp.where(sample[e] == 1, seed, 0.0)


def edge_kernel(
    fluid_hbm, pellet_hbm, porosity_hbm, adjoint_hbm, adjoint_pellet_hbm, theirs, seeds,
    first_out, second_out,
    fluid, pellet, porosity, adjoint, outer_cot, sems,
):
    experiments, comps, nz, nx, ny = fluid_hbm.shape
    first_x = lax.axis_index("xy") == 0
    even = lax.rem(lax.axis_index("gz"), 2) == 0

    def put(at_even, at_odd, where, value):
        @pl.when(even)
        def _():
            at_even[where] = value

        @pl.when(jnp.logical_not(even))
        def _():
            at_odd[where] = value

    ends = (slice(0, 2), slice(nz - 2, nz))
    moves = []
    for j, z in enumerate((0, nz - 1)):
        moves.append((fluid_hbm.at[:, :, ends[j]], fluid.at[j]))
        moves.append((adjoint_hbm.at[:, :, ends[j]], adjoint.at[j]))
        moves.append((porosity_hbm.at[ends[j]], porosity.at[j]))
        moves.append((pellet_hbm.at[:, :, 2:4, z], pellet.at[j]))
        moves.append((adjoint_pellet_hbm.at[:, :, 3, z], outer_cot.at[j]))
    copies = [pltpu.make_async_copy(src, dst, sems.at[i]) for i, (src, dst) in enumerate(moves)]
    for copy in copies:
        copy.start()

    for copy in copies:
        copy.wait()
    for j, z in enumerate((0, nz - 1)):
        inverse_porosity = 1.0 / porosity[j, j]
        advect = ADVECT * inverse_porosity
        exchange = FILM_RATE * (inverse_porosity - 1.0)
        if j == 0:
            advect_above = ADVECT / porosity[0, 1] + AXIAL_MIX
        for e in range(experiments):
            zero = jnp.zeros((comps, nx, ny), jnp.float32)
            here, cot = fluid[j, e, :, j], adjoint[j, e, :, j]
            shells = (None, None, None, outer_cot[j, e])
            _, _, nexts, _, _, late = plane_update(
                here,
                zero if j == 0 else fluid[1, e, :, 0],
                fluid[0, e, :, 1] if j == 0 else zero,
                pair_of(theirs, 2 * e, z),
                pellet[j, e, :, 0],
                pellet[j, e, :, 1],
                cot,
                zero if j == 0 else adjoint[1, e, :, 0],
                advect_above * adjoint[0, e, :, 1] if j == 0 else zero,
                pair_of(theirs, 4 + 2 * e, z),
                shells,
                advect,
                exchange,
                first_x,
            )
            pair = lambda n: slice(4 * n + 2 * e, 4 * n + 2 * e + 2)
            outs = (second_out, first_out) if j == 0 else (first_out, second_out)
            put(*outs, pair(0), here)
            put(*outs, pair(1), cot)
            put(*outs, pair(2), late)
            if j == 1:
                put(*outs, pair(3), nexts)
    for n in range(4 * experiments * comps - 4, 4 * experiments * comps):
        put(second_out, first_out, n, porosity[0, 0])


def inner_kernel(
    fluid, pellet, porosity, adjoint, adjoint_pellet, row_in, seeds,
    pellet_out, late_out, direct_out, grad_out, next_out,
    staged, lower_next, sems,
):
    experiments, comps, nz, nx, ny = fluid.shape
    first_x = lax.axis_index("xy") == 0
    lower_next[...] = jnp.zeros_like(lower_next)

    def send(z):
        return pltpu.make_async_copy(staged.at[z - 1], pellet_out.at[:, :, :, z], sems.at[z - 1])

    def plane(z, carry):
        inverse_porosity = 1.0 / porosity[z]
        advect = ADVECT * inverse_porosity
        advect_above = ADVECT / porosity[z + 1] + AXIAL_MIX
        exchange = FILM_RATE * (inverse_porosity - 1.0)
        under_top = jnp.where(z == nz - 2, 1.0, 0.0)
        grad = jnp.zeros((nx, ny), jnp.float32)
        for e in range(experiments):
            here, below, cot = fluid[e, :, z], fluid[e, :, z - 1], adjoint[e, :, z]
            shells = tuple(adjoint_pellet[e, :, shell, z] for shell in range(4))
            flux, inverse, nexts, flux_next, direct, late = plane_update(
                here,
                below,
                fluid[e, :, z + 1],
                pair_of(row_in, 2 * e, z),
                pellet[e, :, 2, z],
                pellet[e, :, 3, z],
                cot,
                adjoint[e, :, z - 1],
                advect_above * (adjoint[e, :, z + 1] + under_top * pair_of_rows(seeds, 4 + 2 * e)),
                pair_of(row_in, 4 + 2 * e, z),
                shells,
                advect,
                exchange,
                first_x,
            )
            through, shells = pellet_update(shells, direct, flux_next, late, flux, inverse, exchange)
            for shell in range(4):
                staged[z - 1, e, :, shell] = shells[shell]
            late_out[e, :, z] = late
            direct_out[e, :, z] = through
            term = cot * (FILM_RATE * flux_next + ADVECT * (nexts - lower_next[e])) + late * (
                FILM_RATE * flux + ADVECT * (here - below)
            )
            grad = grad + (term[0] + term[1])
            lower_next[e] = nexts
        send(z).start()
        grad_out[z] = grad * (inverse_porosity * inverse_porosity)
        return carry

    lax.fori_loop(1, nz - 1, plane, 0)
    next_out[...] = lower_next[...]
    for z in range(1, nz - 1):
        send(z).wait()


def pair_of_rows(ref, first):
    return jnp.stack([ref[first : first + 1], ref[first + 1 : first + 2]])


def outer_kernel(
    fluid, pellet, porosity, adjoint, adjoint_pellet, first_in, second_in, row_in, seeds, level,
    inner_late, inner_grad, inner_next, picked, spread_a, spread_b, spread_c, inner_pellet,
    pellet_out, late_out, direct_out, grad_out, halo_out, row_out, picked_out,
    staged, sems,
):
    experiments, comps, nz, nx, ny = fluid.shape
    first_x = lax.axis_index("xy") == 0
    first_z = lax.axis_index("gz") == 0
    last_z = lax.axis_index("gz") == lax.axis_size("gz") - 1
    even = lax.rem(lax.axis_index("gz"), 2) == 0

    def up_in(where):
        return jnp.where(even, second_in[where], first_in[where])

    def down_in(where):
        return jnp.where(even, first_in[where], second_in[where])

    picked_out[...] = picked[...] + (spread_a[...] + spread_b[...] + spread_c[...])
    row_out[experiments * comps] = picked_out[...]
    grad_out[1 : nz - 1] = inner_grad[1 : nz - 1]
    sends = []
    for j, z in enumerate((0, nz - 1)):
        inverse_porosity = 1.0 / porosity[z]
        advect = ADVECT * inverse_porosity
        exchange = FILM_RATE * (inverse_porosity - 1.0)
        if j == 0:
            advect_above = ADVECT / porosity[1] + AXIAL_MIX
        else:
            advect_above = ADVECT / jnp.where(last_z, 1.0, down_in(12)) + AXIAL_MIX
        grad = jnp.zeros((nx, ny), jnp.float32)
        grad_next = jnp.zeros((nx, ny), jnp.float32)
        for e in range(experiments):
            pair = lambda n: slice(4 * n + 2 * e, 4 * n + 2 * e + 2)
            here, cot = fluid[e, :, z], adjoint[e, :, z]
            cot_rim = pair_of(row_in, 4 + 2 * e, z)
            if j == 0:
                inlets = []
                for k in range(comps):
                    value = level[e].astype(jnp.float32)
                    value = (1.0 + value) / 4.0 if k == 0 else (4.0 - value) / 4.0
                    inlets.append(jnp.full((nx, ny), value))
                inlet = jnp.stack(inlets)
                below = jnp.where(first_z, inlet, up_in(pair(0)))
                above = fluid[e, :, 1]
                cot_below = up_in(pair(1))
                cot_above = advect_above * adjoint[e, :, 1]
                lower_next = jnp.where(first_z, inlet, up_in(pair(3)) + AXIAL_MIX * here)
                halo_out[pair(0)] = jnp.where(
                    first_z, 0.0, up_in(pair(2)) + (advect + AXIAL_MIX) * cot
                )
            else:
                seed = pair_of_rows(seeds, 4 + 2 * e)
                cot = cot + seed
                cot_rim = cot_rim + seed
                below = fluid[e, :, nz - 2]
                above = jnp.where(last_z, here, down_in(pair(0)))
                cot_below = adjoint[e, :, nz - 2]
                cot_above = jnp.where(last_z, AXIAL_MIX * cot, advect_above * down_in(pair(1)))
                lower_next = inner_next[e]
            shells = tuple(adjoint_pellet[e, :, shell, z] for shell in range(4))
            flux, inverse, nexts, flux_next, direct, late = plane_update(
                here, below, above, pair_of(row_in, 2 * e, z), pellet[e, :, 2, z], pellet[e, :, 3, z],
                cot, cot_below, cot_above, cot_rim, shells, advect, exchange, first_x,
            )
            if j == 1:
                late = late + pair_of_rows(seeds, 2 * e)
                halo_out[pair(1)] = jnp.where(
                    last_z, AXIAL_MIX * late, advect_above * (down_in(pair(2)) + AXIAL_MIX * cot)
                )
            through, shells = pellet_update(shells, direct, flux_next, late, flux, inverse, exchange)
            for shell in range(4):
                staged[j, e, :, shell] = shells[shell]
            late_out[j, e] = late
            direct_out[j, e] = through
            term = cot * (FILM_RATE * flux_next + ADVECT * (nexts - lower_next)) + late * (
                FILM_RATE * flux + ADVECT * (here - below)
            )
            grad = grad + (term[0] + term[1])
            if j == 0:
                follow = adjoint[e, :, 1] * nexts
                grad_next = grad_next + (follow[0] + follow[1])
            for k in range(comps):
                i = 2 * e + k
                if j == 0:
                    row_out[i, 1 : nz - 1] = jnp.where(
                        first_x, inner_late[e, k, 1 : nz - 1, nx - 1, :], inner_late[e, k, 1 : nz - 1, 0, :]
                    )
                row_out[i, z : z + 1] = jnp.where(first_x, late[k, nx - 1 : nx], late[k, 0:1])
        sends.append(pltpu.make_async_copy(staged.at[j], pellet_out.at[:, :, :, z], sems.at[j]))
        sends[j].start()
        grad_out[z] = grad * (inverse_porosity * inverse_porosity)
        if j == 0:
            inverse_porosity = 1.0 / porosity[1]
            grad_out[1] = grad_out[1] - ADVECT * (inverse_porosity * inverse_porosity) * grad_next
    for send in sends:
        send.wait()


def final_kernel(
    porosity, inner_late, inner_direct, edge_late, edge_direct, halo, row_in, fluid_out, done_out
):
    experiments, comps, nz, nx, ny = inner_late.shape
    first_x = lax.axis_index("xy") == 0
    done_out[...] = jnp.zeros_like(done_out)
    for z in range(nz):
        advect = ADVECT / porosity[z]
        if z < nz - 1:
            advect_above = ADVECT / porosity[z + 1] + AXIAL_MIX
        for e in range(experiments):
            def plane_at(w):
                if w in (0, nz - 1):
                    return edge_late[0 if w == 0 else 1, e]
                return inner_late[e, :, w]

            here = plane_at(z)
            lower = plane_at(z - 1) if z > 0 else halo[2 * e : 2 * e + 2]
            upper = advect_above * plane_at(z + 1) if z < nz - 1 else halo[4 + 2 * e : 6 + 2 * e]
            if z in (0, nz - 1):
                direct = edge_direct[0 if z == 0 else 1, e]
            else:
                direct = inner_direct[e, :, z]
            fluid_out[e, :, z] = (
                here
                - (advect + 2.0 * AXIAL_MIX) * here
                + AXIAL_MIX * lower
                + upper
                + RADIAL_MIX * cross_mix(here, pair_of(row_in, 2 * e, z), first_x)
                + direct
            )


def gather_kernel(grad, grad_in, picked, spread_a, spread_b, spread_c, done, grad_out, breakthrough_out):
    grad_out[...] = grad[...] + grad_in[...]
    total = (picked[0:4] + (spread_a[0:4] + spread_b[0:4] + spread_c[0:4]))[:, 0:2]
    shape = breakthrough_out.shape
    row, column = row_index(breakthrough_out), lane_index(breakthrough_out)
    value = jnp.zeros(shape, jnp.float32)
    for e in range(shape[0]):
        for k in range(shape[1]):
            i = e * shape[1] + k
            here = (row == e) & (column == k)
            value = jnp.where(here, jnp.broadcast_to(total[i : i + 1], shape), value)
    breakthrough_out[...] = value


def spread_levels(gz):
    reached = {2 * gz - 2, 2 * gz - 1}
    for n, level in enumerate(SPREAD):
        if n == 2:
            reached |= {i ^ 1 for i in reached}
        senders = set(reached)
        for pairs in level:
            targets = {i for _, i in pairs}
            assert {i for i, _ in pairs} <= senders and not targets & reached
            reached |= targets
    assert reached == set(range(2 * gz))
    return SPREAD


def shards(
    fluid_start,
    pellet_start,
    porosity,
    feed_level,
    sample_step,
    observed_outlet,
    adjoint_fluid_end,
    adjoint_pellet_end,
):
    f32 = jnp.float32
    experiments, comps, nz, nx, ny = fluid_start.shape
    planes = experiments * comps
    gz = lax.axis_size("gz")
    cell_count = nx * lax.axis_size("xy") * ny
    vmem = pl.BlockSpec(memory_space=pltpu.VMEM)
    smem = pl.BlockSpec(memory_space=pltpu.SMEM)
    hbm = pl.BlockSpec(memory_space=pltpu.HBM)
    params = pltpu.CompilerParams(vmem_limit_bytes=5 * 2**20)
    dma = pltpu.SemaphoreType.DMA

    def shape(*dims):
        return jax.ShapeDtypeStruct(dims, f32)

    trades = ([], [])
    for i in range(gz - 1):
        for x in range(2):
            low, high = 2 * i + x, 2 * i + 2 + x
            trades[i % 2].extend([(low, high), (high, low)])
    swap = [(0, 1), (1, 0)]
    levels = spread_levels(gz)

    def spread(picked, level):
        arrivals = [lax.ppermute(picked, ("gz", "xy"), pairs) for pairs in levels[level]]
        return arrivals + [jnp.zeros_like(picked)] * (3 - len(arrivals))

    in_hbm = [
        pltpu.with_memory_space_constraint(x, pltpu.HBM)
        for x in (fluid_start, pellet_start, porosity, adjoint_fluid_end, adjoint_pellet_end)
    ]
    rows = pl.pallas_call(
        pack_kernel,
        out_shape=shape(10, nz, ny),
        in_specs=[hbm] * 4,
        out_specs=vmem,
        scratch_shapes=[
            pltpu.VMEM((experiments, comps, 3, nx, ny), f32),
            pltpu.VMEM((experiments, comps, 2, 2, nx, ny), f32),
            pltpu.VMEM((2, nx, ny), f32),
            pltpu.VMEM((experiments, comps, nz, 8, ny), f32),
            pltpu.VMEM((experiments, comps, nz, 8, ny), f32),
            dma((5,)),
        ],
        compiler_params=params,
        name="pack",
    )(*in_hbm[:4])
    rows_in = lax.ppermute(rows, "xy", swap)

    seeds, picked = pl.pallas_call(
        partial(outlet_kernel, cell_count),
        out_shape=(shape(8, ny), shape(8, ny)),
        in_specs=[vmem, vmem, smem, smem],
        out_specs=[vmem] * 2,
        compiler_params=params,
        name="outlet",
    )(rows, rows_in, sample_step, observed_outlet)
    picked = picked + sum(spread(picked, 0))

    first, second = pl.pallas_call(
        edge_kernel,
        out_shape=(shape(4 * planes, nx, ny), shape(4 * planes, nx, ny)),
        in_specs=[hbm] * 5 + [vmem] * 2,
        out_specs=[vmem] * 2,
        scratch_shapes=[
            pltpu.VMEM((2, experiments, comps, 2, nx, ny), f32),
            pltpu.VMEM((2, experiments, comps, 2, nx, ny), f32),
            pltpu.VMEM((2, 2, nx, ny), f32),
            pltpu.VMEM((2, experiments, comps, 2, nx, ny), f32),
            pltpu.VMEM((2, experiments, comps, nx, ny), f32),
            dma((10,)),
        ],
        compiler_params=params,
        name="edge",
    )(*in_hbm, rows_in, seeds)
    first_in = lax.ppermute(first, ("gz", "xy"), trades[0])
    second_in = lax.ppermute(second, ("gz", "xy"), trades[1])

    adjoint_pellet, late, direct, grad, next_fluid = pl.pallas_call(
        inner_kernel,
        out_shape=(
            shape(*pellet_start.shape),
            shape(*fluid_start.shape),
            shape(*fluid_start.shape),
            shape(nz, nx, ny),
            shape(experiments, comps, nx, ny),
        ),
        in_specs=[vmem] * 7,
        out_specs=[hbm] + [vmem] * 4,
        scratch_shapes=[
            pltpu.VMEM((nz - 2, experiments, comps, 4, nx, ny), f32),
            pltpu.VMEM((experiments, comps, nx, ny), f32),
            dma((nz - 2,)),
        ],
        compiler_params=params,
        cost_estimate=pl.CostEstimate(flops=10**10, bytes_accessed=10**9, transcendentals=0),
        name="inner",
    )(
        fluid_start, pellet_start, porosity, adjoint_fluid_end, adjoint_pellet_end,
        rows_in, seeds,
    )

    adjoint_pellet, edge_late, edge_direct, grad, halo, rows, picked = pl.pallas_call(
        outer_kernel,
        out_shape=(
            shape(*pellet_start.shape),
            shape(2, experiments, comps, nx, ny),
            shape(2, experiments, comps, nx, ny),
            shape(nz, nx, ny),
            shape(2 * planes, nx, ny),
            shape(planes + 1, nz, ny),
            shape(8, ny),
        ),
        in_specs=[vmem] * 9 + [smem] + [vmem] * 7 + [hbm],
        out_specs=[hbm] + [vmem] * 6,
        scratch_shapes=[
            pltpu.VMEM((2, experiments, comps, 4, nx, ny), f32),
            dma((2,)),
        ],
        input_output_aliases={17: 0},
        compiler_params=params,
        name="outer",
    )(
        fluid_start, pellet_start, porosity, adjoint_fluid_end, adjoint_pellet_end,
        first_in, second_in, rows_in, seeds, feed_level,
        late, grad, next_fluid, picked, *spread(picked, 1), adjoint_pellet,
    )
    grad_in = lax.ppermute(grad, "exp", swap)
    rows_in = lax.ppermute(rows, "xy", swap)
    last_z = lax.axis_index("gz") == gz - 1
    picked = picked + jnp.where(last_z, 0.0, rows_in[planes])

    adjoint_fluid, done = pl.pallas_call(
        final_kernel,
        out_shape=(shape(*fluid_start.shape), shape(8, ny)),
        in_specs=[vmem] * 7,
        out_specs=[vmem] * 2,
        compiler_params=params,
        name="final",
    )(porosity, late, direct, edge_late, edge_direct, halo, rows_in)
    gradient, breakthrough = pl.pallas_call(
        gather_kernel,
        out_shape=(shape(nz, nx, ny), shape(experiments, comps)),
        in_specs=[vmem] * 7,
        out_specs=[vmem] * 2,
        compiler_params=params,
        name="gather",
    )(grad, grad_in, picked, *spread(picked, 2), done)
    return (breakthrough, adjoint_fluid, adjoint_pellet, gradient)


def solution(mesh):
    placed = (
        P("exp", None, "gz", "xy", None),
        P("exp", None, None, "gz", "xy", None),
        P("gz", "xy", None),
        P("exp"),
        P("exp"),
        P("exp", None),
        P("exp", None, "gz", "xy", None),
        P("exp", None, None, "gz", "xy", None),
    )
    return jax.shard_map(
        shards,
        mesh=mesh,
        in_specs=placed,
        out_specs=(
            P("exp", None),
            P("exp", None, "gz", "xy", None),
            P("exp", None, None, "gz", "xy", None),
            P("gz", "xy", None),
        ),
        check_vma=False,
    )
```

```python
from functools import partial

import jax
import jax.numpy as jnp
from jax import lax
from jax.experimental import pallas as pl
from jax.experimental.pallas import tpu as pltpu
from jax.sharding import PartitionSpec as P

STEPS = 2

ADVECT = 0.12
AXIAL_MIX = 0.08
RADIAL_MIX = 0.05
FILM_RATE = 0.05
SHELL_MIX = 0.2
PELLET_GAIN = 0.03
AFFINITY = 0.5

SPREAD = ((((126, 20), (127, 53)), ((126, 84), (127, 117))), (((20, 18), (53, 51), (84, 82), (117, 101), (126, 68), (127, 5)), ((20, 24), (53, 57), (84, 88), (117, 115), (126, 106), (127, 37)), ((20, 10), (53, 43), (84, 74), (117, 121), (126, 108), (127, 125))), (((18, 0), (19, 1), (20, 16), (21, 17), (4, 2), (5, 3), (24, 22), (25, 23), (10, 6), (11, 7), (50, 32), (51, 33), (52, 48), (53, 49), (36, 34), (37, 35), (56, 54), (57, 55), (42, 38), (43, 39), (82, 64), (83, 65), (84, 80), (85, 81), (68, 66), (69, 67), (88, 86), (89, 87), (74, 70), (75, 71), (114, 96), (115, 97), (116, 112), (117, 113), (100, 98), (101, 99), (120, 118), (121, 119), (106, 102), (107, 103), (108, 110), (109, 111), (124, 122), (125, 123), (126, 104), (127, 105)), ((20, 28), (21, 29), (24, 30), (25, 31), (10, 12), (11, 13), (4, 8), (5, 9), (52, 60), (53, 61), (56, 62), (57, 63), (42, 44), (43, 45), (36, 40), (37, 41), (84, 92), (85, 93), (88, 94), (89, 95), (74, 76), (75, 77), (68, 72), (69, 73), (18, 14), (19, 15), (126, 78), (127, 79), (50, 46), (51, 47), (120, 58), (121, 59), (124, 90), (125, 91), (106, 26), (107, 27))))

KEEP_END = 1.0 - SHELL_MIX
KEEP_MID = 1.0 - 2.0 * SHELL_MIX


def row_index(cells):
    return lax.broadcasted_iota(jnp.int32, cells.shape, cells.ndim - 2)


def lane_index(cells):
    return lax.broadcasted_iota(jnp.int32, cells.shape, cells.ndim - 1)


def cross_mix(cells, rim, first_x):
    nx, ny = cells.shape[-2:]
    row, lane = row_index(cells), lane_index(cells)
    wall = jnp.where(first_x, 0, nx - 1)
    outside = jnp.where(row == wall, cells, jnp.broadcast_to(rim, cells.shape))
    left = jnp.where(row == 0, outside, pltpu.roll(cells, 1, cells.ndim - 2))
    right = jnp.where(row == nx - 1, outside, pltpu.roll(cells, nx - 1, cells.ndim - 2))
    front = jnp.where(lane == 0, cells, pltpu.roll(cells, 1, cells.ndim - 1))
    back = jnp.where(lane == ny - 1, cells, pltpu.roll(cells, ny - 1, cells.ndim - 1))
    return (left + right) + (front + back) - 4.0 * cells


def film(fluid, inner, outer):
    inverse = 1.0 / (1.0 + AFFINITY * (outer[0] + outer[1]))
    flux = (fluid - outer) * inverse
    outer_next = outer + SHELL_MIX * (inner - outer) + PELLET_GAIN * flux
    return flux, inverse, outer_next


def film_back(flux_cot, flux, inverse):
    direct = flux_cot * inverse
    shared = AFFINITY * (direct[0] * flux[0] + direct[1] * flux[1])
    return direct, -direct - shared


def pack_kernel(
    fluid_hbm, pellet_hbm, porosity_hbm, adjoint_hbm, row_out,
    fluid, pellet, porosity, fluid_edge, adjoint_edge, sems,
):
    experiments, comps, nz, nx, ny = fluid_hbm.shape
    first_x = lax.axis_index("xy") == 0
    tile = pl.multiple_of(jnp.where(first_x, nx - 8, 0), 8)
    edge = pl.ds(tile, 8)
    moves = [
        (fluid_hbm.at[:, :, :, edge], fluid_edge),
        (adjoint_hbm.at[:, :, :, edge], adjoint_edge),
        (fluid_hbm.at[:, :, nz - 3 : nz], fluid),
        (pellet_hbm.at[:, :, 2:4, nz - 2 : nz], pellet),
        (porosity_hbm.at[nz - 2 : nz], porosity),
    ]
    copies = [pltpu.make_async_copy(src, dst, sems.at[i]) for i, (src, dst) in enumerate(moves)]
    for copy in copies:
        copy.start()
    for copy in copies:
        copy.wait()
    for e in range(experiments):
        for k in range(comps):
            i = e * comps + k
            row_out[i] = jnp.where(first_x, fluid_edge[e, k, :, 7, :], fluid_edge[e, k, :, 0, :])
            row_out[4 + i] = jnp.where(first_x, adjoint_edge[e, k, :, 7, :], adjoint_edge[e, k, :, 0, :])
    last_z = lax.axis_index("gz") == lax.axis_size("gz") - 1
    row_out[8:10] = jnp.zeros((2,) + row_out.shape[1:], jnp.float32)

    @pl.when(last_z)
    def _():
        inverse_porosity = 1.0 / porosity[...]
        advect = ADVECT * inverse_porosity
        exchange = FILM_RATE * (inverse_porosity - 1.0)
        weight_below = advect[1] + AXIAL_MIX
        rim = jnp.zeros((comps, 1, ny), jnp.float32)
        for e in range(experiments):
            nexts, shells = [], []
            for j in range(2):
                below, here, above = fluid[e, :, j], fluid[e, :, j + 1], fluid[e, :, min(j + 2, 2)]
                outer, inner = pellet[e, :, 1, j], pellet[e, :, 0, j]
                flux, _, outer_next = film(here, inner, outer)
                nexts.append(
                    here
                    + advect[j] * (below - here)
                    + AXIAL_MIX * (below - 2.0 * here + above)
                    + RADIAL_MIX * cross_mix(here, rim, first_x)
                    - exchange[j] * flux
                )
                shells.append(outer_next)
            inverse = 1.0 / (1.0 + AFFINITY * (shells[1][0] + shells[1][1]))
            film_weight = exchange[1] * inverse
            weight_here = 1.0 - advect[1] - AXIAL_MIX - film_weight
            second = weight_here * nexts[1] + weight_below * nexts[0] + film_weight * shells[1]
            row_out[8, e : e + 1] = jnp.where(first_x, weight_here[nx - 1 : nx], weight_here[0:1])
            for k in range(comps):
                i = e * comps + k
                row_out[9, i : i + 1] = jnp.sum(nexts[1][k], axis=0, keepdims=True)
                row_out[9, 4 + i : 5 + i] = jnp.sum(second[k], axis=0, keepdims=True)
        row_out[8, 2:3] = jnp.where(first_x, weight_below[nx - 1 : nx], weight_below[0:1])
        row_out[8, 3:8] = jnp.zeros((5, ny), jnp.float32)


def plane_update(
    here, below, above, rim, inner, outer, cot, cot_below, cot_above, cot_rim, shells, advect, exchange, first_x
):
    flux, inverse, outer_next = film(here, inner, outer)
    nexts = (
        here
        + advect * (below - here)
        + AXIAL_MIX * (below - 2.0 * here + above)
        + RADIAL_MIX * cross_mix(here, rim, first_x)
        - exchange * flux
    )
    inverse_next = 1.0 / (1.0 + AFFINITY * (outer_next[0] + outer_next[1]))
    direct = (PELLET_GAIN * shells[3] - exchange * cot) * inverse_next
    late = (
        cot
        - (advect + 2.0 * AXIAL_MIX) * cot
        + AXIAL_MIX * cot_below
        + cot_above
        + RADIAL_MIX * cross_mix(cot, cot_rim, first_x)
        + direct
    )
    return flux, inverse, nexts, (nexts - outer_next) * inverse_next, direct, late


def pellet_update(shells, direct, flux_next, late, flux, inverse, exchange):
    core, second, third, outer = shells
    shared = AFFINITY * (direct[0] * flux_next[0] + direct[1] * flux_next[1])
    outer_late = KEEP_END * outer + SHELL_MIX * third - direct - shared
    third_late = KEEP_MID * third + SHELL_MIX * (second + outer)
    second_late = KEEP_MID * second + SHELL_MIX * (core + third)
    core_late = KEEP_END * core + SHELL_MIX * second
    through = (PELLET_GAIN * outer_late - exchange * late) * inverse
    shared = AFFINITY * (through[0] * flux[0] + through[1] * flux[1])
    return through, (
        KEEP_END * core_late + SHELL_MIX * second_late,
        KEEP_MID * second_late + SHELL_MIX * (core_late + third_late),
        KEEP_MID * third_late + SHELL_MIX * (second_late + outer_late),
        KEEP_END * outer_late + SHELL_MIX * third_late - through - shared,
    )


def pair_of(ref, first, z):
    return jnp.stack([ref[first, pl.ds(z, 1)], ref[first + 1, pl.ds(z, 1)]])


def outlet_kernel(cell_count, mine, theirs, sample, observed, seed_out, picked_out):
    nz = mine.shape[1]
    first_x = lax.axis_index("xy") == 0
    last_z = lax.axis_index("gz") == lax.axis_size("gz") - 1
    low = [jnp.where(first_x, mine[i], theirs[i]) for i in (0, 1, 2, 3, 8, 9)]
    high = [jnp.where(first_x, theirs[i], mine[i]) for i in (0, 1, 2, 3, 8, 9)]
    total = low[5] + high[5]
    scale = jnp.where(last_z, 1.0, 0.0)
    picked_out[...] = jnp.zeros_like(picked_out)
    for e in range(2):
        for k in range(2):
            i = e * 2 + k
            top = slice(nz - 1, nz)
            below = slice(nz - 2, nz - 1)
            first = low[i][top] + high[i][top]
            second = (low[4][e : e + 1] * high[i][top] + low[4][2:3] * high[i][below]) + (
                high[4][e : e + 1] * low[i][top] + high[4][2:3] * low[i][below]
            )
            chosen = jnp.where(
                sample[e] == 0,
                total[i : i + 1] + RADIAL_MIX * first,
                total[4 + i : 5 + i] + RADIAL_MIX * second,
            )
            mean = jnp.sum(chosen, axis=1, keepdims=True) / cell_count
            mean = jnp.broadcast_to(mean, chosen.shape)
            picked_out[i : i + 1] = mean * scale
            seed = (mean - observed[e, k]) * scale
            seed_out[i : i + 1] = jnp.where(sample[e] == 0, seed, 0.0)
            seed_out[4 + i : 5 + i] = jnp.where(sample[e] == 1, seed, 0.0)


def edge_kernel(
    fluid_hbm, pellet_hbm, porosity_hbm, adjoint_hbm, adjoint_pellet_hbm, theirs, seeds,
    first_out, second_out,
    fluid, pellet, porosity, adjoint, outer_cot, sems,
):
    experiments, comps, nz, nx, ny = fluid_hbm.shape
    first_x = lax.axis_index("xy") == 0
    even = lax.rem(lax.axis_index("gz"), 2) == 0

    def put(at_even, at_odd, where, value):
        @pl.when(even)
        def _():
            at_even[where] = value

        @pl.when(jnp.logical_not(even))
        def _():
            at_odd[where] = value

    ends = (slice(0, 2), slice(nz - 2, nz))
    moves = []
    for j, z in enumerate((0, nz - 1)):
        moves.append((fluid_hbm.at[:, :, ends[j]], fluid.at[j]))
        moves.append((adjoint_hbm.at[:, :, ends[j]], adjoint.at[j]))
        moves.append((porosity_hbm.at[ends[j]], porosity.at[j]))
        moves.append((pellet_hbm.at[:, :, 2:4, z], pellet.at[j]))
        moves.append((adjoint_pellet_hbm.at[:, :, 3, z], outer_cot.at[j]))
    copies = [pltpu.make_async_copy(src, dst, sems.at[i]) for i, (src, dst) in enumerate(moves)]
    for copy in copies:
        copy.start()

    for copy in copies:
        copy.wait()
    for j, z in enumerate((0, nz - 1)):
        inverse_porosity = 1.0 / porosity[j, j]
        advect = ADVECT * inverse_porosity
        exchange = FILM_RATE * (inverse_porosity - 1.0)
        if j == 0:
            advect_above = ADVECT / porosity[0, 1] + AXIAL_MIX
        for e in range(experiments):
            zero = jnp.zeros((comps, nx, ny), jnp.float32)
            here, cot = fluid[j, e, :, j], adjoint[j, e, :, j]
            shells = (None, None, None, outer_cot[j, e])
            _, _, nexts, _, _, late = plane_update(
                here,
                zero if j == 0 else fluid[1, e, :, 0],
                fluid[0, e, :, 1] if j == 0 else zero,
                pair_of(theirs, 2 * e, z),
                pellet[j, e, :, 0],
                pellet[j, e, :, 1],
                cot,
                zero if j == 0 else adjoint[1, e, :, 0],
                advect_above * adjoint[0, e, :, 1] if j == 0 else zero,
                pair_of(theirs, 4 + 2 * e, z),
                shells,
                advect,
                exchange,
                first_x,
            )
            pair = lambda n: slice(4 * n + 2 * e, 4 * n + 2 * e + 2)
            outs = (second_out, first_out) if j == 0 else (first_out, second_out)
            put(*outs, pair(0), here)
            put(*outs, pair(1), cot)
            put(*outs, pair(2), late)
            if j == 1:
                put(*outs, pair(3), nexts)
    for n in range(4 * experiments * comps - 4, 4 * experiments * comps):
        put(second_out, first_out, n, porosity[0, 0])


def inner_kernel(
    fluid, pellet, porosity, adjoint, adjoint_pellet, row_in, seeds,
    pellet_out, late_out, direct_out, grad_out, next_out,
    staged, lower_next, sems,
):
    experiments, comps, nz, nx, ny = fluid.shape
    first_x = lax.axis_index("xy") == 0
    lower_next[...] = jnp.zeros_like(lower_next)

    def send(z):
        return pltpu.make_async_copy(staged.at[z - 1], pellet_out.at[:, :, :, z], sems.at[z - 1])

    def plane(z, carry):
        inverse_porosity = 1.0 / porosity[z]
        advect = ADVECT * inverse_porosity
        advect_above = ADVECT / porosity[z + 1] + AXIAL_MIX
        exchange = FILM_RATE * (inverse_porosity - 1.0)
        under_top = jnp.where(z == nz - 2, 1.0, 0.0)
        grad = jnp.zeros((nx, ny), jnp.float32)
        for e in range(experiments):
            here, below, cot = fluid[e, :, z], fluid[e, :, z - 1], adjoint[e, :, z]
            shells = tuple(adjoint_pellet[e, :, shell, z] for shell in range(4))
            flux, inverse, nexts, flux_next, direct, late = plane_update(
                here,
                below,
                fluid[e, :, z + 1],
                pair_of(row_in, 2 * e, z),
                pellet[e, :, 2, z],
                pellet[e, :, 3, z],
                cot,
                adjoint[e, :, z - 1],
                advect_above * (adjoint[e, :, z + 1] + under_top * pair_of_rows(seeds, 4 + 2 * e)),
                pair_of(row_in, 4 + 2 * e, z),
                shells,
                advect,
                exchange,
                first_x,
            )
            through, shells = pellet_update(shells, direct, flux_next, late, flux, inverse, exchange)
            for shell in range(4):
                staged[z - 1, e, :, shell] = shells[shell]
            late_out[e, :, z] = late
            direct_out[e, :, z] = through
            term = cot * (FILM_RATE * flux_next + ADVECT * (nexts - lower_next[e])) + late * (
                FILM_RATE * flux + ADVECT * (here - below)
            )
            grad = grad + (term[0] + term[1])
            lower_next[e] = nexts
        send(z).start()
        grad_out[z] = grad * (inverse_porosity * inverse_porosity)
        return carry

    lax.fori_loop(1, nz - 1, plane, 0)
    next_out[...] = lower_next[...]
    for z in range(1, nz - 1):
        send(z).wait()


def pair_of_rows(ref, first):
    return jnp.stack([ref[first : first + 1], ref[first + 1 : first + 2]])


def outer_kernel(
    fluid, pellet, porosity, adjoint, adjoint_pellet, first_in, second_in, row_in, seeds, level,
    inner_late, inner_grad, inner_next, picked, spread_a, spread_b, spread_c, inner_pellet,
    pellet_out, late_out, direct_out, grad_out, halo_out, row_out, picked_out,
    staged, sems,
):
    experiments, comps, nz, nx, ny = fluid.shape
    first_x = lax.axis_index("xy") == 0
    first_z = lax.axis_index("gz") == 0
    last_z = lax.axis_index("gz") == lax.axis_size("gz") - 1
    even = lax.rem(lax.axis_index("gz"), 2) == 0

    def up_in(where):
        return jnp.where(even, second_in[where], first_in[where])

    def down_in(where):
        return jnp.where(even, first_in[where], second_in[where])

    picked_out[...] = picked[...] + (spread_a[...] + spread_b[...] + spread_c[...])
    row_out[experiments * comps] = picked_out[...]
    grad_out[1 : nz - 1] = inner_grad[1 : nz - 1]
    sends = []
    for j, z in enumerate((0, nz - 1)):
        inverse_porosity = 1.0 / porosity[z]
        advect = ADVECT * inverse_porosity
        exchange = FILM_RATE * (inverse_porosity - 1.0)
        if j == 0:
            advect_above = ADVECT / porosity[1] + AXIAL_MIX
        else:
            advect_above = ADVECT / jnp.where(last_z, 1.0, down_in(12)) + AXIAL_MIX
        grad = jnp.zeros((nx, ny), jnp.float32)
        grad_next = jnp.zeros((nx, ny), jnp.float32)
        for e in range(experiments):
            pair = lambda n: slice(4 * n + 2 * e, 4 * n + 2 * e + 2)
            here, cot = fluid[e, :, z], adjoint[e, :, z]
            cot_rim = pair_of(row_in, 4 + 2 * e, z)
            if j == 0:
                inlets = []
                for k in range(comps):
                    value = level[e].astype(jnp.float32)
                    value = (1.0 + value) / 4.0 if k == 0 else (4.0 - value) / 4.0
                    inlets.append(jnp.full((nx, ny), value))
                inlet = jnp.stack(inlets)
                below = jnp.where(first_z, inlet, up_in(pair(0)))
                above = fluid[e, :, 1]
                cot_below = up_in(pair(1))
                cot_above = advect_above * adjoint[e, :, 1]
                lower_next = jnp.where(first_z, inlet, up_in(pair(3)) + AXIAL_MIX * here)
                halo_out[pair(0)] = jnp.where(
                    first_z, 0.0, up_in(pair(2)) + (advect + AXIAL_MIX) * cot
                )
            else:
                seed = pair_of_rows(seeds, 4 + 2 * e)
                cot = cot + seed
                cot_rim = cot_rim + seed
                below = fluid[e, :, nz - 2]
                above = jnp.where(last_z, here, down_in(pair(0)))
                cot_below = adjoint[e, :, nz - 2]
                cot_above = jnp.where(last_z, AXIAL_MIX * cot, advect_above * down_in(pair(1)))
                lower_next = inner_next[e]
            shells = tuple(adjoint_pellet[e, :, shell, z] for shell in range(4))
            flux, inverse, nexts, flux_next, direct, late = plane_update(
                here, below, above, pair_of(row_in, 2 * e, z), pellet[e, :, 2, z], pellet[e, :, 3, z],
                cot, cot_below, cot_above, cot_rim, shells, advect, exchange, first_x,
            )
            if j == 1:
                late = late + pair_of_rows(seeds, 2 * e)
                halo_out[pair(1)] = jnp.where(
                    last_z, AXIAL_MIX * late, advect_above * (down_in(pair(2)) + AXIAL_MIX * cot)
                )
            through, shells = pellet_update(shells, direct, flux_next, late, flux, inverse, exchange)
            for shell in range(4):
                staged[j, e, :, shell] = shells[shell]
            late_out[j, e] = late
            direct_out[j, e] = through
            term = cot * (FILM_RATE * flux_next + ADVECT * (nexts - lower_next)) + late * (
                FILM_RATE * flux + ADVECT * (here - below)
            )
            grad = grad + (term[0] + term[1])
            if j == 0:
                follow = adjoint[e, :, 1] * nexts
                grad_next = grad_next + (follow[0] + follow[1])
            for k in range(comps):
                i = 2 * e + k
                if j == 0:
                    row_out[i, 1 : nz - 1] = jnp.where(
                        first_x, inner_late[e, k, 1 : nz - 1, nx - 1, :], inner_late[e, k, 1 : nz - 1, 0, :]
                    )
                row_out[i, z : z + 1] = jnp.where(first_x, late[k, nx - 1 : nx], late[k, 0:1])
        sends.append(pltpu.make_async_copy(staged.at[j], pellet_out.at[:, :, :, z], sems.at[j]))
        sends[j].start()
        grad_out[z] = grad * (inverse_porosity * inverse_porosity)
        if j == 0:
            inverse_porosity = 1.0 / porosity[1]
            grad_out[1] = grad_out[1] - ADVECT * (inverse_porosity * inverse_porosity) * grad_next
    for send in sends:
        send.wait()


def final_kernel(
    porosity, inner_late, inner_direct, edge_late, edge_direct, halo, row_in, fluid_out, done_out
):
    experiments, comps, nz, nx, ny = inner_late.shape
    first_x = lax.axis_index("xy") == 0
    done_out[...] = jnp.zeros_like(done_out)
    for z in range(nz):
        advect = ADVECT / porosity[z]
        if z < nz - 1:
            advect_above = ADVECT / porosity[z + 1] + AXIAL_MIX
        for e in range(experiments):
            def plane_at(w):
                if w in (0, nz - 1):
                    return edge_late[0 if w == 0 else 1, e]
                return inner_late[e, :, w]

            here = plane_at(z)
            lower = plane_at(z - 1) if z > 0 else halo[2 * e : 2 * e + 2]
            upper = advect_above * plane_at(z + 1) if z < nz - 1 else halo[4 + 2 * e : 6 + 2 * e]
            if z in (0, nz - 1):
                direct = edge_direct[0 if z == 0 else 1, e]
            else:
                direct = inner_direct[e, :, z]
            fluid_out[e, :, z] = (
                here
                - (advect + 2.0 * AXIAL_MIX) * here
                + AXIAL_MIX * lower
                + upper
                + RADIAL_MIX * cross_mix(here, pair_of(row_in, 2 * e, z), first_x)
                + direct
            )


def gather_kernel(grad, grad_in, picked, spread_a, spread_b, spread_c, done, grad_out, breakthrough_out):
    grad_out[...] = grad[...] + grad_in[...]
    total = (picked[0:4] + (spread_a[0:4] + spread_b[0:4] + spread_c[0:4]))[:, 0:2]
    shape = breakthrough_out.shape
    row, column = row_index(breakthrough_out), lane_index(breakthrough_out)
    value = jnp.zeros(shape, jnp.float32)
    for e in range(shape[0]):
        for k in range(shape[1]):
            i = e * shape[1] + k
            here = (row == e) & (column == k)
            value = jnp.where(here, jnp.broadcast_to(total[i : i + 1], shape), value)
    breakthrough_out[...] = value


def spread_levels(gz):
    reached = {2 * gz - 2, 2 * gz - 1}
    for n, level in enumerate(SPREAD):
        if n == 2:
            reached |= {i ^ 1 for i in reached}
        senders = set(reached)
        for pairs in level:
            targets = {i for _, i in pairs}
            assert {i for i, _ in pairs} <= senders and not targets & reached
            reached |= targets
    assert reached == set(range(2 * gz))
    return SPREAD


def shards(
    fluid_start,
    pellet_start,
    porosity,
    feed_level,
    sample_step,
    observed_outlet,
    adjoint_fluid_end,
    adjoint_pellet_end,
):
    f32 = jnp.float32
    experiments, comps, nz, nx, ny = fluid_start.shape
    planes = experiments * comps
    gz = lax.axis_size("gz")
    cell_count = nx * lax.axis_size("xy") * ny
    vmem = pl.BlockSpec(memory_space=pltpu.VMEM)
    smem = pl.BlockSpec(memory_space=pltpu.SMEM)
    hbm = pl.BlockSpec(memory_space=pltpu.HBM)
    params = pltpu.CompilerParams(vmem_limit_bytes=5 * 2**20)
    dma = pltpu.SemaphoreType.DMA

    def shape(*dims):
        return jax.ShapeDtypeStruct(dims, f32)

    trades = ([], [])
    for i in range(gz - 1):
        for x in range(2):
            low, high = 2 * i + x, 2 * i + 2 + x
            trades[i % 2].extend([(low, high), (high, low)])
    swap = [(0, 1), (1, 0)]
    levels = spread_levels(gz)

    def spread(picked, level):
        arrivals = [lax.ppermute(picked, ("gz", "xy"), pairs) for pairs in levels[level]]
        return arrivals + [jnp.zeros_like(picked)] * (3 - len(arrivals))

    in_hbm = [
        pltpu.with_memory_space_constraint(x, pltpu.HBM)
        for x in (fluid_start, pellet_start, porosity, adjoint_fluid_end, adjoint_pellet_end)
    ]
    rows = pl.pallas_call(
        pack_kernel,
        out_shape=shape(10, nz, ny),
        in_specs=[hbm] * 4,
        out_specs=vmem,
        scratch_shapes=[
            pltpu.VMEM((experiments, comps, 3, nx, ny), f32),
            pltpu.VMEM((experiments, comps, 2, 2, nx, ny), f32),
            pltpu.VMEM((2, nx, ny), f32),
            pltpu.VMEM((experiments, comps, nz, 8, ny), f32),
            pltpu.VMEM((experiments, comps, nz, 8, ny), f32),
            dma((5,)),
        ],
        compiler_params=params,
        name="pack",
    )(*in_hbm[:4])
    rows_in = lax.ppermute(rows, "xy", swap)

    seeds, picked = pl.pallas_call(
        partial(outlet_kernel, cell_count),
        out_shape=(shape(8, ny), shape(8, ny)),
        in_specs=[vmem, vmem, smem, smem],
        out_specs=[vmem] * 2,
        compiler_params=params,
        name="outlet",
    )(rows, rows_in, sample_step, observed_outlet)
    picked = picked + sum(spread(picked, 0))

    first, second = pl.pallas_call(
        edge_kernel,
        out_shape=(shape(4 * planes, nx, ny), shape(4 * planes, nx, ny)),
        in_specs=[hbm] * 5 + [vmem] * 2,
        out_specs=[vmem] * 2,
        scratch_shapes=[
            pltpu.VMEM((2, experiments, comps, 2, nx, ny), f32),
            pltpu.VMEM((2, experiments, comps, 2, nx, ny), f32),
            pltpu.VMEM((2, 2, nx, ny), f32),
            pltpu.VMEM((2, experiments, comps, 2, nx, ny), f32),
            pltpu.VMEM((2, experiments, comps, nx, ny), f32),
            dma((10,)),
        ],
        compiler_params=params,
        name="edge",
    )(*in_hbm, rows_in, seeds)
    first_in = lax.ppermute(first, ("gz", "xy"), trades[0])
    second_in = lax.ppermute(second, ("gz", "xy"), trades[1])

    adjoint_pellet, late, direct, grad, next_fluid = pl.pallas_call(
        inner_kernel,
        out_shape=(
            shape(*pellet_start.shape),
            shape(*fluid_start.shape),
            shape(*fluid_start.shape),
            shape(nz, nx, ny),
            shape(experiments, comps, nx, ny),
        ),
        in_specs=[vmem] * 7,
        out_specs=[hbm] + [vmem] * 4,
        scratch_shapes=[
            pltpu.VMEM((nz - 2, experiments, comps, 4, nx, ny), f32),
            pltpu.VMEM((experiments, comps, nx, ny), f32),
            dma((nz - 2,)),
        ],
        compiler_params=params,
        cost_estimate=pl.CostEstimate(flops=10**10, bytes_accessed=10**9, transcendentals=0),
        name="inner",
    )(
        fluid_start, pellet_start, porosity, adjoint_fluid_end, adjoint_pellet_end,
        rows_in, seeds,
    )

    adjoint_pellet, edge_late, edge_direct, grad, halo, rows, picked = pl.pallas_call(
        outer_kernel,
        out_shape=(
            shape(*pellet_start.shape),
            shape(2, experiments, comps, nx, ny),
            shape(2, experiments, comps, nx, ny),
            shape(nz, nx, ny),
            shape(2 * planes, nx, ny),
            shape(planes + 1, nz, ny),
            shape(8, ny),
        ),
        in_specs=[vmem] * 9 + [smem] + [vmem] * 7 + [hbm],
        out_specs=[hbm] + [vmem] * 6,
        scratch_shapes=[
            pltpu.VMEM((2, experiments, comps, 4, nx, ny), f32),
            dma((2,)),
        ],
        input_output_aliases={17: 0},
        compiler_params=params,
        name="outer",
    )(
        fluid_start, pellet_start, porosity, adjoint_fluid_end, adjoint_pellet_end,
        first_in, second_in, rows_in, seeds, feed_level,
        late, grad, next_fluid, picked, *spread(picked, 1), adjoint_pellet,
    )
    grad_in = lax.ppermute(grad, "exp", swap)
    rows_in = lax.ppermute(rows, "xy", swap)
    last_z = lax.axis_index("gz") == gz - 1
    picked = picked + jnp.where(last_z, 0.0, rows_in[planes])

    adjoint_fluid, done = pl.pallas_call(
        final_kernel,
        out_shape=(shape(*fluid_start.shape), shape(8, ny)),
        in_specs=[vmem] * 7,
        out_specs=[vmem] * 2,
        compiler_params=params,
        name="final",
    )(porosity, late, direct, edge_late, edge_direct, halo, rows_in)
    gradient, breakthrough = pl.pallas_call(
        gather_kernel,
        out_shape=(shape(nz, nx, ny), shape(experiments, comps)),
        in_specs=[vmem] * 7,
        out_specs=[vmem] * 2,
        compiler_params=params,
        name="gather",
    )(grad, grad_in, picked, *spread(picked, 2), done)
    return (breakthrough, adjoint_fluid, adjoint_pellet, gradient)


def solution(mesh):
    placed = (
        P("exp", None, "gz", "xy", None),
        P("exp", None, None, "gz", "xy", None),
        P("gz", "xy", None),
        P("exp"),
        P("exp"),
        P("exp", None),
        P("exp", None, "gz", "xy", None),
        P("exp", None, None, "gz", "xy", None),
    )
    return jax.shard_map(
        shards,
        mesh=mesh,
        in_specs=placed,
        out_specs=(
            P("exp", None),
            P("exp", None, "gz", "xy", None),
            P("exp", None, None, "gz", "xy", None),
            P("gz", "xy", None),
        ),
        check_vma=False,
    )
```
